32 devices in a mesh: seq: 8 (over z, y), head: 4 (over x, core).
Axes of the slice: x: 2, y: 2, z: 4, core: 2. Of those that a mesh axis runs over, the one named last changes fastest.
Arguments:
- tokens: bfloat16 [1024, 2560], P('seq'), may hold values from -51 to 51
- raw_keys: bfloat16 [32768, 768], P(('seq', 'head')), may hold values from -6 to 6
- raw_values: bfloat16 [32768, 512], P(('seq', 'head')), may hold values from -6 to 6
- query_weight: bfloat16 [2560, 12288], P('seq', 'head'), may hold values from -0.125 to 0.125
- output_weight: bfloat16 [8192, 2560], P('head', 'seq'), may hold values from -0.09375 to 0.09375
- key_expand: bfloat16 [192, 768], replicated, may hold values from -0.4375 to 0.4375
- key_mix: float32 [32, 768], replicated, may hold values from -1 to 1
- key_reduce: bfloat16 [768, 192], replicated, may hold values from -1.6953125 to 1.6953125
- value_expand: bfloat16 [128, 768], replicated, may hold values from -0.5 to 0.5
- value_mix: float32 [32, 768], replicated, may hold values from -1 to 1
- value_reduce: bfloat16 [768, 128], replicated, may hold values from -0.65625 to 0.65625
Outputs:
- branch_output: bfloat16 [1024, 2560], P('seq', 'head')
The draws below stay inside these ranges and needn't reach their ends.
All inputs are finite; a program needn't handle non-finite values.
Results may differ from the reference program's by a relative error of at most 0.008.
The reference program's roundings to bfloat16 on the way count: a program that leaves them out, or rounds other values in their place, can miss the bound.
Values may be sent and summed in bfloat16 or wider, within the bound.
No kernel may reach another device: no remote copies, remote signals or barrier semaphores. Data moves between devices by JAX's collectives and lax.ppermute only.
A program may use at most 128 MiB of HBM per device.

```python
import jax
import jax.numpy as jnp
from jax import lax

D = 2560
H = 64
G = 4
DK = 192
DV = 128
BLK = 32
STRIDE = 16
HID = 768
NEW = 1024
CTX = 31744
TOTAL = 32768
NB = 2048


def draw_tokens(key, part):
    base_key = jax.random.fold_in(jax.random.fold_in(key, 11), 0)
    return jnp.clip(jax.random.normal(base_key, (NEW, D), jnp.float32), -6.0, 6.0).astype(jnp.bfloat16)


def with_spikes(drawn, own_key, source, target, parts, factor):
    owner, partner = [(jnp.arange(drawn.shape[position]) // (drawn.shape[position] // parts)).reshape([-1 if axis == position else 1 for axis in range(drawn.ndim)]) for position in (source, target)]
    chosen = jax.random.permutation(own_key, parts)[partner]
    strong = (owner == chosen) | (owner == (partner + parts // 2) % parts)
    return jnp.where(strong, factor * drawn, drawn)


def block_levels(stream_key, shape, shards, smallest, high):
    gain, own = 1.0, jax.random.fold_in(stream_key, 6)
    for dim, shards_of in shards:
        heights = jnp.exp(jax.random.uniform(jax.random.fold_in(own, dim), (shards_of,), jnp.float32, smallest / len(shards), high / len(shards)))
        gain = gain * jnp.repeat(heights, shape[dim] // shards_of).reshape([-1 if axis == dim else 1 for axis in range(len(shape))])
    return gain


def gaussian(own_key, extent, deviation, reach, shards=(), kind=jnp.bfloat16):
    loudness = block_levels(own_key, extent, shards, -0.22, 0.18) if shards else 1.0
    result = jax.random.normal(own_key, extent, jnp.float32) * deviation * loudness
    return jnp.minimum(jnp.maximum(result, -reach), reach).astype(kind)


def gaussian_with(own_key, extent, width, reach, shards, heavy, kind=jnp.bfloat16):
    result = width * jax.random.normal(own_key, extent, jnp.float32)
    if shards:
        result = result * block_levels(own_key, extent, shards, -0.22, 0.18)
    return jnp.clip(with_spikes(result, jax.random.fold_in(own_key, 3), *heavy), -reach, reach).astype(kind)


def setup_inputs(seed: int = 0) -> dict:
    key_of = jax.random.split(jax.random.key(seed), 12)
    tokens = draw_tokens(jax.random.fold_in(key_of[11], 71), 0)
    raw_keys = gaussian(key_of[1], (TOTAL, G * DK), 1.0, 6.0, ((0, 32),))
    raw_values = gaussian(key_of[2], (TOTAL, G * DV), 1.0, 6.0, ((0, 32),))
    query_weight = gaussian(key_of[3], (D, H * DK), D ** -0.5, 0.125, ((0, 8), (1, 4)))
    output_weight = gaussian_with(key_of[4], (H * DV, D), (H * DV) ** -0.5, 0.09375, ((0, 4), (1, 8)), (0, 1, 8, 2.0))
    key_expand = gaussian(key_of[5], (DK, HID), DK ** -0.5, 0.4375)
    key_mix = gaussian(key_of[6], (BLK, HID), BLK ** -0.5, 1.0, (), jnp.float32)
    key_reduce = gaussian(key_of[7], (HID, DK), 0.28, 1.6953125)
    value_expand = gaussian(key_of[8], (DV, HID), DV ** -0.5, 0.5)
    value_mix = gaussian(key_of[9], (BLK, HID), BLK ** -0.5, 1.0, (), jnp.float32)
    value_reduce = gaussian(key_of[10], (HID, DV), 0.11, 0.65625)
    return dict(tokens=tokens, raw_keys=raw_keys, raw_values=raw_values, query_weight=query_weight, output_weight=output_weight, key_expand=key_expand, key_mix=key_mix, key_reduce=key_reduce, value_expand=value_expand, value_mix=value_mix, value_reduce=value_reduce)


def compress(raw, expand, position_mix, reduce_weight):
    width_in = expand.shape[0]
    compressed_list = []
    for group in range(G):
        group_tokens = raw[:, group * width_in:(group + 1) * width_in]
        projected = jnp.dot(group_tokens, expand, preferred_element_type=jnp.float32)
        projected = jnp.concatenate([projected, jnp.zeros((STRIDE, projected.shape[1]), jnp.float32)], axis=0)
        projected = projected.reshape(NB + 1, STRIDE, projected.shape[1])
        hidden = jnp.sum(projected[:-1] * position_mix[:STRIDE][None], axis=1)
        hidden = hidden + jnp.sum(projected[1:] * position_mix[STRIDE:][None], axis=1)
        activated = jax.nn.gelu(hidden, approximate=False).astype(jnp.bfloat16)
        compressed_list.append(jnp.dot(activated, reduce_weight, preferred_element_type=jnp.float32).astype(jnp.bfloat16))
    return jnp.stack(compressed_list)


def reference(tokens, raw_keys, raw_values, query_weight, output_weight, key_expand, key_mix, key_reduce, value_expand, value_mix, value_reduce):
    packed_keys = compress(raw_keys, key_expand, key_mix, key_reduce)
    packed_values = compress(raw_values, value_expand, value_mix, value_reduce)
    queries = jnp.dot(tokens, query_weight, preferred_element_type=jnp.float32).astype(jnp.bfloat16)
    queries = queries.reshape(NEW, H, DK).transpose(1, 0, 2)
    positions = CTX + jnp.arange(NEW, dtype=jnp.int32)
    block_index = jnp.arange(NB, dtype=jnp.int32)
    visible = (STRIDE * block_index + BLK - 1)[None, :] <= positions[:, None]
    score_scale = DK ** -0.5

    def one_head(inputs):
        head_queries, head_index = inputs
        group = head_index // (H // G)
        keys_group = lax.dynamic_index_in_dim(packed_keys, group, 0, keepdims=False)
        values_group = lax.dynamic_index_in_dim(packed_values, group, 0, keepdims=False)
        scores = jnp.dot(head_queries, keys_group.T, preferred_element_type=jnp.float32) * score_scale
        scores = jnp.where(visible, scores, -jnp.inf)
        row_max = jnp.max(scores, axis=1, keepdims=True)
        exponent = jnp.exp(scores - row_max)
        row_total = jnp.sum(exponent, axis=1, keepdims=True)
        numerator = jnp.dot(exponent.astype(jnp.bfloat16), values_group, preferred_element_type=jnp.float32)
        return (numerator / row_total).astype(jnp.bfloat16)

    attended = lax.map(one_head, (queries, jnp.arange(H, dtype=jnp.int32)))
    attended = attended.transpose(1, 0, 2).reshape(NEW, H * DV)
    return jnp.dot(attended, output_weight, preferred_element_type=jnp.float32).astype(jnp.bfloat16)
```

```python
import jax
import jax.numpy as jnp
import numpy as np
from jax import lax
from jax.experimental import pallas as pl
from jax.experimental.pallas import tpu as pltpu
from jax.sharding import Mesh
from jax.sharding import PartitionSpec as P

G = 4
BLK = 32
STRIDE = 16
LANES = 128
OUTER = 4
VMEM_LIMIT = 56 * 1024 * 1024


def round_up(value, unit):
    return -(-value // unit) * unit


def swap(block, axis, bit):
    return lax.ppermute(block, axis, [(i, i ^ bit) for i in range(lax.axis_size(axis))])


def window_of(group, width):
    low = group * width // LANES * LANES
    return low, round_up((group + 1) * width, LANES) - low, group * width - low


def compress_one(raw_ref, edge_ref, expand_ref, mix_ref, reduce_ref, sorted_ref, hidden_ref, groups):
    width, units = expand_ref.shape
    tokens = raw_ref.shape[0]
    rows = 8 * STRIDE
    chunks = tokens // rows
    blocks = tokens // STRIDE
    to = lax.broadcasted_iota(jnp.int32, (rows, rows), 0)
    come = lax.broadcasted_iota(jnp.int32, (rows, rows), 1)
    order = (come == (to % 8) * STRIDE + to // 8).astype(jnp.bfloat16)
    for chunk in range(chunks):
        piece = slice(chunk * rows, (chunk + 1) * rows)
        sorted_ref[piece, :] = jnp.dot(
            order, raw_ref[piece, :], preferred_element_type=jnp.float32
        ).astype(jnp.bfloat16)
    tile = 256 if units % 256 == 0 else units
    for group in range(groups):
        low, span, offset = window_of(group, width)
        parts = []
        if offset:
            parts.append(jnp.zeros((offset, units), jnp.bfloat16))
        parts.append(expand_ref[...])
        if span - offset - width:
            parts.append(jnp.zeros((span - offset - width, units), jnp.bfloat16))
        expand = jnp.concatenate(parts, axis=0) if len(parts) > 1 else parts[0]
        for start in range(0, units, tile):
            lanes = slice(start, start + tile)
            weight = expand[:, lanes]
            projected = jnp.dot(
                sorted_ref[:, low : low + span], weight, preferred_element_type=jnp.float32
            ).reshape(chunks, STRIDE, 8, tile)
            mix_low = mix_ref[:STRIDE, lanes][None, :, None, :]
            mix_high = mix_ref[STRIDE:, lanes]
            first = jnp.sum(projected * mix_low, axis=1).reshape(blocks, tile)
            second = jnp.sum(projected * mix_high[None, :, None, :], axis=1).reshape(blocks, tile)
            edge = jnp.dot(edge_ref[:, low : low + span], weight, preferred_element_type=jnp.float32)
            edge = jnp.sum(edge * mix_high, axis=0, keepdims=True)
            hidden = first + jnp.concatenate([second[1:], edge], axis=0)
            half = 0.5 * hidden
            activated = half + half * lax.erf(hidden * np.float32(2.0**-0.5))
            hidden_ref[group * blocks : (group + 1) * blocks, lanes] = activated.astype(jnp.bfloat16)
    return jnp.dot(hidden_ref[...], reduce_ref[...], preferred_element_type=jnp.float32).astype(
        jnp.bfloat16
    )


def compress_kernel(
    raw_keys, raw_values, edge_keys, edge_values, key_expand, key_mix, key_reduce,
    value_expand, value_mix, value_reduce, packed, sorted_keys, sorted_values, hidden,
):
    groups, blocks, _ = packed.shape
    key_width = key_expand.shape[0]
    value_start = round_up(key_width, LANES)
    keys = compress_one(
        raw_keys, edge_keys, key_expand, key_mix, key_reduce, sorted_keys, hidden, groups
    )
    values = compress_one(
        raw_values, edge_values, value_expand, value_mix, value_reduce, sorted_values, hidden, groups
    )
    for group in range(groups):
        rows = slice(group * blocks, (group + 1) * blocks)
        packed[group, :, :key_width] = keys[rows]
        packed[group, :, key_width:value_start] = jnp.zeros(
            (blocks, value_start - key_width), jnp.bfloat16
        )
        packed[group, :, value_start:] = values[rows]


def compress(raw_keys, raw_values, edge_keys, edge_values, *weights):
    key_expand, _, _, value_expand, _, _ = weights
    units = key_expand.shape[1]
    tokens = raw_keys.shape[0]
    blocks = tokens // STRIDE
    width = round_up(key_expand.shape[0], LANES) + value_expand.shape[0]
    flops = 2 * tokens * units * (raw_keys.shape[1] + raw_values.shape[1])
    return pl.pallas_call(
        compress_kernel,
        out_shape=jax.ShapeDtypeStruct((G, blocks, width), jnp.bfloat16),
        scratch_shapes=[
            pltpu.VMEM(raw_keys.shape, jnp.bfloat16),
            pltpu.VMEM(raw_values.shape, jnp.bfloat16),
            pltpu.VMEM((G * blocks, units), jnp.bfloat16),
        ],
        compiler_params=pltpu.CompilerParams(vmem_limit_bytes=VMEM_LIMIT),
        cost_estimate=pl.CostEstimate(
            flops=flops * 6, bytes_accessed=4 * raw_keys.size, transcendentals=0
        ),
        name="compress",
    )(raw_keys, raw_values, edge_keys, edge_values, *weights)


def attend(own, other, weight_own, weight_other, packed, limits, places, key_width, masked):
    rows = own.shape[0]
    heads = weight_own.shape[1] // key_width
    value_start = round_up(key_width, LANES)
    value_width = packed.shape[1] - value_start
    columns = packed.shape[0]
    factor = np.float32(key_width**-0.5 * np.log2(np.e))
    tile = min(256, rows)

    def kernel(own_ref, other_ref, wown_ref, wother_ref, kv_ref, limit_ref, place_ref, out_ref, query_ref):
        query_ref[...] = jnp.dot(
            own_ref[...], wown_ref[...], preferred_element_type=jnp.float32
        ) + jnp.dot(other_ref[...], wother_ref[...], preferred_element_type=jnp.float32)
        keys = kv_ref[:, :key_width]
        values = kv_ref[:, value_start:]
        for head in range(heads):
            for start in range(0, rows, tile):
                query = query_ref[
                    start : start + tile, head * key_width : (head + 1) * key_width
                ].astype(jnp.bfloat16)
                scores = lax.dot_general(
                    query, keys, (((1,), (1,)), ((), ())), preferred_element_type=jnp.float32
                )
                pieces = []
                for low, high, hide in masked:
                    piece = scores[:, low:high]
                    if hide:
                        visible = limit_ref[:, low:high] <= place_ref[start : start + tile, :]
                        piece = jnp.where(visible, piece, -jnp.inf)
                    pieces.append(piece)
                scores = jnp.concatenate(pieces, axis=1) if len(pieces) > 1 else pieces[0]
                top = jnp.max(scores, axis=1, keepdims=True)
                exponent = jnp.exp2((scores - top) * factor)
                total = jnp.sum(exponent, axis=1, keepdims=True)
                numerator = jnp.dot(
                    exponent.astype(jnp.bfloat16), values, preferred_element_type=jnp.float32
                )
                out_ref[
                    start : start + tile, head * value_width : (head + 1) * value_width
                ] = (numerator / total).astype(jnp.bfloat16)

    flops = 2 * rows * heads * (columns * (key_width + value_width) + own.shape[1] * 2 * key_width)
    return pl.pallas_call(
        kernel,
        out_shape=jax.ShapeDtypeStruct((rows, heads * value_width), jnp.bfloat16),
        scratch_shapes=[pltpu.VMEM((rows, heads * key_width), jnp.float32)],
        compiler_params=pltpu.CompilerParams(vmem_limit_bytes=VMEM_LIMIT),
        cost_estimate=pl.CostEstimate(
            flops=flops * 3,
            bytes_accessed=2 * (own.size * 2 + weight_own.size * 2 + packed.size),
            transcendentals=rows * heads * columns,
        ),
        name="attend",
    )(own, other, weight_own, weight_other, packed, limits, places)


def gather_line(block, axis, dim):
    count = lax.axis_size(axis)
    if count != 4:
        return lax.all_gather(block, axis, axis=dim, tiled=True)
    me = lax.axis_index(axis)
    far = swap(block, axis, 2)
    up = lax.ppermute(block, axis, [(i, i + 1) for i in range(3)])
    down = lax.ppermute(block, axis, [(i + 1, i) for i in range(3)])
    passed = lax.ppermute(far, axis, [(1, 0), (2, 3)])
    lower = jnp.where(me == 0, passed, up)
    upper = jnp.where(me == 3, passed, down)
    size = block.shape[dim]
    shape = list(block.shape)
    shape[dim] = count * size
    out = jnp.zeros(shape, block.dtype)
    for piece, place in ((block, me), (lower, (me + 3) % 4), (upper, (me + 1) % 4), (far, me ^ 2)):
        out = lax.dynamic_update_slice_in_dim(out, piece, place * size, dim)
    return out


def gather_pair(block, axis):
    if lax.axis_size(axis) != 2:
        return lax.all_gather(block, axis, axis=0)
    other = swap(block, axis, 1)
    first = lax.axis_index(axis) == 0
    return jnp.stack([jnp.where(first, block, other), jnp.where(first, other, block)])


def shards(
    tokens, raw_keys, raw_values, query_weight, output_weight,
    key_expand, key_mix, key_reduce, value_expand, value_mix, value_reduce,
):
    outer, inner, heads_axis = (lax.axis_size(name) for name in ("outer", "inner", "head"))
    z, y, h = (lax.axis_index(name) for name in ("outer", "inner", "head"))
    key_width, value_width = key_expand.shape[0], value_expand.shape[0]
    row_count, model = tokens.shape
    devices = outer * inner * heads_axis
    blocks = raw_keys.shape[0] // STRIDE
    context = raw_keys.shape[0] * devices - row_count * outer * inner
    part = query_weight.shape[0]
    heads_here = query_weight.shape[1] // key_width // outer
    chunk_count = 2 if heads_here % 2 == 0 else 1
    heads_chunk = heads_here // chunk_count
    fast = inner == 2 and outer == 4 and heads_axis == 4

    split = query_weight.reshape(part, chunk_count, outer, heads_chunk * key_width)
    weights = []
    for chunk in range(chunk_count):
        sent = split[:, chunk].transpose(1, 0, 2)
        weights.append(lax.all_to_all(sent, "outer", split_axis=0, concat_axis=0, tiled=True))

    edge = jnp.concatenate([raw_keys[:STRIDE], raw_values[:STRIDE]], axis=1)
    edge = lax.ppermute(
        edge, ("outer", "inner", "head"), [(i + 1, i) for i in range(devices - 1)]
    )
    edge_keys, edge_values = edge[:, : raw_keys.shape[1]], edge[:, raw_keys.shape[1] :]

    quarter = row_count // heads_axis if fast else row_count
    mine = lax.dynamic_slice_in_dim(tokens, h * quarter, quarter, 0) if fast else tokens
    mine = mine.reshape(quarter, outer, inner, part)
    if inner == 2:
        ordered = [lax.dynamic_index_in_dim(mine, y ^ step, 2, False) for step in range(2)]
    else:
        ordered = [mine[:, :, step] for step in range(inner)]
    mine = jnp.concatenate([piece.reshape(quarter, outer * part) for piece in ordered], axis=1)
    gathered = gather_line(mine, "outer", 0)
    if fast:
        across = swap(gathered, "head", 2)
        rows = outer * quarter
        every = jnp.zeros((heads_axis * rows, model), tokens.dtype)
        pair_here = jnp.concatenate([gathered, across], axis=0)
        pair_there = swap(pair_here, "head", 1)
        for piece, place in (
            (pair_here[:rows], h), (pair_here[rows:], h ^ 2),
            (pair_there[:rows], h ^ 1), (pair_there[rows:], h ^ 3),
        ):
            every = lax.dynamic_update_slice(every, piece, (place * rows, 0))
    else:
        every = gathered
    shape = (every.shape[0] // (outer * quarter), outer, quarter)
    places = (
        context
        + (lax.broadcasted_iota(jnp.int32, shape, 1) * inner + y) * row_count
        + lax.broadcasted_iota(jnp.int32, shape, 0) * quarter
        + lax.broadcasted_iota(jnp.int32, shape, 2)
    ).reshape(-1, 1)

    packed = compress(
        raw_keys, raw_values, edge_keys, edge_values,
        key_expand, key_mix, key_reduce, value_expand, value_mix, value_reduce,
    )
    if heads_axis != G:
        packed = jnp.broadcast_to(packed[:, None], (G, heads_axis // G, *packed.shape[1:]))
        packed = packed.reshape(heads_axis, blocks, -1)
    packed = lax.all_to_all(packed, "head", split_axis=0, concat_axis=0, tiled=True)
    packed = gather_line(packed.reshape(heads_axis * blocks, -1), "outer", 0)
    packed = gather_pair(packed, "inner").reshape(devices * blocks, -1)
    ids = np.arange(devices * blocks).reshape(outer, inner, heads_axis, blocks)
    ids = ids.transpose(1, 0, 2, 3).reshape(-1)
    limits = STRIDE * ids + BLK - 1
    hidden = [bool((limits[i : i + LANES] > context).any()) for i in range(0, len(ids), LANES)]
    masked, start = [], 0
    for i in range(1, len(hidden) + 1):
        if i == len(hidden) or hidden[i] != hidden[start]:
            masked.append((start * LANES, min(i * LANES, len(ids)), hidden[start]))
            start = i
    limits = jnp.asarray(limits[None, :], jnp.int32)

    if inner == 2:
        out_weights = [output_weight, swap(output_weight, "inner", 1)]
    else:
        out_weights = [lax.all_gather(output_weight, "inner", axis=1, tiled=True)]

    total = None
    for chunk in range(chunk_count):
        weight = weights[chunk].reshape(outer * part, heads_chunk * key_width)
        if inner == 2:
            weight_own, weight_other = weight, swap(weight, "inner", 1)
            split_at = outer * part
        else:
            weight = lax.all_gather(weight, "inner", axis=0, tiled=True)
            split_at = inner // 2 * outer * part
            weight_own, weight_other = weight[:split_at], weight[split_at:]
        attended = attend(
            every[:, :split_at], every[:, split_at:], weight_own, weight_other,
            packed, limits, places, key_width, masked,
        )
        attended = gather_line(attended, "outer", 1)
        width = attended.shape[1]
        product = jnp.concatenate(
            [
                jnp.dot(
                    attended, weight[chunk * width : (chunk + 1) * width],
                    preferred_element_type=jnp.float32,
                )
                for weight in out_weights
            ],
            axis=1,
        )
        total = product if total is None else total + product

    columns = total.shape[1]
    if fast:
        x, c = h // 2, h % 2
        total = total.reshape(heads_axis, 2, 2, quarter, columns)
        keep = lax.dynamic_index_in_dim(total, c, 2, False)
        send = lax.dynamic_index_in_dim(total, 1 - c, 2, False).astype(jnp.bfloat16)
        total = keep + swap(send, "head", 1).astype(jnp.float32)
        keep = lax.dynamic_index_in_dim(total, x, 1, False)
        send = lax.dynamic_index_in_dim(total, 1 - x, 1, False).astype(jnp.bfloat16)
        total = keep + swap(send, "head", 2).astype(jnp.float32)
        result = total.astype(jnp.bfloat16).reshape(row_count, columns)
        first, second = result[:, : columns // 2], result[:, columns // 2 :]
        result = jnp.concatenate(
            [jnp.where(y == 0, first, second), jnp.where(y == 0, second, first)], axis=1
        )
        route = [
            ((a * inner + b) * heads_axis + k, (k * inner + b) * heads_axis + a)
            for a in range(outer) for b in range(inner) for k in range(heads_axis)
        ]
        return lax.ppermute(result, ("outer", "inner", "head"), route)
    total = lax.psum_scatter(total, "head", scatter_dimension=0, tiled=True).astype(jnp.bfloat16)
    total = lax.all_gather(total, "head", axis=0, tiled=True)
    total = lax.all_to_all(
        total.reshape(outer, row_count, columns), "outer", split_axis=0, concat_axis=0, tiled=True
    )
    total = total.transpose(1, 0, 2).reshape(row_count, model)
    return lax.dynamic_slice_in_dim(total, h * (model // heads_axis), model // heads_axis, 1)


def solution(mesh):
    seq_count, head_count = mesh.shape["seq"], mesh.shape["head"]
    inner = seq_count // OUTER
    finer = Mesh(
        mesh.devices.reshape(OUTER, inner, head_count), ("outer", "inner", "head")
    )
    seq = ("outer", "inner")
    in_specs = (
        P(seq, None),
        P((*seq, "head"), None),
        P((*seq, "head"), None),
        P(seq, "head"),
        P("head", seq),
        P(), P(), P(), P(), P(), P(),
    )
    return jax.shard_map(
        shards, mesh=finer, in_specs=in_specs, out_specs=P(seq, "head"), check_vma=False
    )
```

```python
import jax
import jax.numpy as jnp
import numpy as np
from jax import lax
from jax.experimental import pallas as pl
from jax.experimental.pallas import tpu as pltpu
from jax.sharding import Mesh
from jax.sharding import PartitionSpec as P

G = 4
BLK = 32
STRIDE = 16
LANES = 128
OUTER = 4
VMEM_LIMIT = 56 * 1024 * 1024


def round_up(value, unit):
    return -(-value // unit) * unit


def swap(block, axis, bit):
    return lax.ppermute(block, axis, [(i, i ^ bit) for i in range(lax.axis_size(axis))])


def window_of(group, width):
    low = group * width // LANES * LANES
    return low, round_up((group + 1) * width, LANES) - low, group * width - low


def compress_one(raw_ref, edge_ref, expand_ref, mix_ref, reduce_ref, sorted_ref, hidden_ref, groups):
    width, units = expand_ref.shape
    tokens = raw_ref.shape[0]
    rows = 8 * STRIDE
    chunks = tokens // rows
    blocks = tokens // STRIDE
    to = lax.broadcasted_iota(jnp.int32, (rows, rows), 0)
    come = lax.broadcasted_iota(jnp.int32, (rows, rows), 1)
    order = (come == (to % 8) * STRIDE + to // 8).astype(jnp.bfloat16)
    for chunk in range(chunks):
        piece = slice(chunk * rows, (chunk + 1) * rows)
        sorted_ref[piece, :] = jnp.dot(
            order, raw_ref[piece, :], preferred_element_type=jnp.float32
        ).astype(jnp.bfloat16)
    tile = 256 if units % 256 == 0 else units
    for group in range(groups):
        low, span, offset = window_of(group, width)
        parts = []
        if offset:
            parts.append(jnp.zeros((offset, units), jnp.bfloat16))
        parts.append(expand_ref[...])
        if span - offset - width:
            parts.append(jnp.zeros((span - offset - width, units), jnp.bfloat16))
        expand = jnp.concatenate(parts, axis=0) if len(parts) > 1 else parts[0]
        for start in range(0, units, tile):
            lanes = slice(start, start + tile)
            weight = expand[:, lanes]
            projected = jnp.dot(
                sorted_ref[:, low : low + span], weight, preferred_element_type=jnp.float32
            ).reshape(chunks, STRIDE, 8, tile)
            mix_low = mix_ref[:STRIDE, lanes][None, :, None, :]
            mix_high = mix_ref[STRIDE:, lanes]
            first = jnp.sum(projected * mix_low, axis=1).reshape(blocks, tile)
            second = jnp.sum(projected * mix_high[None, :, None, :], axis=1).reshape(blocks, tile)
            edge = jnp.dot(edge_ref[:, low : low + span], weight, preferred_element_type=jnp.float32)
            edge = jnp.sum(edge * mix_high, axis=0, keepdims=True)
            hidden = first + jnp.concatenate([second[1:], edge], axis=0)
            half = 0.5 * hidden
            activated = half + half * lax.erf(hidden * np.float32(2.0**-0.5))
            hidden_ref[group * blocks : (group + 1) * blocks, lanes] = activated.astype(jnp.bfloat16)
    return jnp.dot(hidden_ref[...], reduce_ref[...], preferred_element_type=jnp.float32).astype(
        jnp.bfloat16
    )


def compress_kernel(
    raw_keys, raw_values, edge_keys, edge_values, key_expand, key_mix, key_reduce,
    value_expand, value_mix, value_reduce, packed, sorted_keys, sorted_values, hidden,
):
    groups, blocks, _ = packed.shape
    key_width = key_expand.shape[0]
    value_start = round_up(key_width, LANES)
    keys = compress_one(
        raw_keys, edge_keys, key_expand, key_mix, key_reduce, sorted_keys, hidden, groups
    )
    values = compress_one(
        raw_values, edge_values, value_expand, value_mix, value_reduce, sorted_values, hidden, groups
    )
    for group in range(groups):
        rows = slice(group * blocks, (group + 1) * blocks)
        packed[group, :, :key_width] = keys[rows]
        packed[group, :, key_width:value_start] = jnp.zeros(
            (blocks, value_start - key_width), jnp.bfloat16
        )
        packed[group, :, value_start:] = values[rows]


def compress(raw_keys, raw_values, edge_keys, edge_values, *weights):
    key_expand, _, _, value_expand, _, _ = weights
    units = key_expand.shape[1]
    tokens = raw_keys.shape[0]
    blocks = tokens // STRIDE
    width = round_up(key_expand.shape[0], LANES) + value_expand.shape[0]
    flops = 2 * tokens * units * (raw_keys.shape[1] + raw_values.shape[1])
    return pl.pallas_call(
        compress_kernel,
        out_shape=jax.ShapeDtypeStruct((G, blocks, width), jnp.bfloat16),
        scratch_shapes=[
            pltpu.VMEM(raw_keys.shape, jnp.bfloat16),
            pltpu.VMEM(raw_values.shape, jnp.bfloat16),
            pltpu.VMEM((G * blocks, units), jnp.bfloat16),
        ],
        compiler_params=pltpu.CompilerParams(vmem_limit_bytes=VMEM_LIMIT),
        cost_estimate=pl.CostEstimate(
            flops=flops * 6, bytes_accessed=4 * raw_keys.size, transcendentals=0
        ),
        name="compress",
    )(raw_keys, raw_values, edge_keys, edge_values, *weights)


def project(pieces, weights):
    part, depth = pieces[0].shape
    rows = part * len(pieces)
    shares, share, columns = weights[0].shape

    def kernel(*refs):
        piece_refs = refs[: len(pieces)]
        weight_refs = refs[len(pieces) : -2]
        out_ref, all_ref = refs[-2:]
        for index, weight_ref in enumerate(weight_refs):
            for owner in range(shares):
                start = (owner * len(weights) + index) * share
                all_ref[start : start + share, :] = weight_ref[owner]
        for index, piece in enumerate(piece_refs):
            out_ref[index * part : (index + 1) * part, :] = jnp.dot(
                piece[...], all_ref[...], preferred_element_type=jnp.float32
            ).astype(jnp.bfloat16)

    return pl.pallas_call(
        kernel,
        out_shape=jax.ShapeDtypeStruct((rows, columns), jnp.bfloat16),
        scratch_shapes=[pltpu.VMEM((depth, columns), jnp.bfloat16)],
        compiler_params=pltpu.CompilerParams(vmem_limit_bytes=VMEM_LIMIT),
        cost_estimate=pl.CostEstimate(
            flops=2 * rows * depth * columns, bytes_accessed=2 * rows * depth, transcendentals=0
        ),
        name="project",
    )(*pieces, *weights)


def attend(here, queries, head, packed, limits, places, key_width, masked, layout):
    rows_each = queries[0].shape[0]
    rows = rows_each * len(queries)
    value_start = round_up(key_width, LANES)
    value_width = packed.shape[1] - value_start
    columns = packed.shape[0]
    factor = np.float32(key_width**-0.5 * np.log2(np.e))
    tile = min(256, rows_each)
    unit, outputs, sends = layout

    def kernel(here_ref, *refs):
        query_refs = refs[: len(queries)]
        kv_ref, limit_ref, place_ref = refs[len(queries) : len(queries) + 3]
        out_refs = refs[len(queries) + 3 :]
        keys = kv_ref[:, :key_width]
        values = kv_ref[:, value_start:]
        for start in range(0, rows, tile):
            from_ref, at = query_refs[start // rows_each], start % rows_each
            query = from_ref[at : at + tile, head * key_width : (head + 1) * key_width]
            scores = lax.dot_general(
                query, keys, (((1,), (1,)), ((), ())), preferred_element_type=jnp.float32
            )
            pieces = []
            for low, high, hide in masked:
                piece = scores[:, low:high]
                if hide:
                    visible = limit_ref[:, low:high] <= place_ref[start : start + tile, :]
                    piece = jnp.where(visible, piece, -jnp.inf)
                pieces.append(piece)
            scores = jnp.concatenate(pieces, axis=1) if len(pieces) > 1 else pieces[0]
            top = jnp.max(scores, axis=1, keepdims=True)
            exponent = jnp.exp2((scores - top) * factor)
            total = jnp.sum(exponent, axis=1, keepdims=True)
            numerator = jnp.dot(
                exponent.astype(jnp.bfloat16), values, preferred_element_type=jnp.float32
            )
            done = (numerator / total).astype(jnp.bfloat16)
            for low in range(0, tile, unit):
                which, where = sends((start + low) // unit, here_ref[0], here_ref[1])
                if not isinstance(where, int):
                    where = pl.multiple_of(where, unit)
                out_refs[which][pl.ds(where, unit), :] = done[low : low + unit]

    shape = jax.ShapeDtypeStruct((rows // outputs, value_width), jnp.bfloat16)
    return pl.pallas_call(
        kernel,
        out_shape=(shape,) * outputs,
        in_specs=[pl.BlockSpec(memory_space=pltpu.SMEM)]
        + [pl.BlockSpec(memory_space=pltpu.VMEM)] * (len(queries) + 3),
        compiler_params=pltpu.CompilerParams(vmem_limit_bytes=VMEM_LIMIT),
        cost_estimate=pl.CostEstimate(
            flops=2 * rows * columns * (key_width + value_width),
            bytes_accessed=2 * packed.size,
            transcendentals=0,
        ),
        name="attend",
    )(here, *queries, packed, limits, places)


def expel(place, pieces, weights, before, chunk, chunks, shape):
    rows, width = pieces[0].shape
    depth, step, single = 4 * width, weights[0].shape[0], width // 2
    last = shape is not None

    def kernel(place_ref, *refs):
        own, up, down, passed, far = refs[:5]
        weight_refs = refs[5 : 5 + len(weights)]
        rest = refs[5 + len(weights) :]
        before_refs, outs = rest[: len(before)], rest[len(before) :]
        z, core, y = place_ref[0], place_ref[1] & 1, place_ref[2]
        lower = jnp.where(z == 0, passed[...], up[...])
        upper = jnp.where(z == 3, passed[...], down[...])
        for side, weight in enumerate(weight_refs):
            lanes = slice(side * step, (side + 1) * step)
            total = before_refs[0][:, lanes] if before else None
            for block, at in (
                (own[...], z), (lower, (z + 3) & 3), (upper, (z + 1) & 3), (far[...], z ^ 2)
            ):
                starts = [((at * 2 + inner) * chunks + chunk) * single for inner in (y, 1 - y)]
                both = [weight[:, pl.ds(pl.multiple_of(start, single), single)] for start in starts]
                product = lax.dot_general(
                    block, jnp.concatenate(both, axis=1), (((1,), (1,)), ((), ())),
                    preferred_element_type=jnp.float32,
                )
                total = product if total is None else total + product
            if not last:
                outs[0][:, lanes] = total
                continue
            keep_ref, send_ref, hold_ref = outs
            hold_ref[...] = total.reshape(hold_ref.shape)
            keep_ref[:, :, :, lanes] = hold_ref[:, :, pl.ds(core, 1)][:, :, 0]
            send_ref[:, :, :, lanes] = hold_ref[:, :, pl.ds(1 - core, 1)][:, :, 0].astype(jnp.bfloat16)

    columns = step * len(weights)
    if last:
        groups, quarter = shape
        out_shape = (
            jax.ShapeDtypeStruct((groups, 2, quarter, columns), jnp.float32),
            jax.ShapeDtypeStruct((groups, 2, quarter, columns), jnp.bfloat16),
        )
        scratch = [pltpu.VMEM((groups, 2, 2, quarter, step), jnp.float32)]
    else:
        out_shape, scratch = jax.ShapeDtypeStruct((rows, columns), jnp.float32), []
    count = len(pieces) + len(weights) + len(before)
    return pl.pallas_call(
        kernel,
        out_shape=out_shape,
        in_specs=[pl.BlockSpec(memory_space=pltpu.SMEM)]
        + [pl.BlockSpec(memory_space=pltpu.VMEM)] * count,
        scratch_shapes=scratch,
        compiler_params=pltpu.CompilerParams(vmem_limit_bytes=VMEM_LIMIT),
        cost_estimate=pl.CostEstimate(
            flops=2 * rows * depth * columns, bytes_accessed=2 * depth * columns, transcendentals=0
        ),
        name="expel",
    )(place, *pieces, *weights, *before)


def line_pieces(block, axis):
    far = swap(block, axis, 2)
    up = lax.ppermute(block, axis, [(i, i + 1) for i in range(3)])
    down = lax.ppermute(block, axis, [(i + 1, i) for i in range(3)])
    passed = lax.ppermute(far, axis, [(1, 0), (2, 3)])
    return block, up, down, passed, far


def gather_line(block, axis, dim):
    count = lax.axis_size(axis)
    if count != 4:
        return lax.all_gather(block, axis, axis=dim, tiled=True)
    me = lax.axis_index(axis)
    block, up, down, passed, far = line_pieces(block, axis)
    lower = jnp.where(me == 0, passed, up)
    upper = jnp.where(me == 3, passed, down)
    size = block.shape[dim]
    shape = list(block.shape)
    shape[dim] = count * size
    out = jnp.zeros(shape, block.dtype)
    for piece, place in ((block, me), (lower, (me + 3) % 4), (upper, (me + 1) % 4), (far, me ^ 2)):
        out = lax.dynamic_update_slice_in_dim(out, piece, place * size, dim)
    return out


def gather_pair(block, axis):
    if lax.axis_size(axis) != 2:
        return lax.all_gather(block, axis, axis=0)
    other = swap(block, axis, 1)
    first = lax.axis_index(axis) == 0
    return jnp.stack([jnp.where(first, block, other), jnp.where(first, other, block)])


def shards(
    tokens, raw_keys, raw_values, query_weight, output_weight,
    key_expand, key_mix, key_reduce, value_expand, value_mix, value_reduce,
):
    outer, inner, heads_axis = (lax.axis_size(name) for name in ("outer", "inner", "head"))
    z, y, h = (lax.axis_index(name) for name in ("outer", "inner", "head"))
    key_width, value_width = key_expand.shape[0], value_expand.shape[0]
    row_count, model = tokens.shape
    devices = outer * inner * heads_axis
    blocks = raw_keys.shape[0] // STRIDE
    context = raw_keys.shape[0] * devices - row_count * outer * inner
    part = query_weight.shape[0]
    fast = inner == 2 and outer == 4 and heads_axis == 4

    seq_axes = ("outer", "inner") if fast else "outer"
    shares = outer * inner if fast else outer
    share = query_weight.shape[1] // shares
    halves = 2 if fast and part % 32 == 0 else 1
    weight = []
    for half in range(halves):
        rows = slice(half * part // halves, (half + 1) * part // halves)
        sent = jnp.stack([query_weight[rows, i * share : (i + 1) * share] for i in range(shares)])
        weight.append(lax.all_to_all(sent, seq_axes, split_axis=0, concat_axis=0, tiled=True))
    if not fast:
        weight = lax.all_gather(weight[0], "inner", axis=1).reshape(model, share)
    heads_here = share // key_width

    edge = jnp.concatenate([raw_keys[:STRIDE], raw_values[:STRIDE]], axis=1)
    edge = lax.ppermute(
        edge, ("outer", "inner", "head"), [(i + 1, i) for i in range(devices - 1)]
    )
    edge_keys, edge_values = edge[:, : raw_keys.shape[1]], edge[:, raw_keys.shape[1] :]

    if fast:
        quarter = row_count // heads_axis
        mine = lax.dynamic_slice_in_dim(tokens, h * quarter, quarter, 0)
        mine, up, down, passed, far = line_pieces(mine, "outer")
        first = jnp.concatenate([mine, far], axis=0)
        second = jnp.concatenate([jnp.where(z == 0, passed, up), jnp.where(z == 3, passed, down)], axis=0)
        first = jnp.concatenate([first, swap(first, "inner", 1)], axis=0)
        second = jnp.concatenate([second, swap(second, "head", 2)], axis=0)
        pieces = [first, second, swap(first, "head", 2), swap(second, "inner", 1)]
        steps = [
            (0, 0, 0), (3, 0, 0), (0, 1, 0), (3, 1, 0), (1, 0, 0), (2, 0, 0), (1, 0, 2), (2, 0, 2),
            (0, 0, 2), (3, 0, 2), (0, 1, 2), (3, 1, 2), (1, 1, 0), (2, 1, 0), (1, 1, 2), (2, 1, 2),
        ]
        steps = steps + [(a, b, k ^ 1) for a, b, k in steps]
        queries = [
            project(pieces, weight),
            project([swap(piece, "head", 1) for piece in pieces], weight),
        ]

        def of_block(block, z, h):
            line, side, turn = steps[block]
            there = (z, (z + 3) & 3, (z + 1) & 3, z ^ 2)[line]
            return side, ((h ^ turn) * outer + there) * quarter

        bases = []
        for block, (_, side, _) in enumerate(steps):
            where = of_block(block, z, h)[1] // quarter
            bases.append((where % outer * inner + (y ^ side)) * row_count + where // outer * quarter)
        bases = jnp.stack(bases)[:, None] + jnp.arange(quarter)[None, :]
        layout = (quarter, inner, of_block)
    else:
        every = gather_line(tokens, "outer", 0)
        queries = [jnp.dot(every, weight, preferred_element_type=jnp.float32).astype(jnp.bfloat16)]
        bases = (jnp.arange(outer) * inner + y)[:, None] * row_count + jnp.arange(row_count)[None, :]
        layout = (row_count, 1, lambda block, z, h: (0, block * row_count))
    places = (context + bases).astype(jnp.int32).reshape(-1, 1)
    here = jnp.stack([z, h, y]).astype(jnp.int32)

    packed = compress(
        raw_keys, raw_values, edge_keys, edge_values,
        key_expand, key_mix, key_reduce, value_expand, value_mix, value_reduce,
    )
    ids = np.arange(devices * blocks).reshape(outer, inner, heads_axis, blocks)
    if fast:
        stay = lax.dynamic_index_in_dim(packed, h, 0, False)
        away = [lax.dynamic_index_in_dim(packed, h ^ step, 0, False) for step in (1, 2, 3)]
        came = [swap(piece, "head", step) for step, piece in zip((1, 2, 3), away)]
        packed = jnp.concatenate([stay, *came], axis=0)
        bound = np.broadcast_to(ids.max(axis=(2, 3), keepdims=True), ids.shape)
    else:
        packed = jnp.broadcast_to(packed[:, None], (G, heads_axis // G, *packed.shape[1:]))
        packed = packed.reshape(heads_axis, blocks, -1)
        packed = lax.all_to_all(packed, "head", split_axis=0, concat_axis=0, tiled=True)
        packed = packed.reshape(heads_axis * blocks, -1)
        bound = ids
    packed = gather_line(packed, "outer", 0)
    packed = gather_pair(packed, "inner").reshape(devices * blocks, -1)
    bound = (STRIDE * bound + BLK - 1).transpose(1, 0, 2, 3).reshape(-1)
    hidden = [bool((bound[i : i + LANES] > context).any()) for i in range(0, len(bound), LANES)]
    masked, start = [], 0
    for i in range(1, len(hidden) + 1):
        if i == len(hidden) or hidden[i] != hidden[start]:
            masked.append((start * LANES, min(i * LANES, len(bound)), hidden[start]))
            start = i
    if fast:
        column = np.arange(heads_axis)[None, None, :, None]
        ids = ids[:, :, :1] + (column ^ h) * blocks
        limits = (STRIDE * ids + BLK - 1).transpose(1, 0, 2, 3).reshape(1, -1).astype(jnp.int32)
    else:
        limits = (STRIDE * ids + BLK - 1).transpose(1, 0, 2, 3).reshape(1, -1)
        limits = jnp.asarray(limits, jnp.int32)

    if fast:
        turned = output_weight.T
        out_weights = [turned, swap(turned, "inner", 1)]
    else:
        out_weights = lax.all_gather(output_weight, "inner", axis=1, tiled=True)

    total = None
    for head in range(heads_here):
        attended = attend(
            here, queries, head, packed, limits, places, key_width, masked, layout
        )
        if fast:
            last = head == heads_here - 1
            block = jnp.concatenate([attended[0], swap(attended[1], "inner", 1)], axis=1)
            total = expel(
                here, line_pieces(block, "outer"), out_weights, [] if total is None else [total],
                head, heads_here, (heads_axis, quarter) if last else None,
            )
        else:
            attended = gather_line(attended[0], "outer", 1)
            rows = out_weights.reshape(outer, heads_here, value_width, -1)[:, head]
            product = jnp.dot(
                attended, rows.reshape(outer * value_width, -1), preferred_element_type=jnp.float32
            )
            total = product if total is None else total + product

    if fast:
        keep, send = total
        columns = keep.shape[-1]
        total = keep + swap(send, "head", 1).astype(jnp.float32)
        x = h // 2
        keep = lax.dynamic_index_in_dim(total, x, 1, False)
        send = lax.dynamic_index_in_dim(total, 1 - x, 1, False).astype(jnp.bfloat16)
        total = keep + swap(send, "head", 2).astype(jnp.float32)
        result = total.astype(jnp.bfloat16).reshape(row_count, columns)
        first, second = result[:, : columns // 2], result[:, columns // 2 :]
        result = jnp.concatenate(
            [jnp.where(y == 0, first, second), jnp.where(y == 0, second, first)], axis=1
        )
        route = [
            ((a * inner + b) * heads_axis + k, (k * inner + b) * heads_axis + a)
            for a in range(outer) for b in range(inner) for k in range(heads_axis)
        ]
        return lax.ppermute(result, ("outer", "inner", "head"), route)
    columns = total.shape[1]
    total = lax.psum_scatter(total, "head", scatter_dimension=0, tiled=True).astype(jnp.bfloat16)
    total = lax.all_gather(total, "head", axis=0, tiled=True)
    total = lax.all_to_all(
        total.reshape(outer, row_count, columns), "outer", split_axis=0, concat_axis=0, tiled=True
    )
    total = total.transpose(1, 0, 2).reshape(row_count, model)
    return lax.dynamic_slice_in_dim(total, h * (model // heads_axis), model // heads_axis, 1)


def solution(mesh):
    seq_count, head_count = mesh.shape["seq"], mesh.shape["head"]
    inner = seq_count // OUTER
    finer = Mesh(
        mesh.devices.reshape(OUTER, inner, head_count), ("outer", "inner", "head")
    )
    seq = ("outer", "inner")
    in_specs = (
        P(seq, None),
        P((*seq, "head"), None),
        P((*seq, "head"), None),
        P(seq, "head"),
        P("head", seq),
        P(), P(), P(), P(), P(), P(),
    )
    return jax.shard_map(
        shards, mesh=finer, in_specs=in_specs, out_specs=P(seq, "head"), check_vma=False
    )
```

```python
import jax
import jax.numpy as jnp
import numpy as np
from jax import lax
from jax.experimental import pallas as pl
from jax.experimental.pallas import tpu as pltpu
from jax.sharding import Mesh
from jax.sharding import PartitionSpec as P

G = 4
BLK = 32
STRIDE = 16
LANES = 128
OUTER = 4
VMEM_LIMIT = 56 * 1024 * 1024
PROJECT_WEIGHT = 20


def round_up(value, unit):
    return -(-value // unit) * unit


def swap(block, axis, bit):
    return lax.ppermute(block, axis, [(i, i ^ bit) for i in range(lax.axis_size(axis))])


def window_of(group, width):
    low = group * width // LANES * LANES
    return low, round_up((group + 1) * width, LANES) - low, group * width - low


def compress_one(raw_ref, edge_ref, expand_ref, mix_ref, reduce_ref, sorted_ref, hidden_ref, groups):
    width, units = expand_ref.shape
    tokens = raw_ref.shape[0]
    rows = 8 * STRIDE
    chunks = tokens // rows
    blocks = tokens // STRIDE
    to = lax.broadcasted_iota(jnp.int32, (rows, rows), 0)
    come = lax.broadcasted_iota(jnp.int32, (rows, rows), 1)
    order = (come == (to % 8) * STRIDE + to // 8).astype(jnp.bfloat16)
    for chunk in range(chunks):
        piece = slice(chunk * rows, (chunk + 1) * rows)
        sorted_ref[piece, :] = jnp.dot(
            order, raw_ref[piece, :], preferred_element_type=jnp.float32
        ).astype(jnp.bfloat16)
    tile = 256 if units % 256 == 0 else units
    for group in range(groups):
        low, span, offset = window_of(group, width)
        parts = []
        if offset:
            parts.append(jnp.zeros((offset, units), jnp.bfloat16))
        parts.append(expand_ref[...])
        if span - offset - width:
            parts.append(jnp.zeros((span - offset - width, units), jnp.bfloat16))
        expand = jnp.concatenate(parts, axis=0) if len(parts) > 1 else parts[0]
        for start in range(0, units, tile):
            lanes = slice(start, start + tile)
            weight = expand[:, lanes]
            projected = jnp.dot(
                sorted_ref[:, low : low + span], weight, preferred_element_type=jnp.float32
            ).reshape(chunks, STRIDE, 8, tile)
            mix_low = mix_ref[:STRIDE, lanes][None, :, None, :]
            mix_high = mix_ref[STRIDE:, lanes]
            first = jnp.sum(projected * mix_low, axis=1).reshape(blocks, tile)
            second = jnp.sum(projected * mix_high[None, :, None, :], axis=1).reshape(blocks, tile)
            edge = jnp.dot(edge_ref[:, low : low + span], weight, preferred_element_type=jnp.float32)
            edge = jnp.sum(edge * mix_high, axis=0, keepdims=True)
            hidden = first + jnp.concatenate([second[1:], edge], axis=0)
            half = 0.5 * hidden
            activated = half + half * lax.erf(hidden * np.float32(2.0**-0.5))
            hidden_ref[group * blocks : (group + 1) * blocks, lanes] = activated.astype(jnp.bfloat16)
    return jnp.dot(hidden_ref[...], reduce_ref[...], preferred_element_type=jnp.float32).astype(
        jnp.bfloat16
    )


def compress_kernel(
    raw_keys, raw_values, edge_keys, edge_values, key_expand, key_mix, key_reduce,
    value_expand, value_mix, value_reduce, packed, sorted_keys, sorted_values, hidden,
):
    groups, blocks, _ = packed.shape
    key_width = key_expand.shape[0]
    value_start = round_up(key_width, LANES)
    keys = compress_one(
        raw_keys, edge_keys, key_expand, key_mix, key_reduce, sorted_keys, hidden, groups
    )
    values = compress_one(
        raw_values, edge_values, value_expand, value_mix, value_reduce, sorted_values, hidden, groups
    )
    for group in range(groups):
        rows = slice(group * blocks, (group + 1) * blocks)
        packed[group, :, :key_width] = keys[rows]
        packed[group, :, key_width:value_start] = jnp.zeros(
            (blocks, value_start - key_width), jnp.bfloat16
        )
        packed[group, :, value_start:] = values[rows]


def compress(raw_keys, raw_values, edge_keys, edge_values, *weights):
    key_expand, _, _, value_expand, _, _ = weights
    units = key_expand.shape[1]
    tokens = raw_keys.shape[0]
    blocks = tokens // STRIDE
    width = round_up(key_expand.shape[0], LANES) + value_expand.shape[0]
    flops = 2 * tokens * units * (raw_keys.shape[1] + raw_values.shape[1])
    return pl.pallas_call(
        compress_kernel,
        out_shape=jax.ShapeDtypeStruct((G, blocks, width), jnp.bfloat16),
        scratch_shapes=[
            pltpu.VMEM(raw_keys.shape, jnp.bfloat16),
            pltpu.VMEM(raw_values.shape, jnp.bfloat16),
            pltpu.VMEM((G * blocks, units), jnp.bfloat16),
        ],
        compiler_params=pltpu.CompilerParams(vmem_limit_bytes=VMEM_LIMIT),
        cost_estimate=pl.CostEstimate(
            flops=flops, bytes_accessed=2 * raw_keys.size, transcendentals=0
        ),
        name="compress",
    )(raw_keys, raw_values, edge_keys, edge_values, *weights)


def cut(weight, shares):
    rows, columns = weight.shape
    share = columns // shares

    def kernel(in_ref, out_ref):
        out_ref[0] = in_ref[...]

    return pl.pallas_call(
        kernel,
        out_shape=jax.ShapeDtypeStruct((shares, rows, share), weight.dtype),
        grid=(shares,),
        in_specs=[pl.BlockSpec((rows, share), lambda i: (0, i))],
        out_specs=pl.BlockSpec((1, rows, share), lambda i: (i, 0, 0)),
        cost_estimate=pl.CostEstimate(flops=0, bytes_accessed=0, transcendentals=0),
        name="cut",
    )(weight)


def project(pieces, weight):
    part, depth = pieces[0].shape
    rows = part * len(pieces)
    columns = weight.shape[1]
    group = len(pieces) // 2

    def kernel(*refs):
        piece_refs, weight_hbm = refs[: len(pieces)], refs[len(pieces)]
        out_ref, rows_ref, weight_ref, sems = refs[len(pieces) + 1 :]
        copies = [
            pltpu.make_async_copy(
                piece, rows_ref.at[index * part : (index + 1) * part], sems.at[index]
            )
            for index, piece in enumerate(piece_refs)
        ]
        bring = pltpu.make_async_copy(weight_hbm, weight_ref, sems.at[len(pieces)])
        bring.start()
        for copy in copies:
            copy.start()
        bring.wait()
        for start in range(0, len(pieces), group):
            for copy in copies[start : start + group]:
                copy.wait()
            place = slice(start * part, (start + group) * part)
            out_ref[place, :] = jnp.dot(
                rows_ref[place, :], weight_ref[...], preferred_element_type=jnp.float32
            ).astype(jnp.bfloat16)

    return pl.pallas_call(
        kernel,
        out_shape=jax.ShapeDtypeStruct((rows, columns), jnp.bfloat16),
        in_specs=[pl.BlockSpec(memory_space=pl.ANY)] * (len(pieces) + 1),
        scratch_shapes=[
            pltpu.VMEM((rows, depth), jnp.bfloat16),
            pltpu.VMEM((depth, columns), jnp.bfloat16),
            pltpu.SemaphoreType.DMA((len(pieces) + 1,)),
        ],
        compiler_params=pltpu.CompilerParams(vmem_limit_bytes=VMEM_LIMIT),
        cost_estimate=pl.CostEstimate(
            flops=PROJECT_WEIGHT * 2 * rows * depth * columns,
            bytes_accessed=2 * rows * depth, transcendentals=0,
        ),
        name="project",
    )(*pieces, weight)


def attend(here, queries, head, packed, limits, places, key_width, masked, layout):
    rows_each = queries[0].shape[0]
    rows = rows_each * len(queries)
    value_start = round_up(key_width, LANES)
    value_width = packed.shape[1] - value_start
    columns = packed.shape[0]
    factor = np.float32(key_width**-0.5 * np.log2(np.e))
    tile = min(256, rows_each)
    unit, outputs, sends = layout

    def kernel(here_ref, *refs):
        query_refs = refs[: len(queries)]
        kv_ref, limit_ref, place_ref = refs[len(queries) : len(queries) + 3]
        out_refs = refs[len(queries) + 3 :]
        keys = kv_ref[:, :key_width]
        values = kv_ref[:, value_start:]
        for start in range(0, rows, tile):
            from_ref, at = query_refs[start // rows_each], start % rows_each
            query = from_ref[at : at + tile, head * key_width : (head + 1) * key_width]
            scores = lax.dot_general(
                query, keys, (((1,), (1,)), ((), ())), preferred_element_type=jnp.float32
            )
            pieces = []
            for low, high, hide in masked:
                piece = scores[:, low:high]
                if hide:
                    visible = limit_ref[:, low:high] <= place_ref[start : start + tile, :]
                    piece = jnp.where(visible, piece, -jnp.inf)
                pieces.append(piece)
            scores = jnp.concatenate(pieces, axis=1) if len(pieces) > 1 else pieces[0]
            top = jnp.max(scores, axis=1, keepdims=True)
            exponent = jnp.exp2((scores - top) * factor)
            total = jnp.sum(exponent, axis=1, keepdims=True)
            numerator = jnp.dot(
                exponent.astype(jnp.bfloat16), values, preferred_element_type=jnp.float32
            )
            done = (numerator / total).astype(jnp.bfloat16)
            for low in range(0, tile, unit):
                which, where = sends((start + low) // unit, here_ref[0], here_ref[1])
                if not isinstance(where, int):
                    where = pl.multiple_of(where, unit)
                out_refs[which][pl.ds(where, unit), :] = done[low : low + unit]

    shape = jax.ShapeDtypeStruct((rows // outputs, value_width), jnp.bfloat16)
    return pl.pallas_call(
        kernel,
        out_shape=(shape,) * outputs,
        in_specs=[pl.BlockSpec(memory_space=pltpu.SMEM)]
        + [pl.BlockSpec(memory_space=pltpu.VMEM)] * (len(queries) + 3),
        compiler_params=pltpu.CompilerParams(vmem_limit_bytes=VMEM_LIMIT),
        cost_estimate=pl.CostEstimate(
            flops=2 * rows * columns * (key_width + value_width),
            bytes_accessed=2 * packed.size,
            transcendentals=0,
        ),
        name="attend",
    )(here, *queries, packed, limits, places)


def expel(place, pieces, weights, before, chunk, chunks, shape):
    rows, width = pieces[0].shape
    depth, step, single = 4 * width, weights[0].shape[1], width // 2
    last = shape is not None

    def kernel(place_ref, *refs):
        own, up, down, passed, far = refs[:5]
        weight_refs = refs[5 : 5 + len(weights)]
        rest = refs[5 + len(weights) :]
        before_refs, outs = rest[: len(before)], rest[len(before) :]
        z, core, y = place_ref[0], place_ref[1] & 1, place_ref[2]
        lower = jnp.where(z == 0, passed[...], up[...])
        upper = jnp.where(z == 3, passed[...], down[...])
        for side, weight in enumerate(weight_refs):
            lanes = slice(side * step, (side + 1) * step)
            total = before_refs[0][:, lanes] if before else None
            for block, at in (
                (own[...], z), (lower, (z + 3) & 3), (upper, (z + 1) & 3), (far[...], z ^ 2)
            ):
                starts = [((at * 2 + inner) * chunks + chunk) * single for inner in (y, 1 - y)]
                both = [weight[pl.ds(pl.multiple_of(start, single), single), :] for start in starts]
                product = jnp.dot(
                    block, jnp.concatenate(both, axis=0), preferred_element_type=jnp.float32
                )
                total = product if total is None else total + product
            if not last:
                outs[0][:, lanes] = total
                continue
            keep_ref, send_ref, hold_ref = outs
            hold_ref[...] = total.reshape(hold_ref.shape)
            keep_ref[:, :, :, lanes] = hold_ref[:, :, pl.ds(core, 1)][:, :, 0]
            send_ref[:, :, :, lanes] = hold_ref[:, :, pl.ds(1 - core, 1)][:, :, 0].astype(jnp.bfloat16)

    columns = step * len(weights)
    if last:
        groups, quarter = shape
        out_shape = (
            jax.ShapeDtypeStruct((groups, 2, quarter, columns), jnp.float32),
            jax.ShapeDtypeStruct((groups, 2, quarter, columns), jnp.bfloat16),
        )
        scratch = [pltpu.VMEM((groups, 2, 2, quarter, step), jnp.float32)]
    else:
        out_shape, scratch = jax.ShapeDtypeStruct((rows, columns), jnp.float32), []
    count = len(pieces) + len(weights) + len(before)
    return pl.pallas_call(
        kernel,
        out_shape=out_shape,
        in_specs=[pl.BlockSpec(memory_space=pltpu.SMEM)]
        + [pl.BlockSpec(memory_space=pltpu.VMEM)] * count,
        scratch_shapes=scratch,
        compiler_params=pltpu.CompilerParams(vmem_limit_bytes=VMEM_LIMIT),
        cost_estimate=pl.CostEstimate(
            flops=2 * rows * depth * columns, bytes_accessed=2 * depth * columns, transcendentals=0
        ),
        name="expel",
    )(place, *pieces, *weights, *before)


def line_pieces(block, axis):
    far = swap(block, axis, 2)
    up = lax.ppermute(block, axis, [(i, i + 1) for i in range(3)])
    down = lax.ppermute(block, axis, [(i + 1, i) for i in range(3)])
    passed = lax.ppermute(far, axis, [(1, 0), (2, 3)])
    return block, up, down, passed, far


def ring_pieces(block, axis):
    before = lax.ppermute(block, axis, [(i, (i + 1) % 4) for i in range(4)])
    after = lax.ppermute(block, axis, [((i + 1) % 4, i) for i in range(4)])
    return block, before, after, swap(block, axis, 2)


def gather_line(block, axis, dim):
    count = lax.axis_size(axis)
    if count != 4:
        return lax.all_gather(block, axis, axis=dim, tiled=True)
    me = lax.axis_index(axis)
    block, before, after, far = ring_pieces(block, axis)
    size = block.shape[dim]
    shape = list(block.shape)
    shape[dim] = count * size
    out = jnp.zeros(shape, block.dtype)
    for piece, place in ((block, me), (before, (me + 3) % 4), (after, (me + 1) % 4), (far, me ^ 2)):
        out = lax.dynamic_update_slice_in_dim(out, piece, place * size, dim)
    return out


def gather_pair(block, axis):
    if lax.axis_size(axis) != 2:
        return lax.all_gather(block, axis, axis=0)
    other = swap(block, axis, 1)
    first = lax.axis_index(axis) == 0
    return jnp.stack([jnp.where(first, block, other), jnp.where(first, other, block)])


def shards(
    tokens, raw_keys, raw_values, query_weight, output_weight,
    key_expand, key_mix, key_reduce, value_expand, value_mix, value_reduce,
):
    outer, inner, heads_axis = (lax.axis_size(name) for name in ("outer", "inner", "head"))
    z, y, h = (lax.axis_index(name) for name in ("outer", "inner", "head"))
    key_width, value_width = key_expand.shape[0], value_expand.shape[0]
    row_count, model = tokens.shape
    devices = outer * inner * heads_axis
    blocks = raw_keys.shape[0] // STRIDE
    context = raw_keys.shape[0] * devices - row_count * outer * inner
    part = query_weight.shape[0]
    fast = inner == 2 and outer == 4 and heads_axis == 4

    seq_axes = ("outer", "inner") if fast else "outer"
    shares = outer * inner if fast else outer
    share = query_weight.shape[1] // shares
    if fast:
        sent = cut(query_weight, shares)
    else:
        sent = jnp.stack([query_weight[:, i * share : (i + 1) * share] for i in range(shares)])
    weight = lax.all_to_all(sent, seq_axes, split_axis=0, concat_axis=0, tiled=True)
    if not fast:
        weight = lax.all_gather(weight, "inner", axis=1)
    weight = weight.reshape(model, share)
    heads_here = share // key_width

    edge = jnp.concatenate([raw_keys[:STRIDE], raw_values[:STRIDE]], axis=1)
    edge = lax.ppermute(
        edge, ("outer", "inner", "head"), [(i + 1, i) for i in range(devices - 1)]
    )
    edge_keys, edge_values = edge[:, : raw_keys.shape[1]], edge[:, raw_keys.shape[1] :]

    if fast:
        quarter = row_count // heads_axis
        mine = lax.dynamic_slice_in_dim(tokens, h * quarter, quarter, 0)
        mine, before, after, far = ring_pieces(mine, "outer")
        first = jnp.concatenate([mine, far], axis=0)
        second = jnp.concatenate([before, after], axis=0)
        first = jnp.concatenate([first, swap(first, "inner", 1)], axis=0)
        second = jnp.concatenate([second, swap(second, "head", 2)], axis=0)
        pieces = [first, second, swap(first, "head", 2), swap(second, "inner", 1)]
        steps = [
            (0, 0, 0), (3, 0, 0), (0, 1, 0), (3, 1, 0), (1, 0, 0), (2, 0, 0), (1, 0, 2), (2, 0, 2),
            (0, 0, 2), (3, 0, 2), (0, 1, 2), (3, 1, 2), (1, 1, 0), (2, 1, 0), (1, 1, 2), (2, 1, 2),
        ]
        steps = steps + [(a, b, k ^ 1) for a, b, k in steps]
        weight, late = lax.optimization_barrier((weight, pieces[3]))
        partners = [swap(piece, "head", 1) for piece in (*pieces[:3], late)]
        queries = [project([*pieces, *partners], weight)]

        def of_block(block, z, h):
            line, side, turn = steps[block]
            there = (z, (z + 3) & 3, (z + 1) & 3, z ^ 2)[line]
            return side, ((h ^ turn) * outer + there) * quarter

        bases = []
        for block, (_, side, _) in enumerate(steps):
            where = of_block(block, z, h)[1] // quarter
            bases.append((where % outer * inner + (y ^ side)) * row_count + where // outer * quarter)
        bases = jnp.stack(bases)[:, None] + jnp.arange(quarter)[None, :]
        layout = (quarter, inner, of_block)
    else:
        every = gather_line(tokens, "outer", 0)
        queries = [jnp.dot(every, weight, preferred_element_type=jnp.float32).astype(jnp.bfloat16)]
        bases = (jnp.arange(outer) * inner + y)[:, None] * row_count + jnp.arange(row_count)[None, :]
        layout = (row_count, 1, lambda block, z, h: (0, block * row_count))
    places = (context + bases).astype(jnp.int32).reshape(-1, 1)
    here = jnp.stack([z, h, y]).astype(jnp.int32)

    packed = compress(
        raw_keys, raw_values, edge_keys, edge_values,
        key_expand, key_mix, key_reduce, value_expand, value_mix, value_reduce,
    )
    ids = np.arange(devices * blocks).reshape(outer, inner, heads_axis, blocks)
    if fast:
        stay = lax.dynamic_index_in_dim(packed, h, 0, False)
        away = [lax.dynamic_index_in_dim(packed, h ^ step, 0, False) for step in (1, 2, 3)]
        came = [swap(piece, "head", step) for step, piece in zip((1, 2, 3), away)]
        packed = jnp.concatenate([stay, *came], axis=0)
        bound = np.broadcast_to(ids.max(axis=(2, 3), keepdims=True), ids.shape)
    else:
        packed = jnp.broadcast_to(packed[:, None], (G, heads_axis // G, *packed.shape[1:]))
        packed = packed.reshape(heads_axis, blocks, -1)
        packed = lax.all_to_all(packed, "head", split_axis=0, concat_axis=0, tiled=True)
        packed = packed.reshape(heads_axis * blocks, -1)
        bound = ids
    packed = gather_line(packed, "outer", 0)
    packed = gather_pair(packed, "inner").reshape(devices * blocks, -1)
    bound = (STRIDE * bound + BLK - 1).transpose(1, 0, 2, 3).reshape(-1)
    hidden = [bool((bound[i : i + LANES] > context).any()) for i in range(0, len(bound), LANES)]
    masked, start = [], 0
    for i in range(1, len(hidden) + 1):
        if i == len(hidden) or hidden[i] != hidden[start]:
            masked.append((start * LANES, min(i * LANES, len(bound)), hidden[start]))
            start = i
    if fast:
        column = np.arange(heads_axis)[None, None, :, None]
        ids = ids[:, :, :1] + (column ^ h) * blocks
        limits = (STRIDE * ids + BLK - 1).transpose(1, 0, 2, 3).reshape(1, -1).astype(jnp.int32)
    else:
        limits = (STRIDE * ids + BLK - 1).transpose(1, 0, 2, 3).reshape(1, -1)
        limits = jnp.asarray(limits, jnp.int32)

    if fast:
        out_weights = [output_weight, swap(output_weight, "inner", 1)]
    else:
        out_weights = lax.all_gather(output_weight, "inner", axis=1, tiled=True)

    total = None
    for head in range(heads_here):
        attended = attend(
            here, queries, head, packed, limits, places, key_width, masked, layout
        )
        if fast:
            last = head == heads_here - 1
            block = jnp.concatenate([attended[0], swap(attended[1], "inner", 1)], axis=1)
            total = expel(
                here, line_pieces(block, "outer"), out_weights, [] if total is None else [total],
                head, heads_here, (heads_axis, quarter) if last else None,
            )
        else:
            attended = gather_line(attended[0], "outer", 1)
            rows = out_weights.reshape(outer, heads_here, value_width, -1)[:, head]
            product = jnp.dot(
                attended, rows.reshape(outer * value_width, -1), preferred_element_type=jnp.float32
            )
            total = product if total is None else total + product

    if fast:
        keep, send = total
        columns = keep.shape[-1]
        total = keep + swap(send, "head", 1).astype(jnp.float32)
        x = h // 2
        keep = lax.dynamic_index_in_dim(total, x, 1, False)
        send = lax.dynamic_index_in_dim(total, 1 - x, 1, False).astype(jnp.bfloat16)
        total = keep + swap(send, "head", 2).astype(jnp.float32)
        result = total.astype(jnp.bfloat16).reshape(row_count, columns)
        first, second = result[:, : columns // 2], result[:, columns // 2 :]
        result = jnp.concatenate(
            [jnp.where(y == 0, first, second), jnp.where(y == 0, second, first)], axis=1
        )
        route = [
            ((a * inner + b) * heads_axis + k, (k * inner + b) * heads_axis + a)
            for a in range(outer) for b in range(inner) for k in range(heads_axis)
        ]
        return lax.ppermute(result, ("outer", "inner", "head"), route)
    columns = total.shape[1]
    total = lax.psum_scatter(total, "head", scatter_dimension=0, tiled=True).astype(jnp.bfloat16)
    total = lax.all_gather(total, "head", axis=0, tiled=True)
    total = lax.all_to_all(
        total.reshape(outer, row_count, columns), "outer", split_axis=0, concat_axis=0, tiled=True
    )
    total = total.transpose(1, 0, 2).reshape(row_count, model)
    return lax.dynamic_slice_in_dim(total, h * (model // heads_axis), model // heads_axis, 1)


def solution(mesh):
    seq_count, head_count = mesh.shape["seq"], mesh.shape["head"]
    inner = seq_count // OUTER
    finer = Mesh(
        mesh.devices.reshape(OUTER, inner, head_count), ("outer", "inner", "head")
    )
    seq = ("outer", "inner")
    in_specs = (
        P(seq, None),
        P((*seq, "head"), None),
        P((*seq, "head"), None),
        P(seq, "head"),
        P("head", seq),
        P(), P(), P(), P(), P(), P(),
    )
    return jax.shard_map(
        shards, mesh=finer, in_specs=in_specs, out_specs=P(seq, "head"), check_vma=False
    )
```

```python
import jax
import jax.numpy as jnp
import numpy as np
from jax import lax
from jax.experimental import pallas as pl
from jax.experimental.pallas import tpu as pltpu
from jax.sharding import Mesh
from jax.sharding import PartitionSpec as P

G = 4
BLK = 32
STRIDE = 16
LANES = 128
OUTER = 4
VMEM_LIMIT = 20 * 1024 * 1024


def round_up(value, unit):
    return -(-value // unit) * unit


def swap(block, axis, bit):
    return lax.ppermute(block, axis, [(i, i ^ bit) for i in range(lax.axis_size(axis))])


def window_of(group, width):
    low = group * width // LANES * LANES
    return low, round_up((group + 1) * width, LANES) - low, group * width - low


def compress_one(raw_ref, edge_ref, expand_ref, mix_ref, reduce_ref, sorted_ref, hidden_ref, groups):
    width, units = expand_ref.shape
    tokens = raw_ref.shape[0]
    rows = 8 * STRIDE
    chunks = tokens // rows
    blocks = tokens // STRIDE
    to = lax.broadcasted_iota(jnp.int32, (rows, rows), 0)
    come = lax.broadcasted_iota(jnp.int32, (rows, rows), 1)
    order = (come == (to % 8) * STRIDE + to // 8).astype(jnp.bfloat16)
    for chunk in range(chunks):
        piece = slice(chunk * rows, (chunk + 1) * rows)
        sorted_ref[piece, :] = jnp.dot(
            order, raw_ref[piece, :], preferred_element_type=jnp.float32
        ).astype(jnp.bfloat16)
    tile = 256 if units % 256 == 0 else units
    for group in range(groups):
        low, span, offset = window_of(group, width)
        parts = []
        if offset:
            parts.append(jnp.zeros((offset, units), jnp.bfloat16))
        parts.append(expand_ref[...])
        if span - offset - width:
            parts.append(jnp.zeros((span - offset - width, units), jnp.bfloat16))
        expand = jnp.concatenate(parts, axis=0) if len(parts) > 1 else parts[0]
        for start in range(0, units, tile):
            lanes = slice(start, start + tile)
            weight = expand[:, lanes]
            projected = jnp.dot(
                sorted_ref[:, low : low + span], weight, preferred_element_type=jnp.float32
            ).reshape(chunks, STRIDE, 8, tile)
            mix_low = mix_ref[:STRIDE, lanes][None, :, None, :]
            mix_high = mix_ref[STRIDE:, lanes]
            first = jnp.sum(projected * mix_low, axis=1).reshape(blocks, tile)
            second = jnp.sum(projected * mix_high[None, :, None, :], axis=1).reshape(blocks, tile)
            edge = jnp.dot(edge_ref[:, low : low + span], weight, preferred_element_type=jnp.float32)
            edge = jnp.sum(edge * mix_high, axis=0, keepdims=True)
            hidden = first + jnp.concatenate([second[1:], edge], axis=0)
            half = 0.5 * hidden
            activated = half + half * lax.erf(hidden * np.float32(2.0**-0.5))
            hidden_ref[group * blocks : (group + 1) * blocks, lanes] = activated.astype(jnp.bfloat16)
    return jnp.dot(hidden_ref[...], reduce_ref[...], preferred_element_type=jnp.float32).astype(
        jnp.bfloat16
    )


def compress_kernel(
    raw_keys, raw_values, edge_keys, edge_values, key_expand, key_mix, key_reduce,
    value_expand, value_mix, value_reduce, packed, sorted_keys, sorted_values, hidden,
):
    groups, blocks, _ = packed.shape
    key_width = key_expand.shape[0]
    value_start = round_up(key_width, LANES)
    keys = compress_one(
        raw_keys, edge_keys, key_expand, key_mix, key_reduce, sorted_keys, hidden, groups
    )
    values = compress_one(
        raw_values, edge_values, value_expand, value_mix, value_reduce, sorted_values, hidden, groups
    )
    for group in range(groups):
        rows = slice(group * blocks, (group + 1) * blocks)
        packed[group, :, :key_width] = keys[rows]
        packed[group, :, key_width:value_start] = jnp.zeros(
            (blocks, value_start - key_width), jnp.bfloat16
        )
        packed[group, :, value_start:] = values[rows]


def compress(raw_keys, raw_values, edge_keys, edge_values, *weights):
    key_expand, _, _, value_expand, _, _ = weights
    units = key_expand.shape[1]
    tokens = raw_keys.shape[0]
    blocks = tokens // STRIDE
    width = round_up(key_expand.shape[0], LANES) + value_expand.shape[0]
    flops = 2 * tokens * units * (raw_keys.shape[1] + raw_values.shape[1])
    return pl.pallas_call(
        compress_kernel,
        out_shape=jax.ShapeDtypeStruct((G, blocks, width), jnp.bfloat16),
        scratch_shapes=[
            pltpu.VMEM(raw_keys.shape, jnp.bfloat16),
            pltpu.VMEM(raw_values.shape, jnp.bfloat16),
            pltpu.VMEM((G * blocks, units), jnp.bfloat16),
        ],
        compiler_params=pltpu.CompilerParams(vmem_limit_bytes=VMEM_LIMIT),
        cost_estimate=pl.CostEstimate(
            flops=flops, bytes_accessed=2 * raw_keys.size, transcendentals=0
        ),
        name="compress",
    )(raw_keys, raw_values, edge_keys, edge_values, *weights)


def cut(weight, shares, parts):
    rows, columns = weight.shape
    share, part = columns // shares, rows // parts

    def kernel(in_ref, *out_refs):
        for index, out_ref in enumerate(out_refs):
            out_ref[0] = in_ref[index * part : (index + 1) * part, :]

    return pl.pallas_call(
        kernel,
        out_shape=(jax.ShapeDtypeStruct((shares, part, share), weight.dtype),) * parts,
        grid=(shares,),
        in_specs=[pl.BlockSpec((rows, share), lambda i: (0, i))],
        out_specs=(pl.BlockSpec((1, part, share), lambda i: (i, 0, 0)),) * parts,
        cost_estimate=pl.CostEstimate(flops=0, bytes_accessed=0, transcendentals=0),
        name="cut",
    )(weight)


def project(pieces, weights):
    part, depth = pieces[0].shape
    rows = part * len(pieces)
    shares, share, columns = weights[0].shape
    group = len(pieces) // 2
    count = len(pieces)

    def kernel(*refs):
        piece_refs, weight_refs = refs[:count], refs[count : count + len(weights)]
        out_ref, rows_ref, weight_ref, sems = refs[count + len(weights) :]
        copies = [
            pltpu.make_async_copy(
                piece, rows_ref.at[index * part : (index + 1) * part], sems.at[index]
            )
            for index, piece in enumerate(piece_refs)
        ]
        bring = []
        for index, weight in enumerate(weight_refs):
            for owner in range(shares):
                start = (owner * len(weights) + index) * share
                bring.append(
                    pltpu.make_async_copy(
                        weight.at[owner], weight_ref.at[start : start + share],
                        sems.at[count + len(bring)],
                    )
                )
        for copy in bring + copies:
            copy.start()
        for copy in bring:
            copy.wait()
        for start in range(0, count, group):
            for copy in copies[start : start + group]:
                copy.wait()
            place = slice(start * part, (start + group) * part)
            out_ref[place, :] = jnp.dot(
                rows_ref[place, :], weight_ref[...], preferred_element_type=jnp.float32
            ).astype(jnp.bfloat16)

    return pl.pallas_call(
        kernel,
        out_shape=jax.ShapeDtypeStruct((rows, columns), jnp.bfloat16),
        in_specs=[pl.BlockSpec(memory_space=pl.ANY)] * (count + len(weights)),
        scratch_shapes=[
            pltpu.VMEM((rows, depth), jnp.bfloat16),
            pltpu.VMEM((depth, columns), jnp.bfloat16),
            pltpu.SemaphoreType.DMA((count + len(weights) * shares,)),
        ],
        compiler_params=pltpu.CompilerParams(vmem_limit_bytes=VMEM_LIMIT),
        cost_estimate=pl.CostEstimate(
            flops=2 * rows * depth * columns, bytes_accessed=2 * rows * depth, transcendentals=0
        ),
        name="project",
    )(*pieces, *weights)


def attend(here, queries, head, packed, limits, places, key_width, masked, layout):
    rows_each = queries[0].shape[0]
    rows = rows_each * len(queries)
    value_start = round_up(key_width, LANES)
    value_width = packed.shape[1] - value_start
    columns = packed.shape[0]
    factor = np.float32(key_width**-0.5 * np.log2(np.e))
    tile = min(256, rows_each)
    unit, outputs, sends = layout

    def kernel(here_ref, *refs):
        query_refs = refs[: len(queries)]
        kv_ref, limit_ref, place_ref = refs[len(queries) : len(queries) + 3]
        out_refs = refs[len(queries) + 3 :]
        keys = kv_ref[:, :key_width]
        values = kv_ref[:, value_start:]
        for start in range(0, rows, tile):
            from_ref, at = query_refs[start // rows_each], start % rows_each
            query = from_ref[at : at + tile, head * key_width : (head + 1) * key_width]
            scores = lax.dot_general(
                query, keys, (((1,), (1,)), ((), ())), preferred_element_type=jnp.float32
            )
            pieces = []
            for low, high, hide in masked:
                piece = scores[:, low:high]
                if hide:
                    visible = limit_ref[:, low:high] <= place_ref[start : start + tile, :]
                    piece = jnp.where(visible, piece, -jnp.inf)
                pieces.append(piece)
            scores = jnp.concatenate(pieces, axis=1) if len(pieces) > 1 else pieces[0]
            top = jnp.max(scores, axis=1, keepdims=True)
            exponent = jnp.exp2((scores - top) * factor)
            total = jnp.sum(exponent, axis=1, keepdims=True)
            numerator = jnp.dot(
                exponent.astype(jnp.bfloat16), values, preferred_element_type=jnp.float32
            )
            done = (numerator / total).astype(jnp.bfloat16)
            for low in range(0, tile, unit):
                which, where = sends((start + low) // unit, here_ref[0], here_ref[1])
                if not isinstance(where, int):
                    where = pl.multiple_of(where, unit)
                out_refs[which][pl.ds(where, unit), :] = done[low : low + unit]

    shape = jax.ShapeDtypeStruct((rows // outputs, value_width), jnp.bfloat16)
    return pl.pallas_call(
        kernel,
        out_shape=(shape,) * outputs,
        in_specs=[pl.BlockSpec(memory_space=pltpu.SMEM)]
        + [pl.BlockSpec(memory_space=pltpu.VMEM)] * (len(queries) + 3),
        compiler_params=pltpu.CompilerParams(vmem_limit_bytes=VMEM_LIMIT),
        cost_estimate=pl.CostEstimate(
            flops=2 * rows * columns * (key_width + value_width),
            bytes_accessed=2 * packed.size,
            transcendentals=0,
        ),
        name="attend",
    )(here, *queries, packed, limits, places)


def expel(place, pieces, weights, before, chunk, chunks, shape):
    rows, width = pieces[0].shape
    depth, step, single = 4 * width, weights[0].shape[1], width // 2
    last = shape is not None

    def kernel(place_ref, *refs):
        own, up, down, passed, far = refs[:5]
        weight_refs = refs[5 : 5 + len(weights)]
        rest = refs[5 + len(weights) :]
        before_refs, outs = rest[: len(before)], rest[len(before) :]
        z, core, y = place_ref[0], place_ref[1] & 1, place_ref[2]
        lower = jnp.where(z == 0, passed[...], up[...])
        upper = jnp.where(z == 3, passed[...], down[...])
        for side, weight in enumerate(weight_refs):
            lanes = slice(side * step, (side + 1) * step)
            total = before_refs[0][:, lanes] if before else None
            for block, at in (
                (own[...], z), (lower, (z + 3) & 3), (upper, (z + 1) & 3), (far[...], z ^ 2)
            ):
                starts = [((at * 2 + inner) * chunks + chunk) * single for inner in (y, 1 - y)]
                both = [weight[pl.ds(pl.multiple_of(start, single), single), :] for start in starts]
                product = jnp.dot(
                    block, jnp.concatenate(both, axis=0), preferred_element_type=jnp.float32
                )
                total = product if total is None else total + product
            if not last:
                outs[0][:, lanes] = total
                continue
            keep_ref, send_ref, hold_ref = outs
            hold_ref[...] = total.reshape(hold_ref.shape)
            keep_ref[:, :, :, lanes] = hold_ref[:, :, pl.ds(core, 1)][:, :, 0]
            send_ref[:, :, :, lanes] = hold_ref[:, :, pl.ds(1 - core, 1)][:, :, 0].astype(jnp.bfloat16)

    columns = step * len(weights)
    if last:
        groups, quarter = shape
        out_shape = (
            jax.ShapeDtypeStruct((groups, 2, quarter, columns), jnp.float32),
            jax.ShapeDtypeStruct((groups, 2, quarter, columns), jnp.bfloat16),
        )
        scratch = [pltpu.VMEM((groups, 2, 2, quarter, step), jnp.float32)]
    else:
        out_shape, scratch = jax.ShapeDtypeStruct((rows, columns), jnp.float32), []
    count = len(pieces) + len(weights) + len(before)
    return pl.pallas_call(
        kernel,
        out_shape=out_shape,
        in_specs=[pl.BlockSpec(memory_space=pltpu.SMEM)]
        + [pl.BlockSpec(memory_space=pltpu.VMEM)] * count,
        scratch_shapes=scratch,
        compiler_params=pltpu.CompilerParams(vmem_limit_bytes=VMEM_LIMIT),
        cost_estimate=pl.CostEstimate(
            flops=2 * rows * depth * columns, bytes_accessed=2 * depth * columns, transcendentals=0
        ),
        name="expel",
    )(place, *pieces, *weights, *before)


def line_pieces(block, axis):
    far = swap(block, axis, 2)
    up = lax.ppermute(block, axis, [(i, i + 1) for i in range(3)])
    down = lax.ppermute(block, axis, [(i + 1, i) for i in range(3)])
    passed = lax.ppermute(far, axis, [(1, 0), (2, 3)])
    return block, up, down, passed, far


def ring_pieces(block, axis):
    before = lax.ppermute(block, axis, [(i, (i + 1) % 4) for i in range(4)])
    after = lax.ppermute(block, axis, [((i + 1) % 4, i) for i in range(4)])
    return block, before, after, swap(block, axis, 2)


def gather_line(block, axis, dim):
    count = lax.axis_size(axis)
    if count != 4:
        return lax.all_gather(block, axis, axis=dim, tiled=True)
    me = lax.axis_index(axis)
    block, before, after, far = ring_pieces(block, axis)
    size = block.shape[dim]
    shape = list(block.shape)
    shape[dim] = count * size
    out = jnp.zeros(shape, block.dtype)
    for piece, place in ((block, me), (before, (me + 3) % 4), (after, (me + 1) % 4), (far, me ^ 2)):
        out = lax.dynamic_update_slice_in_dim(out, piece, place * size, dim)
    return out


def gather_pair(block, axis):
    if lax.axis_size(axis) != 2:
        return lax.all_gather(block, axis, axis=0)
    other = swap(block, axis, 1)
    first = lax.axis_index(axis) == 0
    return jnp.stack([jnp.where(first, block, other), jnp.where(first, other, block)])


def shards(
    tokens, raw_keys, raw_values, query_weight, output_weight,
    key_expand, key_mix, key_reduce, value_expand, value_mix, value_reduce,
):
    outer, inner, heads_axis = (lax.axis_size(name) for name in ("outer", "inner", "head"))
    z, y, h = (lax.axis_index(name) for name in ("outer", "inner", "head"))
    key_width, value_width = key_expand.shape[0], value_expand.shape[0]
    row_count, model = tokens.shape
    devices = outer * inner * heads_axis
    blocks = raw_keys.shape[0] // STRIDE
    context = raw_keys.shape[0] * devices - row_count * outer * inner
    part = query_weight.shape[0]
    fast = inner == 2 and outer == 4 and heads_axis == 4

    seq_axes = ("outer", "inner") if fast else "outer"
    shares = outer * inner if fast else outer
    share = query_weight.shape[1] // shares

    def exchange(block):
        return lax.all_to_all(block, seq_axes, split_axis=0, concat_axis=0, tiled=True)

    if fast:
        sent = cut(query_weight, shares, 2)
    else:
        weight = exchange(
            jnp.stack([query_weight[:, i * share : (i + 1) * share] for i in range(shares)])
        )
        weight = lax.all_gather(weight, "inner", axis=1).reshape(model, share)
    heads_here = share // key_width

    edge = jnp.concatenate([raw_keys[:STRIDE], raw_values[:STRIDE]], axis=1)
    edge = lax.ppermute(
        edge, ("outer", "inner", "head"), [(i + 1, i) for i in range(devices - 1)]
    )
    edge_keys, edge_values = edge[:, : raw_keys.shape[1]], edge[:, raw_keys.shape[1] :]

    if fast:
        quarter = row_count // heads_axis
        mine = lax.dynamic_slice_in_dim(tokens, h * quarter, quarter, 0)
        mine, before, after, far = ring_pieces(mine, "outer")
        begin, before, after, far, raw_keys, raw_values = lax.optimization_barrier(
            (sent[0], before, after, far, raw_keys, raw_values)
        )
        weight_first = exchange(begin)
        first = jnp.concatenate([mine, far], axis=0)
        second = jnp.concatenate([before, after], axis=0)
        first = jnp.concatenate([first, swap(first, "inner", 1)], axis=0)
        second = jnp.concatenate([second, swap(second, "head", 2)], axis=0)
        pieces = [first, second, swap(first, "head", 2), swap(second, "inner", 1)]
        steps = [
            (0, 0, 0), (3, 0, 0), (0, 1, 0), (3, 1, 0), (1, 0, 0), (2, 0, 0), (1, 0, 2), (2, 0, 2),
            (0, 0, 2), (3, 0, 2), (0, 1, 2), (3, 1, 2), (1, 1, 0), (2, 1, 0), (1, 1, 2), (2, 1, 2),
        ]
        steps = steps + [(a, b, k ^ 1) for a, b, k in steps]
        partners = [swap(piece, "head", 1) for piece in pieces]

        def of_block(block, z, h):
            line, side, turn = steps[block]
            there = (z, (z + 3) & 3, (z + 1) & 3, z ^ 2)[line]
            return side, ((h ^ turn) * outer + there) * quarter

        bases = []
        for block, (_, side, _) in enumerate(steps):
            where = of_block(block, z, h)[1] // quarter
            bases.append((where % outer * inner + (y ^ side)) * row_count + where // outer * quarter)
        bases = jnp.stack(bases)[:, None] + jnp.arange(quarter)[None, :]
        layout = (quarter, inner, of_block)
    else:
        every = gather_line(tokens, "outer", 0)
        queries = [jnp.dot(every, weight, preferred_element_type=jnp.float32).astype(jnp.bfloat16)]
        bases = (jnp.arange(outer) * inner + y)[:, None] * row_count + jnp.arange(row_count)[None, :]
        layout = (row_count, 1, lambda block, z, h: (0, block * row_count))
    places = (context + bases).astype(jnp.int32).reshape(-1, 1)
    here = jnp.stack([z, h, y]).astype(jnp.int32)

    packed = compress(
        raw_keys, raw_values, edge_keys, edge_values,
        key_expand, key_mix, key_reduce, value_expand, value_mix, value_reduce,
    )
    ids = np.arange(devices * blocks).reshape(outer, inner, heads_axis, blocks)
    if fast:
        stay = lax.dynamic_index_in_dim(packed, h, 0, False)
        away = [lax.dynamic_index_in_dim(packed, h ^ step, 0, False) for step in (1, 2, 3)]
        came = [swap(piece, "head", step) for step, piece in zip((1, 2, 3), away)]
        packed = jnp.concatenate([stay, *came], axis=0)
        bound = np.broadcast_to(ids.max(axis=(2, 3), keepdims=True), ids.shape)
    else:
        packed = jnp.broadcast_to(packed[:, None], (G, heads_axis // G, *packed.shape[1:]))
        packed = packed.reshape(heads_axis, blocks, -1)
        packed = lax.all_to_all(packed, "head", split_axis=0, concat_axis=0, tiled=True)
        packed = packed.reshape(heads_axis * blocks, -1)
        bound = ids
    packed = gather_line(packed, "outer", 0)
    if fast:
        begin, packed = lax.optimization_barrier((sent[1], packed))
        queries = [project([*pieces, *partners], [weight_first, exchange(begin)])]
    packed = gather_pair(packed, "inner").reshape(devices * blocks, -1)
    bound = (STRIDE * bound + BLK - 1).transpose(1, 0, 2, 3).reshape(-1)
    hidden = [bool((bound[i : i + LANES] > context).any()) for i in range(0, len(bound), LANES)]
    masked, start = [], 0
    for i in range(1, len(hidden) + 1):
        if i == len(hidden) or hidden[i] != hidden[start]:
            masked.append((start * LANES, min(i * LANES, len(bound)), hidden[start]))
            start = i
    if fast:
        column = np.arange(heads_axis)[None, None, :, None]
        ids = ids[:, :, :1] + (column ^ h) * blocks
        limits = (STRIDE * ids + BLK - 1).transpose(1, 0, 2, 3).reshape(1, -1).astype(jnp.int32)
    else:
        limits = (STRIDE * ids + BLK - 1).transpose(1, 0, 2, 3).reshape(1, -1)
        limits = jnp.asarray(limits, jnp.int32)

    if fast:
        out_weights = [output_weight, swap(output_weight, "inner", 1)]
    else:
        out_weights = lax.all_gather(output_weight, "inner", axis=1, tiled=True)

    total = None
    for head in range(heads_here):
        attended = attend(
            here, queries, head, packed, limits, places, key_width, masked, layout
        )
        if fast:
            last = head == heads_here - 1
            block = jnp.concatenate([attended[0], swap(attended[1], "inner", 1)], axis=1)
            total = expel(
                here, line_pieces(block, "outer"), out_weights, [] if total is None else [total],
                head, heads_here, (heads_axis, quarter) if last else None,
            )
        else:
            attended = gather_line(attended[0], "outer", 1)
            rows = out_weights.reshape(outer, heads_here, value_width, -1)[:, head]
            product = jnp.dot(
                attended, rows.reshape(outer * value_width, -1), preferred_element_type=jnp.float32
            )
            total = product if total is None else total + product

    if fast:
        keep, send = total
        columns = keep.shape[-1]
        total = keep + swap(send, "head", 1).astype(jnp.float32)
        x = h // 2
        keep = lax.dynamic_index_in_dim(total, x, 1, False)
        send = lax.dynamic_index_in_dim(total, 1 - x, 1, False).astype(jnp.bfloat16)
        total = keep + swap(send, "head", 2).astype(jnp.float32)
        result = total.astype(jnp.bfloat16).reshape(row_count, columns)
        first, second = result[:, : columns // 2], result[:, columns // 2 :]
        result = jnp.concatenate(
            [jnp.where(y == 0, first, second), jnp.where(y == 0, second, first)], axis=1
        )
        route = [
            ((a * inner + b) * heads_axis + k, (k * inner + b) * heads_axis + a)
            for a in range(outer) for b in range(inner) for k in range(heads_axis)
        ]
        return lax.ppermute(result, ("outer", "inner", "head"), route)
    columns = total.shape[1]
    total = lax.psum_scatter(total, "head", scatter_dimension=0, tiled=True).astype(jnp.bfloat16)
    total = lax.all_gather(total, "head", axis=0, tiled=True)
    total = lax.all_to_all(
        total.reshape(outer, row_count, columns), "outer", split_axis=0, concat_axis=0, tiled=True
    )
    total = total.transpose(1, 0, 2).reshape(row_count, model)
    return lax.dynamic_slice_in_dim(total, h * (model // heads_axis), model // heads_axis, 1)


def solution(mesh):
    seq_count, head_count = mesh.shape["seq"], mesh.shape["head"]
    inner = seq_count // OUTER
    finer = Mesh(
        mesh.devices.reshape(OUTER, inner, head_count), ("outer", "inner", "head")
    )
    seq = ("outer", "inner")
    in_specs = (
        P(seq, None),
        P((*seq, "head"), None),
        P((*seq, "head"), None),
        P(seq, "head"),
        P("head", seq),
        P(), P(), P(), P(), P(), P(),
    )
    return jax.shard_map(
        shards, mesh=finer, in_specs=in_specs, out_specs=P(seq, "head"), check_vma=False
    )
```

```python
import jax
import jax.numpy as jnp
import numpy as np
from jax import lax
from jax.experimental import pallas as pl
from jax.experimental.pallas import tpu as pltpu
from jax.sharding import Mesh
from jax.sharding import PartitionSpec as P

G = 4
BLK = 32
STRIDE = 16
LANES = 128
OUTER = 4
VMEM_LIMIT = 20 * 1024 * 1024


def round_up(value, unit):
    return -(-value // unit) * unit


def swap(block, axis, bit):
    return lax.ppermute(block, axis, [(i, i ^ bit) for i in range(lax.axis_size(axis))])


def window_of(group, width):
    low = group * width // LANES * LANES
    return low, round_up((group + 1) * width, LANES) - low, group * width - low


def compress_one(raw_ref, edge_ref, expand_ref, mix_ref, reduce_ref, sorted_ref, hidden_ref, groups):
    width, units = expand_ref.shape
    tokens = raw_ref.shape[0]
    rows = 8 * STRIDE
    chunks = tokens // rows
    blocks = tokens // STRIDE
    to = lax.broadcasted_iota(jnp.int32, (rows, rows), 0)
    come = lax.broadcasted_iota(jnp.int32, (rows, rows), 1)
    order = (come == (to % 8) * STRIDE + to // 8).astype(jnp.bfloat16)
    for chunk in range(chunks):
        piece = slice(chunk * rows, (chunk + 1) * rows)
        sorted_ref[piece, :] = jnp.dot(
            order, raw_ref[piece, :], preferred_element_type=jnp.float32
        ).astype(jnp.bfloat16)
    tile = 256 if units % 256 == 0 else units
    for group in range(groups):
        low, span, offset = window_of(group, width)
        parts = []
        if offset:
            parts.append(jnp.zeros((offset, units), jnp.bfloat16))
        parts.append(expand_ref[...])
        if span - offset - width:
            parts.append(jnp.zeros((span - offset - width, units), jnp.bfloat16))
        expand = jnp.concatenate(parts, axis=0) if len(parts) > 1 else parts[0]
        for start in range(0, units, tile):
            lanes = slice(start, start + tile)
            weight = expand[:, lanes]
            projected = jnp.dot(
                sorted_ref[:, low : low + span], weight, preferred_element_type=jnp.float32
            ).reshape(chunks, STRIDE, 8, tile)
            mix_low = mix_ref[:STRIDE, lanes][None, :, None, :]
            mix_high = mix_ref[STRIDE:, lanes]
            first = jnp.sum(projected * mix_low, axis=1).reshape(blocks, tile)
            second = jnp.sum(projected * mix_high[None, :, None, :], axis=1).reshape(blocks, tile)
            edge = jnp.dot(edge_ref[:, low : low + span], weight, preferred_element_type=jnp.float32)
            edge = jnp.sum(edge * mix_high, axis=0, keepdims=True)
            hidden = first + jnp.concatenate([second[1:], edge], axis=0)
            half = 0.5 * hidden
            activated = half + half * lax.erf(hidden * np.float32(2.0**-0.5))
            hidden_ref[group * blocks : (group + 1) * blocks, lanes] = activated.astype(jnp.bfloat16)
    return jnp.dot(hidden_ref[...], reduce_ref[...], preferred_element_type=jnp.float32).astype(
        jnp.bfloat16
    )


def compress_kernel(
    raw_keys, raw_values, edge_keys, edge_values, key_expand, key_mix, key_reduce,
    value_expand, value_mix, value_reduce, packed, sorted_keys, sorted_values, hidden,
):
    groups, blocks, _ = packed.shape
    key_width = key_expand.shape[0]
    value_start = round_up(key_width, LANES)
    keys = compress_one(
        raw_keys, edge_keys, key_expand, key_mix, key_reduce, sorted_keys, hidden, groups
    )
    values = compress_one(
        raw_values, edge_values, value_expand, value_mix, value_reduce, sorted_values, hidden, groups
    )
    for group in range(groups):
        rows = slice(group * blocks, (group + 1) * blocks)
        packed[group, :, :key_width] = keys[rows]
        packed[group, :, key_width:value_start] = jnp.zeros(
            (blocks, value_start - key_width), jnp.bfloat16
        )
        packed[group, :, value_start:] = values[rows]


def compress(raw_keys, raw_values, edge_keys, edge_values, *weights):
    key_expand, _, _, value_expand, _, _ = weights
    units = key_expand.shape[1]
    tokens = raw_keys.shape[0]
    blocks = tokens // STRIDE
    width = round_up(key_expand.shape[0], LANES) + value_expand.shape[0]
    flops = 2 * tokens * units * (raw_keys.shape[1] + raw_values.shape[1])
    return pl.pallas_call(
        compress_kernel,
        out_shape=jax.ShapeDtypeStruct((G, blocks, width), jnp.bfloat16),
        scratch_shapes=[
            pltpu.VMEM(raw_keys.shape, jnp.bfloat16),
            pltpu.VMEM(raw_values.shape, jnp.bfloat16),
            pltpu.VMEM((G * blocks, units), jnp.bfloat16),
        ],
        compiler_params=pltpu.CompilerParams(vmem_limit_bytes=VMEM_LIMIT),
        cost_estimate=pl.CostEstimate(
            flops=flops, bytes_accessed=2 * raw_keys.size, transcendentals=0
        ),
        name="compress",
    )(raw_keys, raw_values, edge_keys, edge_values, *weights)


def cut(weight, shares, parts):
    rows, columns = weight.shape
    share, part = columns // shares, rows // parts

    def kernel(in_ref, *out_refs):
        for index, out_ref in enumerate(out_refs):
            out_ref[0] = in_ref[index * part : (index + 1) * part, :]

    return pl.pallas_call(
        kernel,
        out_shape=(jax.ShapeDtypeStruct((shares, part, share), weight.dtype),) * parts,
        grid=(shares,),
        in_specs=[pl.BlockSpec((rows, share), lambda i: (0, i))],
        out_specs=(pl.BlockSpec((1, part, share), lambda i: (i, 0, 0)),) * parts,
        cost_estimate=pl.CostEstimate(flops=0, bytes_accessed=0, transcendentals=0),
        name="cut",
    )(weight)


def project(pieces, weights):
    part, depth = pieces[0].shape
    rows = part * len(pieces)
    shares, share, columns = weights[0].shape
    group = len(pieces) // 2
    count = len(pieces)

    def kernel(*refs):
        piece_refs, weight_refs = refs[:count], refs[count : count + len(weights)]
        out_ref, rows_ref, weight_ref, sems = refs[count + len(weights) :]
        copies = [
            pltpu.make_async_copy(
                piece, rows_ref.at[index * part : (index + 1) * part], sems.at[index]
            )
            for index, piece in enumerate(piece_refs)
        ]
        bring = []
        for index, weight in enumerate(weight_refs):
            for owner in range(shares):
                start = (owner * len(weights) + index) * share
                bring.append(
                    pltpu.make_async_copy(
                        weight.at[owner], weight_ref.at[start : start + share],
                        sems.at[count + len(bring)],
                    )
                )
        for copy in bring + copies:
            copy.start()
        for copy in bring:
            copy.wait()
        for start in range(0, count, group):
            for copy in copies[start : start + group]:
                copy.wait()
            place = slice(start * part, (start + group) * part)
            out_ref[place, :] = jnp.dot(
                rows_ref[place, :], weight_ref[...], preferred_element_type=jnp.float32
            ).astype(jnp.bfloat16)

    return pl.pallas_call(
        kernel,
        out_shape=jax.ShapeDtypeStruct((rows, columns), jnp.bfloat16),
        in_specs=[pl.BlockSpec(memory_space=pl.ANY)] * (count + len(weights)),
        scratch_shapes=[
            pltpu.VMEM((rows, depth), jnp.bfloat16),
            pltpu.VMEM((depth, columns), jnp.bfloat16),
            pltpu.SemaphoreType.DMA((count + len(weights) * shares,)),
        ],
        compiler_params=pltpu.CompilerParams(vmem_limit_bytes=VMEM_LIMIT),
        cost_estimate=pl.CostEstimate(
            flops=2 * rows * depth * columns, bytes_accessed=2 * rows * depth, transcendentals=0
        ),
        name="project",
    )(*pieces, *weights)


def attend(here, queries, head, packed, limits, places, key_width, masked, layout):
    rows_each = queries[0].shape[0]
    rows = rows_each * len(queries)
    value_start = round_up(key_width, LANES)
    value_width = packed.shape[1] - value_start
    columns = packed.shape[0]
    factor = np.float32(key_width**-0.5 * np.log2(np.e))
    tile = min(256, rows_each)
    unit, outputs, sends = layout

    def kernel(here_ref, *refs):
        query_refs = refs[: len(queries)]
        kv_ref, limit_ref, place_ref = refs[len(queries) : len(queries) + 3]
        out_refs = refs[len(queries) + 3 :]
        keys = kv_ref[:, :key_width]
        values = kv_ref[:, value_start:]
        for start in range(0, rows, tile):
            from_ref, at = query_refs[start // rows_each], start % rows_each
            query = from_ref[at : at + tile, head * key_width : (head + 1) * key_width]
            scores = lax.dot_general(
                query, keys, (((1,), (1,)), ((), ())), preferred_element_type=jnp.float32
            )
            pieces = []
            for low, high, hide in masked:
                piece = scores[:, low:high]
                if hide:
                    visible = limit_ref[:, low:high] <= place_ref[start : start + tile, :]
                    piece = jnp.where(visible, piece, -jnp.inf)
                pieces.append(piece)
            scores = jnp.concatenate(pieces, axis=1) if len(pieces) > 1 else pieces[0]
            top = jnp.max(scores, axis=1, keepdims=True)
            exponent = jnp.exp2((scores - top) * factor)
            total = jnp.sum(exponent, axis=1, keepdims=True)
            numerator = jnp.dot(
                exponent.astype(jnp.bfloat16), values, preferred_element_type=jnp.float32
            )
            done = (numerator / total).astype(jnp.bfloat16)
            for low in range(0, tile, unit):
                which, where = sends((start + low) // unit, here_ref[0], here_ref[1])
                if not isinstance(where, int):
                    where = pl.multiple_of(where, unit)
                out_refs[which][pl.ds(where, unit), :] = done[low : low + unit]

    shape = jax.ShapeDtypeStruct((rows // outputs, value_width), jnp.bfloat16)
    return pl.pallas_call(
        kernel,
        out_shape=(shape,) * outputs,
        in_specs=[pl.BlockSpec(memory_space=pltpu.SMEM)]
        + [pl.BlockSpec(memory_space=pltpu.VMEM)] * (len(queries) + 3),
        compiler_params=pltpu.CompilerParams(vmem_limit_bytes=VMEM_LIMIT),
        cost_estimate=pl.CostEstimate(
            flops=2 * rows * columns * (key_width + value_width),
            bytes_accessed=2 * packed.size,
            transcendentals=0,
        ),
        name="attend",
    )(here, *queries, packed, limits, places)


def expel(place, pieces, weights, before, chunk, chunks, shape):
    rows, width = pieces[0].shape
    depth, step, single = 4 * width, weights[0].shape[0], width // 2
    last = shape is not None

    def kernel(place_ref, *refs):
        own, up, down, passed, far = refs[:5]
        weight_refs = refs[5 : 5 + len(weights)]
        rest = refs[5 + len(weights) :]
        before_refs, outs = rest[: len(before)], rest[len(before) :]
        z, core, y = place_ref[0], place_ref[1] & 1, place_ref[2]
        lower = jnp.where(z == 0, passed[...], up[...])
        upper = jnp.where(z == 3, passed[...], down[...])
        for side, weight in enumerate(weight_refs):
            lanes = slice(side * step, (side + 1) * step)
            total = before_refs[0][:, lanes] if before else None
            for block, at in (
                (own[...], z), (lower, (z + 3) & 3), (upper, (z + 1) & 3), (far[...], z ^ 2)
            ):
                starts = [((at * 2 + inner) * chunks + chunk) * single for inner in (y, 1 - y)]
                both = [weight[:, pl.ds(pl.multiple_of(start, single), single)] for start in starts]
                product = lax.dot_general(
                    block, jnp.concatenate(both, axis=1), (((1,), (1,)), ((), ())),
                    preferred_element_type=jnp.float32,
                )
                total = product if total is None else total + product
            if not last:
                outs[0][:, lanes] = total
                continue
            keep_ref, send_ref, hold_ref = outs
            hold_ref[...] = total.reshape(hold_ref.shape)
            keep_ref[:, :, :, lanes] = hold_ref[:, :, pl.ds(core, 1)][:, :, 0]
            send_ref[:, :, :, lanes] = hold_ref[:, :, pl.ds(1 - core, 1)][:, :, 0].astype(jnp.bfloat16)

    columns = step * len(weights)
    if last:
        groups, quarter = shape
        out_shape = (
            jax.ShapeDtypeStruct((groups, 2, quarter, columns), jnp.float32),
            jax.ShapeDtypeStruct((groups, 2, quarter, columns), jnp.bfloat16),
        )
        scratch = [pltpu.VMEM((groups, 2, 2, quarter, step), jnp.float32)]
    else:
        out_shape, scratch = jax.ShapeDtypeStruct((rows, columns), jnp.float32), []
    count = len(pieces) + len(weights) + len(before)
    return pl.pallas_call(
        kernel,
        out_shape=out_shape,
        in_specs=[pl.BlockSpec(memory_space=pltpu.SMEM)]
        + [pl.BlockSpec(memory_space=pltpu.VMEM)] * count,
        scratch_shapes=scratch,
        compiler_params=pltpu.CompilerParams(vmem_limit_bytes=VMEM_LIMIT),
        cost_estimate=pl.CostEstimate(
            flops=2 * rows * depth * columns, bytes_accessed=2 * depth * columns, transcendentals=0
        ),
        name="expel",
    )(place, *pieces, *weights, *before)


def line_pieces(block, axis):
    far = swap(block, axis, 2)
    up = lax.ppermute(block, axis, [(i, i + 1) for i in range(3)])
    down = lax.ppermute(block, axis, [(i + 1, i) for i in range(3)])
    passed = lax.ppermute(far, axis, [(1, 0), (2, 3)])
    return block, up, down, passed, far


def ring_pieces(block, axis):
    before = lax.ppermute(block, axis, [(i, (i + 1) % 4) for i in range(4)])
    after = lax.ppermute(block, axis, [((i + 1) % 4, i) for i in range(4)])
    return block, before, after, swap(block, axis, 2)


def gather_line(block, axis, dim):
    count = lax.axis_size(axis)
    if count != 4:
        return lax.all_gather(block, axis, axis=dim, tiled=True)
    me = lax.axis_index(axis)
    block, before, after, far = ring_pieces(block, axis)
    size = block.shape[dim]
    shape = list(block.shape)
    shape[dim] = count * size
    out = jnp.zeros(shape, block.dtype)
    for piece, place in ((block, me), (before, (me + 3) % 4), (after, (me + 1) % 4), (far, me ^ 2)):
        out = lax.dynamic_update_slice_in_dim(out, piece, place * size, dim)
    return out


def gather_pair(block, axis):
    if lax.axis_size(axis) != 2:
        return lax.all_gather(block, axis, axis=0)
    other = swap(block, axis, 1)
    first = lax.axis_index(axis) == 0
    return jnp.stack([jnp.where(first, block, other), jnp.where(first, other, block)])


def shards(
    tokens, raw_keys, raw_values, query_weight, output_weight,
    key_expand, key_mix, key_reduce, value_expand, value_mix, value_reduce,
):
    outer, inner, heads_axis = (lax.axis_size(name) for name in ("outer", "inner", "head"))
    z, y, h = (lax.axis_index(name) for name in ("outer", "inner", "head"))
    key_width, value_width = key_expand.shape[0], value_expand.shape[0]
    row_count, model = tokens.shape
    devices = outer * inner * heads_axis
    blocks = raw_keys.shape[0] // STRIDE
    context = raw_keys.shape[0] * devices - row_count * outer * inner
    part = query_weight.shape[0]
    fast = inner == 2 and outer == 4 and heads_axis == 4

    if fast:
        turned = output_weight.T
        out_weights = [turned, swap(turned, "inner", 1)]
    else:
        out_weights = lax.all_gather(output_weight, "inner", axis=1, tiled=True)

    seq_axes = ("outer", "inner") if fast else "outer"
    shares = outer * inner if fast else outer
    share = query_weight.shape[1] // shares

    def exchange(block):
        return lax.all_to_all(block, seq_axes, split_axis=0, concat_axis=0, tiled=True)

    if fast:
        sent = cut(query_weight, shares, 2)
    else:
        weight = exchange(
            jnp.stack([query_weight[:, i * share : (i + 1) * share] for i in range(shares)])
        )
        weight = lax.all_gather(weight, "inner", axis=1).reshape(model, share)
    heads_here = share // key_width

    edge = jnp.concatenate([raw_keys[:STRIDE], raw_values[:STRIDE]], axis=1)
    edge = lax.ppermute(
        edge, ("outer", "inner", "head"), [(i + 1, i) for i in range(devices - 1)]
    )
    edge_keys, edge_values = edge[:, : raw_keys.shape[1]], edge[:, raw_keys.shape[1] :]

    if fast:
        quarter = row_count // heads_axis
        mine = lax.dynamic_slice_in_dim(tokens, h * quarter, quarter, 0)
        mine, before, after, far = ring_pieces(mine, "outer")
        begin, before, after, far, raw_keys, raw_values = lax.optimization_barrier(
            (sent[0], before, after, far, raw_keys, raw_values)
        )
        weight_first = exchange(begin)
        near = jnp.concatenate([mine, before, after, far], axis=0)
        beside = swap(near, "inner", 1)
        pieces = [near, beside, swap(near, "head", 2)]
        steps = [(line, side, turn) for turn in (0, 2) for side in (0, 1) for line in range(4)]
        steps = steps + [(a, b, k ^ 1) for a, b, k in steps]
        def of_block(block, z, h):
            line, side, turn = steps[block]
            there = (z, (z + 3) & 3, (z + 1) & 3, z ^ 2)[line]
            return side, ((h ^ turn) * outer + there) * quarter

        bases = []
        for block, (_, side, _) in enumerate(steps):
            where = of_block(block, z, h)[1] // quarter
            bases.append((where % outer * inner + (y ^ side)) * row_count + where // outer * quarter)
        bases = jnp.stack(bases)[:, None] + jnp.arange(quarter)[None, :]
        layout = (quarter, inner, of_block)
    else:
        every = gather_line(tokens, "outer", 0)
        queries = [jnp.dot(every, weight, preferred_element_type=jnp.float32).astype(jnp.bfloat16)]
        bases = (jnp.arange(outer) * inner + y)[:, None] * row_count + jnp.arange(row_count)[None, :]
        layout = (row_count, 1, lambda block, z, h: (0, block * row_count))
    places = (context + bases).astype(jnp.int32).reshape(-1, 1)
    here = jnp.stack([z, h, y]).astype(jnp.int32)

    packed = compress(
        raw_keys, raw_values, edge_keys, edge_values,
        key_expand, key_mix, key_reduce, value_expand, value_mix, value_reduce,
    )
    ids = np.arange(devices * blocks).reshape(outer, inner, heads_axis, blocks)
    if fast:
        stay = lax.dynamic_index_in_dim(packed, h, 0, False)
        away = [lax.dynamic_index_in_dim(packed, h ^ step, 0, False) for step in (1, 2, 3)]
        came = [swap(piece, "head", step) for step, piece in zip((1, 2, 3), away)]
        packed = jnp.concatenate([stay, *came], axis=0)
        bound = np.broadcast_to(ids.max(axis=(2, 3), keepdims=True), ids.shape)
    else:
        packed = jnp.broadcast_to(packed[:, None], (G, heads_axis // G, *packed.shape[1:]))
        packed = packed.reshape(heads_axis, blocks, -1)
        packed = lax.all_to_all(packed, "head", split_axis=0, concat_axis=0, tiled=True)
        packed = packed.reshape(heads_axis * blocks, -1)
        bound = ids
    if fast:
        packed, out_weights[1], pieces = lax.optimization_barrier((packed, out_weights[1], pieces))
        pieces.append(swap(pieces[1], "head", 2))
        partners = [swap(piece, "head", 1) for piece in pieces]
    packed = gather_line(packed, "outer", 0)
    if fast:
        begin, packed = lax.optimization_barrier((sent[1], packed))
        queries = [project([*pieces, *partners], [weight_first, exchange(begin)])]
    packed = gather_pair(packed, "inner").reshape(devices * blocks, -1)
    bound = (STRIDE * bound + BLK - 1).transpose(1, 0, 2, 3).reshape(-1)
    hidden = [bool((bound[i : i + LANES] > context).any()) for i in range(0, len(bound), LANES)]
    masked, start = [], 0
    for i in range(1, len(hidden) + 1):
        if i == len(hidden) or hidden[i] != hidden[start]:
            masked.append((start * LANES, min(i * LANES, len(bound)), hidden[start]))
            start = i
    if fast:
        column = np.arange(heads_axis)[None, None, :, None]
        ids = ids[:, :, :1] + (column ^ h) * blocks
        limits = (STRIDE * ids + BLK - 1).transpose(1, 0, 2, 3).reshape(1, -1).astype(jnp.int32)
    else:
        limits = (STRIDE * ids + BLK - 1).transpose(1, 0, 2, 3).reshape(1, -1)
        limits = jnp.asarray(limits, jnp.int32)

    total = None
    for head in range(heads_here):
        attended = attend(
            here, queries, head, packed, limits, places, key_width, masked, layout
        )
        if fast:
            last = head == heads_here - 1
            block = jnp.concatenate([attended[0], swap(attended[1], "inner", 1)], axis=1)
            total = expel(
                here, line_pieces(block, "outer"), out_weights, [] if total is None else [total],
                head, heads_here, (heads_axis, quarter) if last else None,
            )
        else:
            attended = gather_line(attended[0], "outer", 1)
            rows = out_weights.reshape(outer, heads_here, value_width, -1)[:, head]
            product = jnp.dot(
                attended, rows.reshape(outer * value_width, -1), preferred_element_type=jnp.float32
            )
            total = product if total is None else total + product

    if fast:
        keep, send = total
        columns = keep.shape[-1]
        total = keep + swap(send, "head", 1).astype(jnp.float32)
        x = h // 2
        keep = lax.dynamic_index_in_dim(total, x, 1, False)
        send = lax.dynamic_index_in_dim(total, 1 - x, 1, False).astype(jnp.bfloat16)
        total = keep + swap(send, "head", 2).astype(jnp.float32)
        result = total.astype(jnp.bfloat16).reshape(row_count, columns)
        first, second = result[:, : columns // 2], result[:, columns // 2 :]
        result = jnp.concatenate(
            [jnp.where(y == 0, first, second), jnp.where(y == 0, second, first)], axis=1
        )
        route = [
            ((a * inner + b) * heads_axis + k, (k * inner + b) * heads_axis + a)
            for a in range(outer) for b in range(inner) for k in range(heads_axis)
        ]
        return lax.ppermute(result, ("outer", "inner", "head"), route)
    columns = total.shape[1]
    total = lax.psum_scatter(total, "head", scatter_dimension=0, tiled=True).astype(jnp.bfloat16)
    total = lax.all_gather(total, "head", axis=0, tiled=True)
    total = lax.all_to_all(
        total.reshape(outer, row_count, columns), "outer", split_axis=0, concat_axis=0, tiled=True
    )
    total = total.transpose(1, 0, 2).reshape(row_count, model)
    return lax.dynamic_slice_in_dim(total, h * (model // heads_axis), model // heads_axis, 1)


def solution(mesh):
    seq_count, head_count = mesh.shape["seq"], mesh.shape["head"]
    inner = seq_count // OUTER
    finer = Mesh(
        mesh.devices.reshape(OUTER, inner, head_count), ("outer", "inner", "head")
    )
    seq = ("outer", "inner")
    in_specs = (
        P(seq, None),
        P((*seq, "head"), None),
        P((*seq, "head"), None),
        P(seq, "head"),
        P("head", seq),
        P(), P(), P(), P(), P(), P(),
    )
    return jax.shard_map(
        shards, mesh=finer, in_specs=in_specs, out_specs=P(seq, "head"), check_vma=False
    )
```

```python
import jax
import jax.numpy as jnp
import numpy as np
from jax import lax
from jax.experimental import pallas as pl
from jax.experimental.pallas import tpu as pltpu
from jax.sharding import Mesh
from jax.sharding import PartitionSpec as P

G = 4
BLK = 32
STRIDE = 16
LANES = 128
OUTER = 4
VMEM_LIMIT = 20 * 1024 * 1024


def round_up(value, unit):
    return -(-value // unit) * unit


def swap(block, axis, bit):
    return lax.ppermute(block, axis, [(i, i ^ bit) for i in range(lax.axis_size(axis))])


def window_of(group, width):
    low = group * width // LANES * LANES
    return low, round_up((group + 1) * width, LANES) - low, group * width - low


def compress_one(raw_ref, edge_ref, expand_ref, mix_ref, reduce_ref, sorted_ref, hidden_ref, groups):
    width, units = expand_ref.shape
    tokens = raw_ref.shape[0]
    rows = 8 * STRIDE
    chunks = tokens // rows
    blocks = tokens // STRIDE
    to = lax.broadcasted_iota(jnp.int32, (rows, rows), 0)
    come = lax.broadcasted_iota(jnp.int32, (rows, rows), 1)
    order = (come == (to % 8) * STRIDE + to // 8).astype(jnp.bfloat16)
    for chunk in range(chunks):
        piece = slice(chunk * rows, (chunk + 1) * rows)
        sorted_ref[piece, :] = jnp.dot(
            order, raw_ref[piece, :], preferred_element_type=jnp.float32
        ).astype(jnp.bfloat16)
    tile = 256 if units % 256 == 0 else units
    for group in range(groups):
        low, span, offset = window_of(group, width)
        parts = []
        if offset:
            parts.append(jnp.zeros((offset, units), jnp.bfloat16))
        parts.append(expand_ref[...])
        if span - offset - width:
            parts.append(jnp.zeros((span - offset - width, units), jnp.bfloat16))
        expand = jnp.concatenate(parts, axis=0) if len(parts) > 1 else parts[0]
        for start in range(0, units, tile):
            lanes = slice(start, start + tile)
            weight = expand[:, lanes]
            projected = jnp.dot(
                sorted_ref[:, low : low + span], weight, preferred_element_type=jnp.float32
            ).reshape(chunks, STRIDE, 8, tile)
            mix_low = mix_ref[:STRIDE, lanes][None, :, None, :]
            mix_high = mix_ref[STRIDE:, lanes]
            first = jnp.sum(projected * mix_low, axis=1).reshape(blocks, tile)
            second = jnp.sum(projected * mix_high[None, :, None, :], axis=1).reshape(blocks, tile)
            edge = jnp.dot(edge_ref[:, low : low + span], weight, preferred_element_type=jnp.float32)
            edge = jnp.sum(edge * mix_high, axis=0, keepdims=True)
            hidden = first + jnp.concatenate([second[1:], edge], axis=0)
            half = 0.5 * hidden
            activated = half + half * lax.erf(hidden * np.float32(2.0**-0.5))
            hidden_ref[group * blocks : (group + 1) * blocks, lanes] = activated.astype(jnp.bfloat16)
    return jnp.dot(hidden_ref[...], reduce_ref[...], preferred_element_type=jnp.float32).astype(
        jnp.bfloat16
    )


def compress_kernel(
    raw_keys, raw_values, edge_keys, edge_values, key_expand, key_mix, key_reduce,
    value_expand, value_mix, value_reduce, packed, sorted_keys, sorted_values, hidden,
):
    groups, blocks, _ = packed.shape
    key_width = key_expand.shape[0]
    value_start = round_up(key_width, LANES)
    keys = compress_one(
        raw_keys, edge_keys, key_expand, key_mix, key_reduce, sorted_keys, hidden, groups
    )
    values = compress_one(
        raw_values, edge_values, value_expand, value_mix, value_reduce, sorted_values, hidden, groups
    )
    for group in range(groups):
        rows = slice(group * blocks, (group + 1) * blocks)
        packed[group, :, :key_width] = keys[rows]
        packed[group, :, key_width:value_start] = jnp.zeros(
            (blocks, value_start - key_width), jnp.bfloat16
        )
        packed[group, :, value_start:] = values[rows]


def compress(raw_keys, raw_values, edge_keys, edge_values, *weights):
    key_expand, _, _, value_expand, _, _ = weights
    units = key_expand.shape[1]
    tokens = raw_keys.shape[0]
    blocks = tokens // STRIDE
    width = round_up(key_expand.shape[0], LANES) + value_expand.shape[0]
    flops = 2 * tokens * units * (raw_keys.shape[1] + raw_values.shape[1])
    return pl.pallas_call(
        compress_kernel,
        out_shape=jax.ShapeDtypeStruct((G, blocks, width), jnp.bfloat16),
        scratch_shapes=[
            pltpu.VMEM(raw_keys.shape, jnp.bfloat16),
            pltpu.VMEM(raw_values.shape, jnp.bfloat16),
            pltpu.VMEM((G * blocks, units), jnp.bfloat16),
        ],
        compiler_params=pltpu.CompilerParams(vmem_limit_bytes=VMEM_LIMIT),
        cost_estimate=pl.CostEstimate(
            flops=flops, bytes_accessed=2 * raw_keys.size, transcendentals=0
        ),
        name="compress",
    )(raw_keys, raw_values, edge_keys, edge_values, *weights)


def cut(weight, shares, parts):
    rows, columns = weight.shape
    share, part = columns // shares, rows // parts

    def kernel(in_ref, *refs):
        out_refs, sems = refs[:-1], refs[-1]
        copies = [
            pltpu.make_async_copy(
                in_ref.at[index * part : (index + 1) * part, owner * share : (owner + 1) * share],
                out_ref.at[owner],
                sems.at[index * shares + owner],
            )
            for index, out_ref in enumerate(out_refs)
            for owner in range(shares)
        ]
        for copy in copies:
            copy.start()
        for copy in copies:
            copy.wait()

    return pl.pallas_call(
        kernel,
        out_shape=(jax.ShapeDtypeStruct((shares, part, share), weight.dtype),) * parts,
        in_specs=[pl.BlockSpec(memory_space=pl.ANY)],
        out_specs=(pl.BlockSpec(memory_space=pl.ANY),) * parts,
        scratch_shapes=[pltpu.SemaphoreType.DMA((parts * shares,))],
        cost_estimate=pl.CostEstimate(flops=0, bytes_accessed=0, transcendentals=0),
        name="cut",
    )(weight)


def project(pieces, weights):
    part, depth = pieces[0].shape
    rows = part * len(pieces)
    shares, share, columns = weights[0].shape
    group = len(pieces) // 2
    count = len(pieces)

    def kernel(*refs):
        piece_refs, weight_refs = refs[:count], refs[count : count + len(weights)]
        out_ref, rows_ref, weight_ref, sems = refs[count + len(weights) :]
        copies = [
            pltpu.make_async_copy(
                piece, rows_ref.at[index * part : (index + 1) * part], sems.at[index]
            )
            for index, piece in enumerate(piece_refs)
        ]
        bring = []
        for index, weight in enumerate(weight_refs):
            for owner in range(shares):
                start = (owner * len(weights) + index) * share
                bring.append(
                    pltpu.make_async_copy(
                        weight.at[owner], weight_ref.at[start : start + share],
                        sems.at[count + len(bring)],
                    )
                )
        for copy in bring + copies:
            copy.start()
        for copy in bring:
            copy.wait()
        for start in range(0, count, group):
            for copy in copies[start : start + group]:
                copy.wait()
            place = slice(start * part, (start + group) * part)
            out_ref[place, :] = jnp.dot(
                rows_ref[place, :], weight_ref[...], preferred_element_type=jnp.float32
            ).astype(jnp.bfloat16)

    return pl.pallas_call(
        kernel,
        out_shape=jax.ShapeDtypeStruct((rows, columns), jnp.bfloat16),
        in_specs=[pl.BlockSpec(memory_space=pl.ANY)] * (count + len(weights)),
        scratch_shapes=[
            pltpu.VMEM((rows, depth), jnp.bfloat16),
            pltpu.VMEM((depth, columns), jnp.bfloat16),
            pltpu.SemaphoreType.DMA((count + len(weights) * shares,)),
        ],
        compiler_params=pltpu.CompilerParams(vmem_limit_bytes=VMEM_LIMIT),
        cost_estimate=pl.CostEstimate(
            flops=2 * rows * depth * columns, bytes_accessed=2 * rows * depth, transcendentals=0
        ),
        name="project",
    )(*pieces, *weights)


def attend(here, queries, head, packed, limits, places, key_width, masked, layout):
    rows_each = queries[0].shape[0]
    rows = rows_each * len(queries)
    value_start = round_up(key_width, LANES)
    value_width = packed.shape[1] - value_start
    columns = packed.shape[0]
    factor = np.float32(key_width**-0.5 * np.log2(np.e))
    tile = min(256, rows_each)
    unit, outputs, sends = layout

    def kernel(here_ref, *refs):
        query_refs = refs[: len(queries)]
        kv_ref, limit_ref, place_ref = refs[len(queries) : len(queries) + 3]
        out_refs = refs[len(queries) + 3 :]
        keys = kv_ref[:, :key_width]
        values = kv_ref[:, value_start:]
        for start in range(0, rows, tile):
            from_ref, at = query_refs[start // rows_each], start % rows_each
            query = from_ref[at : at + tile, head * key_width : (head + 1) * key_width]
            scores = lax.dot_general(
                query, keys, (((1,), (1,)), ((), ())), preferred_element_type=jnp.float32
            )
            pieces = []
            for low, high, hide in masked:
                piece = scores[:, low:high]
                if hide:
                    visible = limit_ref[:, low:high] <= place_ref[start : start + tile, :]
                    piece = jnp.where(visible, piece, -jnp.inf)
                pieces.append(piece)
            scores = jnp.concatenate(pieces, axis=1) if len(pieces) > 1 else pieces[0]
            top = jnp.max(scores, axis=1, keepdims=True)
            exponent = jnp.exp2((scores - top) * factor)
            total = jnp.sum(exponent, axis=1, keepdims=True)
            numerator = jnp.dot(
                exponent.astype(jnp.bfloat16), values, preferred_element_type=jnp.float32
            )
            done = (numerator / total).astype(jnp.bfloat16)
            for low in range(0, tile, unit):
                which, where = sends((start + low) // unit, here_ref[0], here_ref[1])
                if not isinstance(where, int):
                    where = pl.multiple_of(where, unit)
                out_refs[which][pl.ds(where, unit), :] = done[low : low + unit]

    shape = jax.ShapeDtypeStruct((rows // outputs, value_width), jnp.bfloat16)
    return pl.pallas_call(
        kernel,
        out_shape=(shape,) * outputs,
        in_specs=[pl.BlockSpec(memory_space=pltpu.SMEM)]
        + [pl.BlockSpec(memory_space=pltpu.VMEM)] * (len(queries) + 3),
        compiler_params=pltpu.CompilerParams(vmem_limit_bytes=VMEM_LIMIT),
        cost_estimate=pl.CostEstimate(
            flops=2 * rows * columns * (key_width + value_width),
            bytes_accessed=2 * packed.size,
            transcendentals=0,
        ),
        name="attend",
    )(here, *queries, packed, limits, places)


def expel(place, pieces, weights, before, chunk, chunks, shape):
    rows, width = pieces[0].shape
    depth, step, single = 4 * width, weights[0].shape[0], width // 2
    last = shape is not None

    def kernel(place_ref, *refs):
        own, up, down, passed, far = refs[:5]
        weight_refs = refs[5 : 5 + len(weights)]
        rest = refs[5 + len(weights) :]
        before_refs, outs = rest[: len(before)], rest[len(before) :]
        z, core, y = place_ref[0], place_ref[1] & 1, place_ref[2]
        lower = jnp.where(z == 0, passed[...], up[...])
        upper = jnp.where(z == 3, passed[...], down[...])
        for side, weight in enumerate(weight_refs):
            lanes = slice(side * step, (side + 1) * step)
            total = before_refs[0][:, lanes] if before else None
            for block, at in (
                (own[...], z), (lower, (z + 3) & 3), (upper, (z + 1) & 3), (far[...], z ^ 2)
            ):
                starts = [((at * 2 + inner) * chunks + chunk) * single for inner in (y, 1 - y)]
                both = [weight[:, pl.ds(pl.multiple_of(start, single), single)] for start in starts]
                product = lax.dot_general(
                    block, jnp.concatenate(both, axis=1), (((1,), (1,)), ((), ())),
                    preferred_element_type=jnp.float32,
                )
                total = product if total is None else total + product
            if not last:
                outs[0][:, lanes] = total
                continue
            keep_ref, send_ref, hold_ref = outs
            hold_ref[...] = total.reshape(hold_ref.shape)
            keep_ref[:, :, :, lanes] = hold_ref[:, :, pl.ds(core, 1)][:, :, 0]
            send_ref[:, :, :, lanes] = hold_ref[:, :, pl.ds(1 - core, 1)][:, :, 0].astype(jnp.bfloat16)

    columns = step * len(weights)
    if last:
        groups, quarter = shape
        out_shape = (
            jax.ShapeDtypeStruct((groups, 2, quarter, columns), jnp.float32),
            jax.ShapeDtypeStruct((groups, 2, quarter, columns), jnp.bfloat16),
        )
        scratch = [pltpu.VMEM((groups, 2, 2, quarter, step), jnp.float32)]
    else:
        out_shape, scratch = jax.ShapeDtypeStruct((rows, columns), jnp.float32), []
    count = len(pieces) + len(weights) + len(before)
    return pl.pallas_call(
        kernel,
        out_shape=out_shape,
        in_specs=[pl.BlockSpec(memory_space=pltpu.SMEM)]
        + [pl.BlockSpec(memory_space=pltpu.VMEM)] * count,
        scratch_shapes=scratch,
        compiler_params=pltpu.CompilerParams(vmem_limit_bytes=VMEM_LIMIT),
        cost_estimate=pl.CostEstimate(
            flops=2 * rows * depth * columns, bytes_accessed=2 * depth * columns, transcendentals=0
        ),
        name="expel",
    )(place, *pieces, *weights, *before)


def line_pieces(block, axis):
    far = swap(block, axis, 2)
    up = lax.ppermute(block, axis, [(i, i + 1) for i in range(3)])
    down = lax.ppermute(block, axis, [(i + 1, i) for i in range(3)])
    passed = lax.ppermute(far, axis, [(1, 0), (2, 3)])
    return block, up, down, passed, far


def ring_pieces(block, axis):
    before = lax.ppermute(block, axis, [(i, (i + 1) % 4) for i in range(4)])
    after = lax.ppermute(block, axis, [((i + 1) % 4, i) for i in range(4)])
    return block, before, after, swap(block, axis, 2)


def gather_line(block, axis, dim):
    count = lax.axis_size(axis)
    if count != 4:
        return lax.all_gather(block, axis, axis=dim, tiled=True)
    me = lax.axis_index(axis)
    block, before, after, far = ring_pieces(block, axis)
    size = block.shape[dim]
    shape = list(block.shape)
    shape[dim] = count * size
    out = jnp.zeros(shape, block.dtype)
    for piece, place in ((block, me), (before, (me + 3) % 4), (after, (me + 1) % 4), (far, me ^ 2)):
        out = lax.dynamic_update_slice_in_dim(out, piece, place * size, dim)
    return out


def gather_pair(block, axis):
    if lax.axis_size(axis) != 2:
        return lax.all_gather(block, axis, axis=0)
    other = swap(block, axis, 1)
    first = lax.axis_index(axis) == 0
    return jnp.stack([jnp.where(first, block, other), jnp.where(first, other, block)])


def shards(
    tokens, raw_keys, raw_values, query_weight, output_weight,
    key_expand, key_mix, key_reduce, value_expand, value_mix, value_reduce,
):
    outer, inner, heads_axis = (lax.axis_size(name) for name in ("outer", "inner", "head"))
    z, y, h = (lax.axis_index(name) for name in ("outer", "inner", "head"))
    key_width, value_width = key_expand.shape[0], value_expand.shape[0]
    row_count, model = tokens.shape
    devices = outer * inner * heads_axis
    blocks = raw_keys.shape[0] // STRIDE
    context = raw_keys.shape[0] * devices - row_count * outer * inner
    part = query_weight.shape[0]
    fast = inner == 2 and outer == 4 and heads_axis == 4

    edge = jnp.concatenate([raw_keys[:STRIDE], raw_values[:STRIDE]], axis=1)
    edge = lax.ppermute(
        edge, ("outer", "inner", "head"), [(i + 1, i) for i in range(devices - 1)]
    )

    if fast:
        turned, edge = lax.optimization_barrier((output_weight.T, edge))
        out_weights = [turned, swap(turned, "inner", 1)]
    else:
        out_weights = lax.all_gather(output_weight, "inner", axis=1, tiled=True)

    seq_axes = ("outer", "inner") if fast else "outer"
    shares = outer * inner if fast else outer
    share = query_weight.shape[1] // shares

    def exchange(block):
        return lax.all_to_all(block, seq_axes, split_axis=0, concat_axis=0, tiled=True)

    if fast:
        sent = cut(query_weight, shares, 2)
    else:
        weight = exchange(
            jnp.stack([query_weight[:, i * share : (i + 1) * share] for i in range(shares)])
        )
        weight = lax.all_gather(weight, "inner", axis=1).reshape(model, share)
    heads_here = share // key_width

    edge_keys, edge_values = edge[:, : raw_keys.shape[1]], edge[:, raw_keys.shape[1] :]
    packed = compress(
        raw_keys, raw_values, edge_keys, edge_values,
        key_expand, key_mix, key_reduce, value_expand, value_mix, value_reduce,
    )

    if fast:
        quarter = row_count // heads_axis
        mine = lax.dynamic_slice_in_dim(tokens, h * quarter, quarter, 0)
        mine, before, after, far = ring_pieces(mine, "outer")
        begin, before, after, far, packed = lax.optimization_barrier(
            (sent[0], before, after, far, packed)
        )
        weight_first = exchange(begin)
        near = jnp.concatenate([mine, before, after, far], axis=0)
        beside = swap(near, "inner", 1)
        pieces = [near, beside, swap(near, "head", 2)]
        steps = [(line, side, turn) for turn in (0, 2) for side in (0, 1) for line in range(4)]
        steps = steps + [(a, b, k ^ 1) for a, b, k in steps]
        def of_block(block, z, h):
            line, side, turn = steps[block]
            there = (z, (z + 3) & 3, (z + 1) & 3, z ^ 2)[line]
            return side, ((h ^ turn) * outer + there) * quarter

        bases = []
        for block, (_, side, _) in enumerate(steps):
            where = of_block(block, z, h)[1] // quarter
            bases.append((where % outer * inner + (y ^ side)) * row_count + where // outer * quarter)
        bases = jnp.stack(bases)[:, None] + jnp.arange(quarter)[None, :]
        layout = (quarter, inner, of_block)
    else:
        every = gather_line(tokens, "outer", 0)
        queries = [jnp.dot(every, weight, preferred_element_type=jnp.float32).astype(jnp.bfloat16)]
        bases = (jnp.arange(outer) * inner + y)[:, None] * row_count + jnp.arange(row_count)[None, :]
        layout = (row_count, 1, lambda block, z, h: (0, block * row_count))
    places = (context + bases).astype(jnp.int32).reshape(-1, 1)
    here = jnp.stack([z, h, y]).astype(jnp.int32)

    ids = np.arange(devices * blocks).reshape(outer, inner, heads_axis, blocks)
    if fast:
        stay = lax.dynamic_index_in_dim(packed, h, 0, False)
        away = [lax.dynamic_index_in_dim(packed, h ^ step, 0, False) for step in (1, 2, 3)]
        came = [swap(piece, "head", step) for step, piece in zip((1, 2, 3), away)]
        packed = jnp.concatenate([stay, *came], axis=0)
        bound = np.broadcast_to(ids.max(axis=(2, 3), keepdims=True), ids.shape)
    else:
        packed = jnp.broadcast_to(packed[:, None], (G, heads_axis // G, *packed.shape[1:]))
        packed = packed.reshape(heads_axis, blocks, -1)
        packed = lax.all_to_all(packed, "head", split_axis=0, concat_axis=0, tiled=True)
        packed = packed.reshape(heads_axis * blocks, -1)
        bound = ids
    if fast:
        packed, out_weights[1], pieces = lax.optimization_barrier((packed, out_weights[1], pieces))
        pieces.append(swap(pieces[1], "head", 2))
        partners = [swap(piece, "head", 1) for piece in pieces]
    packed = gather_line(packed, "outer", 0)
    if fast:
        begin, packed = lax.optimization_barrier((sent[1], packed))
        queries = [project([*pieces, *partners], [weight_first, exchange(begin)])]
    packed = gather_pair(packed, "inner").reshape(devices * blocks, -1)
    bound = (STRIDE * bound + BLK - 1).transpose(1, 0, 2, 3).reshape(-1)
    hidden = [bool((bound[i : i + LANES] > context).any()) for i in range(0, len(bound), LANES)]
    masked, start = [], 0
    for i in range(1, len(hidden) + 1):
        if i == len(hidden) or hidden[i] != hidden[start]:
            masked.append((start * LANES, min(i * LANES, len(bound)), hidden[start]))
            start = i
    if fast:
        column = np.arange(heads_axis)[None, None, :, None]
        ids = ids[:, :, :1] + (column ^ h) * blocks
        limits = (STRIDE * ids + BLK - 1).transpose(1, 0, 2, 3).reshape(1, -1).astype(jnp.int32)
    else:
        limits = (STRIDE * ids + BLK - 1).transpose(1, 0, 2, 3).reshape(1, -1)
        limits = jnp.asarray(limits, jnp.int32)

    total = None
    for head in range(heads_here):
        attended = attend(
            here, queries, head, packed, limits, places, key_width, masked, layout
        )
        if fast:
            last = head == heads_here - 1
            block = jnp.concatenate([attended[0], swap(attended[1], "inner", 1)], axis=1)
            total = expel(
                here, line_pieces(block, "outer"), out_weights, [] if total is None else [total],
                head, heads_here, (heads_axis, quarter) if last else None,
            )
        else:
            attended = gather_line(attended[0], "outer", 1)
            rows = out_weights.reshape(outer, heads_here, value_width, -1)[:, head]
            product = jnp.dot(
                attended, rows.reshape(outer * value_width, -1), preferred_element_type=jnp.float32
            )
            total = product if total is None else total + product

    if fast:
        keep, send = total
        columns = keep.shape[-1]
        total = keep + swap(send, "head", 1).astype(jnp.float32)
        x = h // 2
        keep = lax.dynamic_index_in_dim(total, x, 1, False)
        send = lax.dynamic_index_in_dim(total, 1 - x, 1, False).astype(jnp.bfloat16)
        total = keep + swap(send, "head", 2).astype(jnp.float32)
        result = total.astype(jnp.bfloat16).reshape(row_count, columns)
        first, second = result[:, : columns // 2], result[:, columns // 2 :]
        result = jnp.concatenate(
            [jnp.where(y == 0, first, second), jnp.where(y == 0, second, first)], axis=1
        )
        route = [
            ((a * inner + b) * heads_axis + k, (k * inner + b) * heads_axis + a)
            for a in range(outer) for b in range(inner) for k in range(heads_axis)
        ]
        return lax.ppermute(result, ("outer", "inner", "head"), route)
    columns = total.shape[1]
    total = lax.psum_scatter(total, "head", scatter_dimension=0, tiled=True).astype(jnp.bfloat16)
    total = lax.all_gather(total, "head", axis=0, tiled=True)
    total = lax.all_to_all(
        total.reshape(outer, row_count, columns), "outer", split_axis=0, concat_axis=0, tiled=True
    )
    total = total.transpose(1, 0, 2).reshape(row_count, model)
    return lax.dynamic_slice_in_dim(total, h * (model // heads_axis), model // heads_axis, 1)


def solution(mesh):
    seq_count, head_count = mesh.shape["seq"], mesh.shape["head"]
    inner = seq_count // OUTER
    finer = Mesh(
        mesh.devices.reshape(OUTER, inner, head_count), ("outer", "inner", "head")
    )
    seq = ("outer", "inner")
    in_specs = (
        P(seq, None),
        P((*seq, "head"), None),
        P((*seq, "head"), None),
        P(seq, "head"),
        P("head", seq),
        P(), P(), P(), P(), P(), P(),
    )
    return jax.shard_map(
        shards, mesh=finer, in_specs=in_specs, out_specs=P(seq, "head"), check_vma=False
    )
```

```python
import jax
import jax.numpy as jnp
import numpy as np
from jax import lax
from jax.experimental import pallas as pl
from jax.experimental.pallas import tpu as pltpu
from jax.sharding import Mesh
from jax.sharding import PartitionSpec as P

G = 4
BLK = 32
STRIDE = 16
LANES = 128
OUTER = 4
VMEM_LIMIT = 20 * 1024 * 1024


def round_up(value, unit):
    return -(-value // unit) * unit


def swap(block, axis, bit):
    return lax.ppermute(block, axis, [(i, i ^ bit) for i in range(lax.axis_size(axis))])


def window_of(group, width):
    low = group * width // LANES * LANES
    return low, round_up((group + 1) * width, LANES) - low, group * width - low


def compress_one(raw_ref, edge_ref, expand_ref, mix_ref, reduce_ref, sorted_ref, hidden_ref, groups):
    width, units = expand_ref.shape
    tokens = raw_ref.shape[0]
    rows = 8 * STRIDE
    chunks = tokens // rows
    blocks = tokens // STRIDE
    to = lax.broadcasted_iota(jnp.int32, (rows, rows), 0)
    come = lax.broadcasted_iota(jnp.int32, (rows, rows), 1)
    order = (come == (to % 8) * STRIDE + to // 8).astype(jnp.bfloat16)
    for chunk in range(chunks):
        piece = slice(chunk * rows, (chunk + 1) * rows)
        sorted_ref[piece, :] = jnp.dot(
            order, raw_ref[piece, :], preferred_element_type=jnp.float32
        ).astype(jnp.bfloat16)
    tile = 256 if units % 256 == 0 else units
    for group in range(groups):
        low, span, offset = window_of(group, width)
        parts = []
        if offset:
            parts.append(jnp.zeros((offset, units), jnp.bfloat16))
        parts.append(expand_ref[...])
        if span - offset - width:
            parts.append(jnp.zeros((span - offset - width, units), jnp.bfloat16))
        expand = jnp.concatenate(parts, axis=0) if len(parts) > 1 else parts[0]
        for start in range(0, units, tile):
            lanes = slice(start, start + tile)
            weight = expand[:, lanes]
            projected = jnp.dot(
                sorted_ref[:, low : low + span], weight, preferred_element_type=jnp.float32
            ).reshape(chunks, STRIDE, 8, tile)
            mix_low = mix_ref[:STRIDE, lanes][None, :, None, :]
            mix_high = mix_ref[STRIDE:, lanes]
            first = jnp.sum(projected * mix_low, axis=1).reshape(blocks, tile)
            second = jnp.sum(projected * mix_high[None, :, None, :], axis=1).reshape(blocks, tile)
            edge = jnp.dot(edge_ref[:, low : low + span], weight, preferred_element_type=jnp.float32)
            edge = jnp.sum(edge * mix_high, axis=0, keepdims=True)
            hidden = first + jnp.concatenate([second[1:], edge], axis=0)
            half = 0.5 * hidden
            activated = half + half * lax.erf(hidden * np.float32(2.0**-0.5))
            hidden_ref[group * blocks : (group + 1) * blocks, lanes] = activated.astype(jnp.bfloat16)
    return jnp.dot(hidden_ref[...], reduce_ref[...], preferred_element_type=jnp.float32).astype(
        jnp.bfloat16
    )


def compress_kernel(
    raw_keys, raw_values, edge_keys, edge_values, key_expand, key_mix, key_reduce,
    value_expand, value_mix, value_reduce, packed, sorted_keys, sorted_values, hidden,
):
    groups, blocks, _ = packed.shape
    key_width = key_expand.shape[0]
    value_start = round_up(key_width, LANES)
    keys = compress_one(
        raw_keys, edge_keys, key_expand, key_mix, key_reduce, sorted_keys, hidden, groups
    )
    values = compress_one(
        raw_values, edge_values, value_expand, value_mix, value_reduce, sorted_values, hidden, groups
    )
    for group in range(groups):
        rows = slice(group * blocks, (group + 1) * blocks)
        packed[group, :, :key_width] = keys[rows]
        packed[group, :, key_width:value_start] = jnp.zeros(
            (blocks, value_start - key_width), jnp.bfloat16
        )
        packed[group, :, value_start:] = values[rows]


def compress(raw_keys, raw_values, edge_keys, edge_values, *weights):
    key_expand, _, _, value_expand, _, _ = weights
    units = key_expand.shape[1]
    tokens = raw_keys.shape[0]
    blocks = tokens // STRIDE
    width = round_up(key_expand.shape[0], LANES) + value_expand.shape[0]
    flops = 2 * tokens * units * (raw_keys.shape[1] + raw_values.shape[1])
    return pl.pallas_call(
        compress_kernel,
        out_shape=jax.ShapeDtypeStruct((G, blocks, width), jnp.bfloat16),
        scratch_shapes=[
            pltpu.VMEM(raw_keys.shape, jnp.bfloat16),
            pltpu.VMEM(raw_values.shape, jnp.bfloat16),
            pltpu.VMEM((G * blocks, units), jnp.bfloat16),
        ],
        compiler_params=pltpu.CompilerParams(vmem_limit_bytes=56 * 1024 * 1024),
        cost_estimate=pl.CostEstimate(
            flops=flops, bytes_accessed=2 * raw_keys.size, transcendentals=0
        ),
        name="compress",
    )(raw_keys, raw_values, edge_keys, edge_values, *weights)


def cut(weight, shares, parts):
    rows, columns = weight.shape
    share, part = columns // shares, rows // parts

    def kernel(in_ref, *out_refs):
        for index, out_ref in enumerate(out_refs):
            out_ref[0] = in_ref[index * part : (index + 1) * part, :]

    return pl.pallas_call(
        kernel,
        out_shape=(jax.ShapeDtypeStruct((shares, part, share), weight.dtype),) * parts,
        grid=(shares,),
        in_specs=[pl.BlockSpec((rows, share), lambda i: (0, i))],
        out_specs=(pl.BlockSpec((1, part, share), lambda i: (i, 0, 0)),) * parts,
        cost_estimate=pl.CostEstimate(flops=0, bytes_accessed=0, transcendentals=0),
        name="cut",
    )(weight)


def project(pieces, weights):
    part, depth = pieces[0].shape
    rows = part * len(pieces)
    shares, share, columns = weights[0].shape
    group = len(pieces) // 2
    count = len(pieces)

    def kernel(*refs):
        piece_refs, weight_refs = refs[:count], refs[count : count + len(weights)]
        out_ref, rows_ref, weight_ref, sems = refs[count + len(weights) :]
        copies = [
            pltpu.make_async_copy(
                piece, rows_ref.at[index * part : (index + 1) * part], sems.at[index]
            )
            for index, piece in enumerate(piece_refs)
        ]
        bring = []
        for index, weight in enumerate(weight_refs):
            for owner in range(shares):
                start = (owner * len(weights) + index) * share
                bring.append(
                    pltpu.make_async_copy(
                        weight.at[owner], weight_ref.at[start : start + share],
                        sems.at[count + len(bring)],
                    )
                )
        for copy in bring + copies:
            copy.start()
        for copy in bring:
            copy.wait()
        for start in range(0, count, group):
            for copy in copies[start : start + group]:
                copy.wait()
            place = slice(start * part, (start + group) * part)
            out_ref[place, :] = jnp.dot(
                rows_ref[place, :], weight_ref[...], preferred_element_type=jnp.float32
            ).astype(jnp.bfloat16)

    return pl.pallas_call(
        kernel,
        out_shape=jax.ShapeDtypeStruct((rows, columns), jnp.bfloat16),
        in_specs=[pl.BlockSpec(memory_space=pl.ANY)] * (count + len(weights)),
        scratch_shapes=[
            pltpu.VMEM((rows, depth), jnp.bfloat16),
            pltpu.VMEM((depth, columns), jnp.bfloat16),
            pltpu.SemaphoreType.DMA((count + len(weights) * shares,)),
        ],
        compiler_params=pltpu.CompilerParams(vmem_limit_bytes=VMEM_LIMIT),
        cost_estimate=pl.CostEstimate(
            flops=2 * rows * depth * columns, bytes_accessed=2 * rows * depth, transcendentals=0
        ),
        name="project",
    )(*pieces, *weights)


def attend(here, queries, head, packed, limits, places, key_width, masked, layout):
    rows_each = queries[0].shape[0]
    rows = rows_each * len(queries)
    value_start = round_up(key_width, LANES)
    value_width = packed.shape[1] - value_start
    columns = packed.shape[0]
    factor = np.float32(key_width**-0.5 * np.log2(np.e))
    tile = min(256, rows_each)
    unit, outputs, sends = layout

    def kernel(here_ref, *refs):
        query_refs = refs[: len(queries)]
        kv_ref, limit_ref, place_ref = refs[len(queries) : len(queries) + 3]
        out_refs = refs[len(queries) + 3 :]
        keys = kv_ref[:, :key_width]
        values = kv_ref[:, value_start:]
        for start in range(0, rows, tile):
            from_ref, at = query_refs[start // rows_each], start % rows_each
            query = from_ref[at : at + tile, head * key_width : (head + 1) * key_width]
            scores = lax.dot_general(
                query, keys, (((1,), (1,)), ((), ())), preferred_element_type=jnp.float32
            )
            pieces = []
            for low, high, hide in masked:
                piece = scores[:, low:high]
                if hide:
                    visible = limit_ref[:, low:high] <= place_ref[start : start + tile, :]
                    piece = jnp.where(visible, piece, -jnp.inf)
                pieces.append(piece)
            scores = jnp.concatenate(pieces, axis=1) if len(pieces) > 1 else pieces[0]
            top = jnp.max(scores, axis=1, keepdims=True)
            exponent = jnp.exp2((scores - top) * factor)
            total = jnp.sum(exponent, axis=1, keepdims=True)
            numerator = jnp.dot(
                exponent.astype(jnp.bfloat16), values, preferred_element_type=jnp.float32
            )
            done = (numerator / total).astype(jnp.bfloat16)
            for low in range(0, tile, unit):
                which, where = sends((start + low) // unit, here_ref[0], here_ref[1])
                if not isinstance(where, int):
                    where = pl.multiple_of(where, unit)
                out_refs[which][pl.ds(where, unit), :] = done[low : low + unit]

    shape = jax.ShapeDtypeStruct((rows // outputs, value_width), jnp.bfloat16)
    return pl.pallas_call(
        kernel,
        out_shape=(shape,) * outputs,
        in_specs=[pl.BlockSpec(memory_space=pltpu.SMEM)]
        + [pl.BlockSpec(memory_space=pltpu.VMEM)] * (len(queries) + 3),
        compiler_params=pltpu.CompilerParams(vmem_limit_bytes=VMEM_LIMIT),
        cost_estimate=pl.CostEstimate(
            flops=2 * rows * columns * (key_width + value_width),
            bytes_accessed=2 * packed.size,
            transcendentals=0,
        ),
        name="attend",
    )(here, *queries, packed, limits, places)


def expel(place, pieces, weights, before, chunk, chunks, shape):
    rows, width = pieces[0].shape
    depth, step, single = 4 * width, weights[0].shape[0], width // 2
    last = shape is not None

    def kernel(place_ref, *refs):
        own, up, down, passed, far = refs[:5]
        weight_refs = refs[5 : 5 + len(weights)]
        rest = refs[5 + len(weights) :]
        before_refs, outs = rest[: len(before)], rest[len(before) :]
        z, core, y = place_ref[0], place_ref[1] & 1, place_ref[2]
        lower = jnp.where(z == 0, passed[...], up[...])
        upper = jnp.where(z == 3, passed[...], down[...])
        for side, weight in enumerate(weight_refs):
            lanes = slice(side * step, (side + 1) * step)
            total = before_refs[0][:, lanes] if before else None
            for block, at in (
                (own[...], z), (lower, (z + 3) & 3), (upper, (z + 1) & 3), (far[...], z ^ 2)
            ):
                starts = [((at * 2 + inner) * chunks + chunk) * single for inner in (y, 1 - y)]
                both = [weight[:, pl.ds(pl.multiple_of(start, single), single)] for start in starts]
                product = lax.dot_general(
                    block, jnp.concatenate(both, axis=1), (((1,), (1,)), ((), ())),
                    preferred_element_type=jnp.float32,
                )
                total = product if total is None else total + product
            if not last:
                outs[0][:, lanes] = total
                continue
            keep_ref, send_ref, hold_ref = outs
            hold_ref[...] = total.reshape(hold_ref.shape)
            keep_ref[:, :, :, lanes] = hold_ref[:, :, pl.ds(core, 1)][:, :, 0]
            send_ref[:, :, :, lanes] = hold_ref[:, :, pl.ds(1 - core, 1)][:, :, 0].astype(jnp.bfloat16)

    columns = step * len(weights)
    if last:
        groups, quarter = shape
        out_shape = (
            jax.ShapeDtypeStruct((groups, 2, quarter, columns), jnp.float32),
            jax.ShapeDtypeStruct((groups, 2, quarter, columns), jnp.bfloat16),
        )
        scratch = [pltpu.VMEM((groups, 2, 2, quarter, step), jnp.float32)]
    else:
        out_shape, scratch = jax.ShapeDtypeStruct((rows, columns), jnp.float32), []
    count = len(pieces) + len(weights) + len(before)
    return pl.pallas_call(
        kernel,
        out_shape=out_shape,
        in_specs=[pl.BlockSpec(memory_space=pltpu.SMEM)]
        + [pl.BlockSpec(memory_space=pltpu.VMEM)] * count,
        scratch_shapes=scratch,
        compiler_params=pltpu.CompilerParams(vmem_limit_bytes=VMEM_LIMIT),
        cost_estimate=pl.CostEstimate(
            flops=2 * rows * depth * columns, bytes_accessed=2 * depth * columns, transcendentals=0
        ),
        name="expel",
    )(place, *pieces, *weights, *before)


def line_pieces(block, axis):
    far = swap(block, axis, 2)
    up = lax.ppermute(block, axis, [(i, i + 1) for i in range(3)])
    down = lax.ppermute(block, axis, [(i + 1, i) for i in range(3)])
    passed = lax.ppermute(far, axis, [(1, 0), (2, 3)])
    return block, up, down, passed, far


def ring_pieces(block, axis):
    before = lax.ppermute(block, axis, [(i, (i + 1) % 4) for i in range(4)])
    after = lax.ppermute(block, axis, [((i + 1) % 4, i) for i in range(4)])
    return block, before, after, swap(block, axis, 2)


def gather_line(block, axis, dim):
    count = lax.axis_size(axis)
    if count != 4:
        return lax.all_gather(block, axis, axis=dim, tiled=True)
    me = lax.axis_index(axis)
    block, before, after, far = ring_pieces(block, axis)
    size = block.shape[dim]
    shape = list(block.shape)
    shape[dim] = count * size
    out = jnp.zeros(shape, block.dtype)
    for piece, place in ((block, me), (before, (me + 3) % 4), (after, (me + 1) % 4), (far, me ^ 2)):
        out = lax.dynamic_update_slice_in_dim(out, piece, place * size, dim)
    return out


def gather_pair(block, axis):
    if lax.axis_size(axis) != 2:
        return lax.all_gather(block, axis, axis=0)
    other = swap(block, axis, 1)
    first = lax.axis_index(axis) == 0
    return jnp.stack([jnp.where(first, block, other), jnp.where(first, other, block)])


def shards(
    tokens, raw_keys, raw_values, query_weight, output_weight,
    key_expand, key_mix, key_reduce, value_expand, value_mix, value_reduce,
):
    outer, inner, heads_axis = (lax.axis_size(name) for name in ("outer", "inner", "head"))
    z, y, h = (lax.axis_index(name) for name in ("outer", "inner", "head"))
    key_width, value_width = key_expand.shape[0], value_expand.shape[0]
    row_count, model = tokens.shape
    devices = outer * inner * heads_axis
    blocks = raw_keys.shape[0] // STRIDE
    context = raw_keys.shape[0] * devices - row_count * outer * inner
    part = query_weight.shape[0]
    fast = inner == 2 and outer == 4 and heads_axis == 4

    edge = jnp.concatenate([raw_keys[:STRIDE], raw_values[:STRIDE]], axis=1)
    edge = lax.ppermute(
        edge, ("outer", "inner", "head"), [(i + 1, i) for i in range(devices - 1)]
    )

    if fast:
        out_weights = [output_weight.T]
    else:
        out_weights = lax.all_gather(output_weight, "inner", axis=1, tiled=True)

    seq_axes = ("outer", "inner") if fast else "outer"
    shares = outer * inner if fast else outer
    share = query_weight.shape[1] // shares

    def exchange(block):
        return lax.all_to_all(block, seq_axes, split_axis=0, concat_axis=0, tiled=True)

    if fast:
        sent = cut(query_weight, shares, 2)
    else:
        weight = exchange(
            jnp.stack([query_weight[:, i * share : (i + 1) * share] for i in range(shares)])
        )
        weight = lax.all_gather(weight, "inner", axis=1).reshape(model, share)
    heads_here = share // key_width

    if fast:
        quarter = row_count // heads_axis
        mine = lax.dynamic_slice_in_dim(tokens, h * quarter, quarter, 0)
        mine, before, after, far = ring_pieces(mine, "outer")
        begin, before, after, far, edge = lax.optimization_barrier(
            (sent[0], before, after, far, edge)
        )
        weight_first = exchange(begin)
        near = jnp.concatenate([mine, before, after, far], axis=0)
        beside = swap(near, "inner", 1)
        beside, turned = lax.optimization_barrier((beside, out_weights[0]))
        out_weights.append(swap(turned, "inner", 1))
        pieces = [near, beside, swap(near, "head", 2)]
        steps = [(line, side, turn) for turn in (0, 2) for side in (0, 1) for line in range(4)]
        steps = steps + [(a, b, k ^ 1) for a, b, k in steps]
        def of_block(block, z, h):
            line, side, turn = steps[block]
            there = (z, (z + 3) & 3, (z + 1) & 3, z ^ 2)[line]
            return side, ((h ^ turn) * outer + there) * quarter

        bases = []
        for block, (_, side, _) in enumerate(steps):
            where = of_block(block, z, h)[1] // quarter
            bases.append((where % outer * inner + (y ^ side)) * row_count + where // outer * quarter)
        bases = jnp.stack(bases)[:, None] + jnp.arange(quarter)[None, :]
        layout = (quarter, inner, of_block)
    else:
        every = gather_line(tokens, "outer", 0)
        queries = [jnp.dot(every, weight, preferred_element_type=jnp.float32).astype(jnp.bfloat16)]
        bases = (jnp.arange(outer) * inner + y)[:, None] * row_count + jnp.arange(row_count)[None, :]
        layout = (row_count, 1, lambda block, z, h: (0, block * row_count))
    places = (context + bases).astype(jnp.int32).reshape(-1, 1)
    here = jnp.stack([z, h, y]).astype(jnp.int32)

    edge_keys, edge_values = edge[:, : raw_keys.shape[1]], edge[:, raw_keys.shape[1] :]
    packed = compress(
        raw_keys, raw_values, edge_keys, edge_values,
        key_expand, key_mix, key_reduce, value_expand, value_mix, value_reduce,
    )
    ids = np.arange(devices * blocks).reshape(outer, inner, heads_axis, blocks)
    if fast:
        stay = lax.dynamic_index_in_dim(packed, h, 0, False)
        away = [lax.dynamic_index_in_dim(packed, h ^ step, 0, False) for step in (1, 2, 3)]
        came = [swap(piece, "head", step) for step, piece in zip((1, 2, 3), away)]
        packed = jnp.concatenate([stay, *came], axis=0)
        bound = np.broadcast_to(ids.max(axis=(2, 3), keepdims=True), ids.shape)
    else:
        packed = jnp.broadcast_to(packed[:, None], (G, heads_axis // G, *packed.shape[1:]))
        packed = packed.reshape(heads_axis, blocks, -1)
        packed = lax.all_to_all(packed, "head", split_axis=0, concat_axis=0, tiled=True)
        packed = packed.reshape(heads_axis * blocks, -1)
        bound = ids
    if fast:
        packed, pieces = lax.optimization_barrier((packed, pieces))
        pieces.append(swap(pieces[1], "head", 2))
        pieces, out_weights[1] = lax.optimization_barrier((pieces, out_weights[1]))
        partners = [swap(piece, "head", 1) for piece in pieces]
    packed = gather_line(packed, "outer", 0)
    if fast:
        begin, packed = lax.optimization_barrier((sent[1], packed))
        queries = [project([*pieces, *partners], [weight_first, exchange(begin)])]
    packed = gather_pair(packed, "inner").reshape(devices * blocks, -1)
    bound = (STRIDE * bound + BLK - 1).transpose(1, 0, 2, 3).reshape(-1)
    hidden = [bool((bound[i : i + LANES] > context).any()) for i in range(0, len(bound), LANES)]
    masked, start = [], 0
    for i in range(1, len(hidden) + 1):
        if i == len(hidden) or hidden[i] != hidden[start]:
            masked.append((start * LANES, min(i * LANES, len(bound)), hidden[start]))
            start = i
    if fast:
        column = np.arange(heads_axis)[None, None, :, None]
        ids = ids[:, :, :1] + (column ^ h) * blocks
        limits = (STRIDE * ids + BLK - 1).transpose(1, 0, 2, 3).reshape(1, -1).astype(jnp.int32)
    else:
        limits = (STRIDE * ids + BLK - 1).transpose(1, 0, 2, 3).reshape(1, -1)
        limits = jnp.asarray(limits, jnp.int32)

    total = None
    for head in range(heads_here):
        attended = attend(
            here, queries, head, packed, limits, places, key_width, masked, layout
        )
        if fast:
            last = head == heads_here - 1
            block = jnp.concatenate([attended[0], swap(attended[1], "inner", 1)], axis=1)
            total = expel(
                here, line_pieces(block, "outer"), out_weights, [] if total is None else [total],
                head, heads_here, (heads_axis, quarter) if last else None,
            )
        else:
            attended = gather_line(attended[0], "outer", 1)
            rows = out_weights.reshape(outer, heads_here, value_width, -1)[:, head]
            product = jnp.dot(
                attended, rows.reshape(outer * value_width, -1), preferred_element_type=jnp.float32
            )
            total = product if total is None else total + product

    if fast:
        keep, send = total
        columns = keep.shape[-1]
        total = keep + swap(send, "head", 1).astype(jnp.float32)
        x = h // 2
        keep = lax.dynamic_index_in_dim(total, x, 1, False)
        send = lax.dynamic_index_in_dim(total, 1 - x, 1, False).astype(jnp.bfloat16)
        total = keep + swap(send, "head", 2).astype(jnp.float32)
        result = total.astype(jnp.bfloat16).reshape(row_count, columns)
        first, second = result[:, : columns // 2], result[:, columns // 2 :]
        result = jnp.concatenate(
            [jnp.where(y == 0, first, second), jnp.where(y == 0, second, first)], axis=1
        )
        route = [
            ((a * inner + b) * heads_axis + k, (k * inner + b) * heads_axis + a)
            for a in range(outer) for b in range(inner) for k in range(heads_axis)
        ]
        return lax.ppermute(result, ("outer", "inner", "head"), route)
    columns = total.shape[1]
    total = lax.psum_scatter(total, "head", scatter_dimension=0, tiled=True).astype(jnp.bfloat16)
    total = lax.all_gather(total, "head", axis=0, tiled=True)
    total = lax.all_to_all(
        total.reshape(outer, row_count, columns), "outer", split_axis=0, concat_axis=0, tiled=True
    )
    total = total.transpose(1, 0, 2).reshape(row_count, model)
    return lax.dynamic_slice_in_dim(total, h * (model // heads_axis), model // heads_axis, 1)


def solution(mesh):
    seq_count, head_count = mesh.shape["seq"], mesh.shape["head"]
    inner = seq_count // OUTER
    finer = Mesh(
        mesh.devices.reshape(OUTER, inner, head_count), ("outer", "inner", "head")
    )
    seq = ("outer", "inner")
    in_specs = (
        P(seq, None),
        P((*seq, "head"), None),
        P((*seq, "head"), None),
        P(seq, "head"),
        P("head", seq),
        P(), P(), P(), P(), P(), P(),
    )
    return jax.shard_map(
        shards, mesh=finer, in_specs=in_specs, out_specs=P(seq, "head"), check_vma=False
    )
```

```python
import jax
import jax.numpy as jnp
import numpy as np
from jax import lax
from jax.experimental import pallas as pl
from jax.experimental.pallas import tpu as pltpu
from jax.sharding import Mesh
from jax.sharding import PartitionSpec as P

G = 4
BLK = 32
STRIDE = 16
LANES = 128
OUTER = 4
VMEM_LIMIT = 20 * 1024 * 1024


def round_up(value, unit):
    return -(-value // unit) * unit


def swap(block, axis, bit):
    return lax.ppermute(block, axis, [(i, i ^ bit) for i in range(lax.axis_size(axis))])


def window_of(group, width):
    low = group * width // LANES * LANES
    return low, round_up((group + 1) * width, LANES) - low, group * width - low


def compress_one(raw_ref, edge_ref, expand_ref, mix_ref, reduce_ref, sorted_ref, hidden_ref, groups):
    width, units = expand_ref.shape
    tokens = raw_ref.shape[0]
    rows = 8 * STRIDE
    chunks = tokens // rows
    blocks = tokens // STRIDE
    to = lax.broadcasted_iota(jnp.int32, (rows, rows), 0)
    come = lax.broadcasted_iota(jnp.int32, (rows, rows), 1)
    order = (come == (to % 8) * STRIDE + to // 8).astype(jnp.bfloat16)
    for chunk in range(chunks):
        piece = slice(chunk * rows, (chunk + 1) * rows)
        sorted_ref[piece, :] = jnp.dot(
            order, raw_ref[piece, :], preferred_element_type=jnp.float32
        ).astype(jnp.bfloat16)
    tile = 256 if units % 256 == 0 else units
    for group in range(groups):
        low, span, offset = window_of(group, width)
        parts = []
        if offset:
            parts.append(jnp.zeros((offset, units), jnp.bfloat16))
        parts.append(expand_ref[...])
        if span - offset - width:
            parts.append(jnp.zeros((span - offset - width, units), jnp.bfloat16))
        expand = jnp.concatenate(parts, axis=0) if len(parts) > 1 else parts[0]
        for start in range(0, units, tile):
            lanes = slice(start, start + tile)
            weight = expand[:, lanes]
            projected = jnp.dot(
                sorted_ref[:, low : low + span], weight, preferred_element_type=jnp.float32
            ).reshape(chunks, STRIDE, 8, tile)
            mix_low = mix_ref[:STRIDE, lanes][None, :, None, :]
            mix_high = mix_ref[STRIDE:, lanes]
            first = jnp.sum(projected * mix_low, axis=1).reshape(blocks, tile)
            second = jnp.sum(projected * mix_high[None, :, None, :], axis=1).reshape(blocks, tile)
            edge = jnp.dot(edge_ref[:, low : low + span], weight, preferred_element_type=jnp.float32)
            edge = jnp.sum(edge * mix_high, axis=0, keepdims=True)
            hidden = first + jnp.concatenate([second[1:], edge], axis=0)
            half = 0.5 * hidden
            activated = half + half * lax.erf(hidden * np.float32(2.0**-0.5))
            hidden_ref[group * blocks : (group + 1) * blocks, lanes] = activated.astype(jnp.bfloat16)
    return jnp.dot(hidden_ref[...], reduce_ref[...], preferred_element_type=jnp.float32).astype(
        jnp.bfloat16
    )


def compress_kernel(
    raw_keys, raw_values, edge_keys, edge_values, key_expand, key_mix, key_reduce,
    value_expand, value_mix, value_reduce, packed, sorted_keys, sorted_values, hidden,
):
    groups, blocks, _ = packed.shape
    key_width = key_expand.shape[0]
    value_start = round_up(key_width, LANES)
    keys = compress_one(
        raw_keys, edge_keys, key_expand, key_mix, key_reduce, sorted_keys, hidden, groups
    )
    values = compress_one(
        raw_values, edge_values, value_expand, value_mix, value_reduce, sorted_values, hidden, groups
    )
    for group in range(groups):
        rows = slice(group * blocks, (group + 1) * blocks)
        packed[group, :, :key_width] = keys[rows]
        packed[group, :, key_width:value_start] = jnp.zeros(
            (blocks, value_start - key_width), jnp.bfloat16
        )
        packed[group, :, value_start:] = values[rows]


def compress(raw_keys, raw_values, edge_keys, edge_values, *weights):
    key_expand, _, _, value_expand, _, _ = weights
    units = key_expand.shape[1]
    tokens = raw_keys.shape[0]
    blocks = tokens // STRIDE
    width = round_up(key_expand.shape[0], LANES) + value_expand.shape[0]
    flops = 2 * tokens * units * (raw_keys.shape[1] + raw_values.shape[1])
    return pl.pallas_call(
        compress_kernel,
        out_shape=jax.ShapeDtypeStruct((G, blocks, width), jnp.bfloat16),
        scratch_shapes=[
            pltpu.VMEM(raw_keys.shape, jnp.bfloat16),
            pltpu.VMEM(raw_values.shape, jnp.bfloat16),
            pltpu.VMEM((G * blocks, units), jnp.bfloat16),
        ],
        compiler_params=pltpu.CompilerParams(vmem_limit_bytes=56 * 1024 * 1024),
        cost_estimate=pl.CostEstimate(
            flops=flops, bytes_accessed=2 * raw_keys.size, transcendentals=0
        ),
        name="compress",
    )(raw_keys, raw_values, edge_keys, edge_values, *weights)


def cut(weight, shares, parts):
    rows, columns = weight.shape
    share, part = columns // shares, rows // parts

    def kernel(in_ref, *out_refs):
        for index, out_ref in enumerate(out_refs):
            out_ref[0] = in_ref[index * part : (index + 1) * part, :]

    return pl.pallas_call(
        kernel,
        out_shape=(jax.ShapeDtypeStruct((shares, part, share), weight.dtype),) * parts,
        grid=(shares,),
        in_specs=[pl.BlockSpec((rows, share), lambda i: (0, i))],
        out_specs=(pl.BlockSpec((1, part, share), lambda i: (i, 0, 0)),) * parts,
        cost_estimate=pl.CostEstimate(flops=0, bytes_accessed=0, transcendentals=0),
        name="cut",
    )(weight)


def project(pieces, weights):
    part, depth = pieces[0].shape
    rows = part * len(pieces)
    shares, share, columns = weights[0].shape
    group = len(pieces) // 2
    count = len(pieces)

    def kernel(*refs):
        piece_refs, weight_refs = refs[:count], refs[count : count + len(weights)]
        out_ref, rows_ref, weight_ref, sems = refs[count + len(weights) :]
        copies = [
            pltpu.make_async_copy(
                piece, rows_ref.at[index * part : (index + 1) * part], sems.at[index]
            )
            for index, piece in enumerate(piece_refs)
        ]
        bring = []
        for index, weight in enumerate(weight_refs):
            for owner in range(shares):
                start = (owner * len(weights) + index) * share
                bring.append(
                    pltpu.make_async_copy(
                        weight.at[owner], weight_ref.at[start : start + share],
                        sems.at[count + len(bring)],
                    )
                )
        for copy in bring + copies:
            copy.start()
        for copy in bring:
            copy.wait()
        for start in range(0, count, group):
            for copy in copies[start : start + group]:
                copy.wait()
            place = slice(start * part, (start + group) * part)
            out_ref[place, :] = jnp.dot(
                rows_ref[place, :], weight_ref[...], preferred_element_type=jnp.float32
            ).astype(jnp.bfloat16)

    return pl.pallas_call(
        kernel,
        out_shape=jax.ShapeDtypeStruct((rows, columns), jnp.bfloat16),
        in_specs=[pl.BlockSpec(memory_space=pl.ANY)] * (count + len(weights)),
        scratch_shapes=[
            pltpu.VMEM((rows, depth), jnp.bfloat16),
            pltpu.VMEM((depth, columns), jnp.bfloat16),
            pltpu.SemaphoreType.DMA((count + len(weights) * shares,)),
        ],
        compiler_params=pltpu.CompilerParams(vmem_limit_bytes=VMEM_LIMIT),
        cost_estimate=pl.CostEstimate(
            flops=2 * rows * depth * columns, bytes_accessed=2 * rows * depth, transcendentals=0
        ),
        name="project",
    )(*pieces, *weights)


def attend(here, queries, head, packed, limits, places, key_width, masked, layout):
    rows_each = queries[0].shape[0]
    rows = rows_each * len(queries)
    value_start = round_up(key_width, LANES)
    value_width = packed.shape[1] - value_start
    columns = packed.shape[0]
    factor = np.float32(key_width**-0.5 * np.log2(np.e))
    tile = min(256, rows_each)
    unit, outputs, sends = layout

    def kernel(here_ref, *refs):
        query_refs = refs[: len(queries)]
        kv_ref, limit_ref, place_ref = refs[len(queries) : len(queries) + 3]
        out_refs = refs[len(queries) + 3 :]
        keys = kv_ref[:, :key_width]
        values = kv_ref[:, value_start:]
        for start in range(0, rows, tile):
            from_ref, at = query_refs[start // rows_each], start % rows_each
            query = from_ref[at : at + tile, head * key_width : (head + 1) * key_width]
            scores = lax.dot_general(
                query, keys, (((1,), (1,)), ((), ())), preferred_element_type=jnp.float32
            )
            pieces = []
            for low, high, hide in masked:
                piece = scores[:, low:high]
                if hide:
                    visible = limit_ref[:, low:high] <= place_ref[start : start + tile, :]
                    piece = jnp.where(visible, piece, -jnp.inf)
                pieces.append(piece)
            scores = jnp.concatenate(pieces, axis=1) if len(pieces) > 1 else pieces[0]
            top = jnp.max(scores, axis=1, keepdims=True)
            exponent = jnp.exp2((scores - top) * factor)
            total = jnp.sum(exponent, axis=1, keepdims=True)
            numerator = jnp.dot(
                exponent.astype(jnp.bfloat16), values, preferred_element_type=jnp.float32
            )
            done = (numerator / total).astype(jnp.bfloat16)
            for low in range(0, tile, unit):
                which, where = sends((start + low) // unit, here_ref[0], here_ref[1])
                if not isinstance(where, int):
                    where = pl.multiple_of(where, unit)
                out_refs[which][pl.ds(where, unit), :] = done[low : low + unit]

    shape = jax.ShapeDtypeStruct((rows // outputs, value_width), jnp.bfloat16)
    return pl.pallas_call(
        kernel,
        out_shape=(shape,) * outputs,
        in_specs=[pl.BlockSpec(memory_space=pltpu.SMEM)]
        + [pl.BlockSpec(memory_space=pltpu.VMEM)] * (len(queries) + 3),
        compiler_params=pltpu.CompilerParams(vmem_limit_bytes=VMEM_LIMIT),
        cost_estimate=pl.CostEstimate(
            flops=2 * rows * columns * (key_width + value_width),
            bytes_accessed=2 * packed.size,
            transcendentals=0,
        ),
        name="attend",
    )(here, *queries, packed, limits, places)


def expel(place, pieces, weights, before, chunk, chunks, shape):
    rows, width = pieces[0].shape
    depth, step, single = 4 * width, weights[0].shape[0], width // 2
    last = shape is not None

    def kernel(place_ref, *refs):
        own, up, down, passed, far = refs[:5]
        weight_refs = refs[5 : 5 + len(weights)]
        rest = refs[5 + len(weights) :]
        before_refs, outs = rest[: len(before)], rest[len(before) :]
        z, core, y = place_ref[0], place_ref[1] & 1, place_ref[2]
        lower = jnp.where(z == 0, passed[...], up[...])
        upper = jnp.where(z == 3, passed[...], down[...])
        for side, weight in enumerate(weight_refs):
            lanes = slice(side * step, (side + 1) * step)
            total = before_refs[0][:, lanes] if before else None
            for block, at in (
                (own[...], z), (lower, (z + 3) & 3), (upper, (z + 1) & 3), (far[...], z ^ 2)
            ):
                starts = [((at * 2 + inner) * chunks + chunk) * single for inner in (y, 1 - y)]
                both = [weight[:, pl.ds(pl.multiple_of(start, single), single)] for start in starts]
                product = lax.dot_general(
                    block, jnp.concatenate(both, axis=1), (((1,), (1,)), ((), ())),
                    preferred_element_type=jnp.float32,
                )
                total = product if total is None else total + product
            if not last:
                outs[0][:, lanes] = total
                continue
            keep_ref, send_ref, hold_ref = outs
            hold_ref[...] = total.reshape(hold_ref.shape)
            keep_ref[:, :, :, lanes] = hold_ref[:, :, pl.ds(core, 1)][:, :, 0]
            send_ref[:, :, :, lanes] = hold_ref[:, :, pl.ds(1 - core, 1)][:, :, 0].astype(jnp.bfloat16)

    columns = step * len(weights)
    if last:
        groups, quarter = shape
        out_shape = (
            jax.ShapeDtypeStruct((groups, 2, quarter, columns), jnp.float32),
            jax.ShapeDtypeStruct((groups, 2, quarter, columns), jnp.bfloat16),
        )
        scratch = [pltpu.VMEM((groups, 2, 2, quarter, step), jnp.float32)]
    else:
        out_shape, scratch = jax.ShapeDtypeStruct((rows, columns), jnp.float32), []
    count = len(pieces) + len(weights) + len(before)
    return pl.pallas_call(
        kernel,
        out_shape=out_shape,
        in_specs=[pl.BlockSpec(memory_space=pltpu.SMEM)]
        + [pl.BlockSpec(memory_space=pltpu.VMEM)] * count,
        scratch_shapes=scratch,
        compiler_params=pltpu.CompilerParams(vmem_limit_bytes=VMEM_LIMIT),
        cost_estimate=pl.CostEstimate(
            flops=2 * rows * depth * columns, bytes_accessed=2 * depth * columns, transcendentals=0
        ),
        name="expel",
    )(place, *pieces, *weights, *before)


def line_pieces(block, axis):
    far = swap(block, axis, 2)
    up = lax.ppermute(block, axis, [(i, i + 1) for i in range(3)])
    down = lax.ppermute(block, axis, [(i + 1, i) for i in range(3)])
    passed = lax.ppermute(far, axis, [(1, 0), (2, 3)])
    return block, up, down, passed, far


def ring_pieces(block, axis):
    before = lax.ppermute(block, axis, [(i, (i + 1) % 4) for i in range(4)])
    after = lax.ppermute(block, axis, [((i + 1) % 4, i) for i in range(4)])
    return block, before, after, swap(block, axis, 2)


def gather_line(block, axis, dim):
    count = lax.axis_size(axis)
    if count != 4:
        return lax.all_gather(block, axis, axis=dim, tiled=True)
    me = lax.axis_index(axis)
    block, before, after, far = ring_pieces(block, axis)
    size = block.shape[dim]
    shape = list(block.shape)
    shape[dim] = count * size
    out = jnp.zeros(shape, block.dtype)
    for piece, place in ((block, me), (before, (me + 3) % 4), (after, (me + 1) % 4), (far, me ^ 2)):
        out = lax.dynamic_update_slice_in_dim(out, piece, place * size, dim)
    return out


def gather_pair(block, axis):
    if lax.axis_size(axis) != 2:
        return lax.all_gather(block, axis, axis=0)
    other = swap(block, axis, 1)
    first = lax.axis_index(axis) == 0
    return jnp.stack([jnp.where(first, block, other), jnp.where(first, other, block)])


def shards(
    tokens, raw_keys, raw_values, query_weight, output_weight,
    key_expand, key_mix, key_reduce, value_expand, value_mix, value_reduce,
):
    outer, inner, heads_axis = (lax.axis_size(name) for name in ("outer", "inner", "head"))
    z, y, h = (lax.axis_index(name) for name in ("outer", "inner", "head"))
    key_width, value_width = key_expand.shape[0], value_expand.shape[0]
    row_count, model = tokens.shape
    devices = outer * inner * heads_axis
    blocks = raw_keys.shape[0] // STRIDE
    context = raw_keys.shape[0] * devices - row_count * outer * inner
    part = query_weight.shape[0]
    fast = inner == 2 and outer == 4 and heads_axis == 4

    edge = jnp.concatenate([raw_keys[:STRIDE], raw_values[:STRIDE]], axis=1)
    edge = lax.ppermute(
        edge, ("outer", "inner", "head"), [(i + 1, i) for i in range(devices - 1)]
    )

    if fast:
        turned, edge = lax.optimization_barrier((output_weight.T, edge))
        out_weights = [turned, swap(turned, "inner", 1)]
    else:
        out_weights = lax.all_gather(output_weight, "inner", axis=1, tiled=True)

    seq_axes = ("outer", "inner") if fast else "outer"
    shares = outer * inner if fast else outer
    share = query_weight.shape[1] // shares

    def exchange(block):
        return lax.all_to_all(block, seq_axes, split_axis=0, concat_axis=0, tiled=True)

    if fast:
        sent = cut(query_weight, shares, 2)
    else:
        weight = exchange(
            jnp.stack([query_weight[:, i * share : (i + 1) * share] for i in range(shares)])
        )
        weight = lax.all_gather(weight, "inner", axis=1).reshape(model, share)
    heads_here = share // key_width

    if fast:
        quarter = row_count // heads_axis
        mine = lax.dynamic_slice_in_dim(tokens, h * quarter, quarter, 0)
        mine, before, after, far = ring_pieces(mine, "outer")
        begin, before, after, far, edge = lax.optimization_barrier(
            (sent[0], before, after, far, edge)
        )
        weight_first = exchange(begin)
        near = jnp.concatenate([mine, before, after, far], axis=0)
        beside = swap(near, "inner", 1)
        pieces = [near, beside, swap(near, "head", 2)]
        steps = [(line, side, turn) for turn in (0, 2) for side in (0, 1) for line in range(4)]
        steps = steps + [(a, b, k ^ 1) for a, b, k in steps]
        def of_block(block, z, h):
            line, side, turn = steps[block]
            there = (z, (z + 3) & 3, (z + 1) & 3, z ^ 2)[line]
            return side, ((h ^ turn) * outer + there) * quarter

        bases = []
        for block, (_, side, _) in enumerate(steps):
            where = of_block(block, z, h)[1] // quarter
            bases.append((where % outer * inner + (y ^ side)) * row_count + where // outer * quarter)
        bases = jnp.stack(bases)[:, None] + jnp.arange(quarter)[None, :]
        layout = (quarter, inner, of_block)
    else:
        every = gather_line(tokens, "outer", 0)
        queries = [jnp.dot(every, weight, preferred_element_type=jnp.float32).astype(jnp.bfloat16)]
        bases = (jnp.arange(outer) * inner + y)[:, None] * row_count + jnp.arange(row_count)[None, :]
        layout = (row_count, 1, lambda block, z, h: (0, block * row_count))
    places = (context + bases).astype(jnp.int32).reshape(-1, 1)
    here = jnp.stack([z, h, y]).astype(jnp.int32)

    edge_keys, edge_values = edge[:, : raw_keys.shape[1]], edge[:, raw_keys.shape[1] :]
    packed = compress(
        raw_keys, raw_values, edge_keys, edge_values,
        key_expand, key_mix, key_reduce, value_expand, value_mix, value_reduce,
    )
    ids = np.arange(devices * blocks).reshape(outer, inner, heads_axis, blocks)
    if fast:
        stay = lax.dynamic_index_in_dim(packed, h, 0, False)
        away = [lax.dynamic_index_in_dim(packed, h ^ step, 0, False) for step in (1, 2, 3)]
        came = [swap(piece, "head", step) for step, piece in zip((1, 2, 3), away)]
        packed = jnp.concatenate([stay, *came], axis=0)
        bound = np.broadcast_to(ids.max(axis=(2, 3), keepdims=True), ids.shape)
    else:
        packed = jnp.broadcast_to(packed[:, None], (G, heads_axis // G, *packed.shape[1:]))
        packed = packed.reshape(heads_axis, blocks, -1)
        packed = lax.all_to_all(packed, "head", split_axis=0, concat_axis=0, tiled=True)
        packed = packed.reshape(heads_axis * blocks, -1)
        bound = ids
    if fast:
        packed, out_weights[1] = lax.optimization_barrier((packed, out_weights[1]))
    packed = gather_line(packed, "outer", 0)
    if fast:
        begin, packed, pieces = lax.optimization_barrier((sent[1], packed, pieces))
        pieces.append(swap(pieces[1], "head", 2))
        partners = [swap(piece, "head", 1) for piece in pieces]
        queries = [project([*pieces, *partners], [weight_first, exchange(begin)])]
    packed = gather_pair(packed, "inner").reshape(devices * blocks, -1)
    bound = (STRIDE * bound + BLK - 1).transpose(1, 0, 2, 3).reshape(-1)
    hidden = [bool((bound[i : i + LANES] > context).any()) for i in range(0, len(bound), LANES)]
    masked, start = [], 0
    for i in range(1, len(hidden) + 1):
        if i == len(hidden) or hidden[i] != hidden[start]:
            masked.append((start * LANES, min(i * LANES, len(bound)), hidden[start]))
            start = i
    if fast:
        column = np.arange(heads_axis)[None, None, :, None]
        ids = ids[:, :, :1] + (column ^ h) * blocks
        limits = (STRIDE * ids + BLK - 1).transpose(1, 0, 2, 3).reshape(1, -1).astype(jnp.int32)
    else:
        limits = (STRIDE * ids + BLK - 1).transpose(1, 0, 2, 3).reshape(1, -1)
        limits = jnp.asarray(limits, jnp.int32)

    total = None
    for head in range(heads_here):
        attended = attend(
            here, queries, head, packed, limits, places, key_width, masked, layout
        )
        if fast:
            last = head == heads_here - 1
            block = jnp.concatenate([attended[0], swap(attended[1], "inner", 1)], axis=1)
            total = expel(
                here, line_pieces(block, "outer"), out_weights, [] if total is None else [total],
                head, heads_here, (heads_axis, quarter) if last else None,
            )
        else:
            attended = gather_line(attended[0], "outer", 1)
            rows = out_weights.reshape(outer, heads_here, value_width, -1)[:, head]
            product = jnp.dot(
                attended, rows.reshape(outer * value_width, -1), preferred_element_type=jnp.float32
            )
            total = product if total is None else total + product

    if fast:
        keep, send = total
        columns = keep.shape[-1]
        total = keep + swap(send, "head", 1).astype(jnp.float32)
        x = h // 2
        keep = lax.dynamic_index_in_dim(total, x, 1, False)
        send = lax.dynamic_index_in_dim(total, 1 - x, 1, False).astype(jnp.bfloat16)
        total = keep + swap(send, "head", 2).astype(jnp.float32)
        result = total.astype(jnp.bfloat16).reshape(row_count, columns)
        first, second = result[:, : columns // 2], result[:, columns // 2 :]
        result = jnp.concatenate(
            [jnp.where(y == 0, first, second), jnp.where(y == 0, second, first)], axis=1
        )
        route = [
            ((a * inner + b) * heads_axis + k, (k * inner + b) * heads_axis + a)
            for a in range(outer) for b in range(inner) for k in range(heads_axis)
        ]
        return lax.ppermute(result, ("outer", "inner", "head"), route)
    columns = total.shape[1]
    total = lax.psum_scatter(total, "head", scatter_dimension=0, tiled=True).astype(jnp.bfloat16)
    total = lax.all_gather(total, "head", axis=0, tiled=True)
    total = lax.all_to_all(
        total.reshape(outer, row_count, columns), "outer", split_axis=0, concat_axis=0, tiled=True
    )
    total = total.transpose(1, 0, 2).reshape(row_count, model)
    return lax.dynamic_slice_in_dim(total, h * (model // heads_axis), model // heads_axis, 1)


def solution(mesh):
    seq_count, head_count = mesh.shape["seq"], mesh.shape["head"]
    inner = seq_count // OUTER
    finer = Mesh(
        mesh.devices.reshape(OUTER, inner, head_count), ("outer", "inner", "head")
    )
    seq = ("outer", "inner")
    in_specs = (
        P(seq, None),
        P((*seq, "head"), None),
        P((*seq, "head"), None),
        P(seq, "head"),
        P("head", seq),
        P(), P(), P(), P(), P(), P(),
    )
    return jax.shard_map(
        shards, mesh=finer, in_specs=in_specs, out_specs=P(seq, "head"), check_vma=False
    )
```

```python
import jax
import jax.numpy as jnp
import numpy as np
from jax import lax
from jax.experimental import pallas as pl
from jax.experimental.pallas import tpu as pltpu
from jax.sharding import Mesh
from jax.sharding import PartitionSpec as P

G = 4
BLK = 32
STRIDE = 16
LANES = 128
OUTER = 4
VMEM_LIMIT = 20 * 1024 * 1024


def round_up(value, unit):
    return -(-value // unit) * unit


def swap(block, axis, bit):
    return lax.ppermute(block, axis, [(i, i ^ bit) for i in range(lax.axis_size(axis))])


def window_of(group, width):
    low = group * width // LANES * LANES
    return low, round_up((group + 1) * width, LANES) - low, group * width - low


def compress_one(raw_ref, edge_ref, expand_ref, mix_ref, reduce_ref, sorted_ref, hidden_ref, groups):
    width, units = expand_ref.shape
    tokens = raw_ref.shape[0]
    rows = 8 * STRIDE
    chunks = tokens // rows
    blocks = tokens // STRIDE
    to = lax.broadcasted_iota(jnp.int32, (rows, rows), 0)
    come = lax.broadcasted_iota(jnp.int32, (rows, rows), 1)
    order = (come == (to % 8) * STRIDE + to // 8).astype(jnp.bfloat16)
    for chunk in range(chunks):
        piece = slice(chunk * rows, (chunk + 1) * rows)
        sorted_ref[piece, :] = jnp.dot(
            order, raw_ref[piece, :], preferred_element_type=jnp.float32
        ).astype(jnp.bfloat16)
    tile = 256 if units % 256 == 0 else units
    for group in range(groups):
        low, span, offset = window_of(group, width)
        parts = []
        if offset:
            parts.append(jnp.zeros((offset, units), jnp.bfloat16))
        parts.append(expand_ref[...])
        if span - offset - width:
            parts.append(jnp.zeros((span - offset - width, units), jnp.bfloat16))
        expand = jnp.concatenate(parts, axis=0) if len(parts) > 1 else parts[0]
        for start in range(0, units, tile):
            lanes = slice(start, start + tile)
            weight = expand[:, lanes]
            projected = jnp.dot(
                sorted_ref[:, low : low + span], weight, preferred_element_type=jnp.float32
            ).reshape(chunks, STRIDE, 8, tile)
            mix_low = mix_ref[:STRIDE, lanes][None, :, None, :]
            mix_high = mix_ref[STRIDE:, lanes]
            first = jnp.sum(projected * mix_low, axis=1).reshape(blocks, tile)
            second = jnp.sum(projected * mix_high[None, :, None, :], axis=1).reshape(blocks, tile)
            edge = jnp.dot(edge_ref[:, low : low + span], weight, preferred_element_type=jnp.float32)
            edge = jnp.sum(edge * mix_high, axis=0, keepdims=True)
            hidden = first + jnp.concatenate([second[1:], edge], axis=0)
            half = 0.5 * hidden
            activated = half + half * lax.erf(hidden * np.float32(2.0**-0.5))
            hidden_ref[group * blocks : (group + 1) * blocks, lanes] = activated.astype(jnp.bfloat16)
    return jnp.dot(hidden_ref[...], reduce_ref[...], preferred_element_type=jnp.float32).astype(
        jnp.bfloat16
    )


def compress_kernel(
    raw_keys, raw_values, edge_keys, edge_values, key_expand, key_mix, key_reduce,
    value_expand, value_mix, value_reduce, packed, sorted_keys, sorted_values, hidden,
):
    groups, blocks, _ = packed.shape
    key_width = key_expand.shape[0]
    value_start = round_up(key_width, LANES)
    keys = compress_one(
        raw_keys, edge_keys, key_expand, key_mix, key_reduce, sorted_keys, hidden, groups
    )
    values = compress_one(
        raw_values, edge_values, value_expand, value_mix, value_reduce, sorted_values, hidden, groups
    )
    for group in range(groups):
        rows = slice(group * blocks, (group + 1) * blocks)
        packed[group, :, :key_width] = keys[rows]
        packed[group, :, key_width:value_start] = jnp.zeros(
            (blocks, value_start - key_width), jnp.bfloat16
        )
        packed[group, :, value_start:] = values[rows]


def compress(raw_keys, raw_values, edge_keys, edge_values, *weights):
    key_expand, _, _, value_expand, _, _ = weights
    units = key_expand.shape[1]
    tokens = raw_keys.shape[0]
    blocks = tokens // STRIDE
    width = round_up(key_expand.shape[0], LANES) + value_expand.shape[0]
    flops = 2 * tokens * units * (raw_keys.shape[1] + raw_values.shape[1])
    return pl.pallas_call(
        compress_kernel,
        out_shape=jax.ShapeDtypeStruct((G, blocks, width), jnp.bfloat16),
        scratch_shapes=[
            pltpu.VMEM(raw_keys.shape, jnp.bfloat16),
            pltpu.VMEM(raw_values.shape, jnp.bfloat16),
            pltpu.VMEM((G * blocks, units), jnp.bfloat16),
        ],
        compiler_params=pltpu.CompilerParams(vmem_limit_bytes=56 * 1024 * 1024),
        cost_estimate=pl.CostEstimate(
            flops=flops, bytes_accessed=2 * raw_keys.size, transcendentals=0
        ),
        name="compress",
    )(raw_keys, raw_values, edge_keys, edge_values, *weights)


def cut(weight, shares, parts):
    rows, columns = weight.shape
    share, part = columns // shares, rows // parts

    def kernel(in_ref, *out_refs):
        for index, out_ref in enumerate(out_refs):
            out_ref[0] = in_ref[index * part : (index + 1) * part, :]

    return pl.pallas_call(
        kernel,
        out_shape=(jax.ShapeDtypeStruct((shares, part, share), weight.dtype),) * parts,
        grid=(shares,),
        in_specs=[pl.BlockSpec((rows, share), lambda i: (0, i))],
        out_specs=(pl.BlockSpec((1, part, share), lambda i: (i, 0, 0)),) * parts,
        cost_estimate=pl.CostEstimate(flops=0, bytes_accessed=0, transcendentals=0),
        name="cut",
    )(weight)


def project(pieces, weights):
    part, depth = pieces[0].shape
    rows = part * len(pieces)
    shares, share, columns = weights[0].shape
    group = len(pieces) // 2
    count = len(pieces)

    def kernel(*refs):
        piece_refs, weight_refs = refs[:count], refs[count : count + len(weights)]
        out_ref, rows_ref, weight_ref, sems = refs[count + len(weights) :]
        copies = [
            pltpu.make_async_copy(
                piece, rows_ref.at[index * part : (index + 1) * part], sems.at[index]
            )
            for index, piece in enumerate(piece_refs)
        ]
        bring = []
        for index, weight in enumerate(weight_refs):
            for owner in range(shares):
                start = (owner * len(weights) + index) * share
                bring.append(
                    pltpu.make_async_copy(
                        weight.at[owner], weight_ref.at[start : start + share],
                        sems.at[count + len(bring)],
                    )
                )
        for copy in bring + copies:
            copy.start()
        for copy in bring:
            copy.wait()
        for start in range(0, count, group):
            for copy in copies[start : start + group]:
                copy.wait()
            place = slice(start * part, (start + group) * part)
            out_ref[place, :] = jnp.dot(
                rows_ref[place, :], weight_ref[...], preferred_element_type=jnp.float32
            ).astype(jnp.bfloat16)

    return pl.pallas_call(
        kernel,
        out_shape=jax.ShapeDtypeStruct((rows, columns), jnp.bfloat16),
        in_specs=[pl.BlockSpec(memory_space=pl.ANY)] * (count + len(weights)),
        scratch_shapes=[
            pltpu.VMEM((rows, depth), jnp.bfloat16),
            pltpu.VMEM((depth, columns), jnp.bfloat16),
            pltpu.SemaphoreType.DMA((count + len(weights) * shares,)),
        ],
        compiler_params=pltpu.CompilerParams(vmem_limit_bytes=VMEM_LIMIT),
        cost_estimate=pl.CostEstimate(
            flops=2 * rows * depth * columns, bytes_accessed=2 * rows * depth, transcendentals=0
        ),
        name="project",
    )(*pieces, *weights)


def attend(here, queries, head, packed, starts, limits, places, key_width, masked, layout):
    rows_each = queries[0].shape[0]
    rows = rows_each * len(queries)
    value_start = round_up(key_width, LANES)
    value_width = packed[0].shape[1] - value_start
    size = packed[0].shape[0]
    columns = size * len(packed)
    count = len(packed)
    factor = np.float32(key_width**-0.5 * np.log2(np.e))
    tile = min(256, rows_each)
    unit, outputs, sends = layout

    def kernel(here_ref, *refs):
        piece_refs, query_refs = refs[:count], refs[count : count + len(queries)]
        limit_ref, place_ref = refs[count + len(queries) : count + len(queries) + 2]
        out_refs, kv_ref, sems = refs[count + len(queries) + 2 : -2], refs[-2], refs[-1]
        copies = []
        for index, piece in enumerate(piece_refs):
            start = starts(index, here_ref[0], here_ref[2])
            if not isinstance(start, int):
                start = pl.multiple_of(start * size, size)
            copies.append(
                pltpu.make_async_copy(piece, kv_ref.at[pl.ds(start, size)], sems.at[index])
            )
        for copy in copies:
            copy.start()
        for copy in copies:
            copy.wait()
        keys = kv_ref[:, :key_width]
        values = kv_ref[:, value_start:]
        for start in range(0, rows, tile):
            from_ref, at = query_refs[start // rows_each], start % rows_each
            query = from_ref[at : at + tile, head * key_width : (head + 1) * key_width]
            scores = lax.dot_general(
                query, keys, (((1,), (1,)), ((), ())), preferred_element_type=jnp.float32
            )
            pieces = []
            for low, high, hide in masked:
                piece = scores[:, low:high]
                if hide:
                    visible = limit_ref[:, low:high] <= place_ref[start : start + tile, :]
                    piece = jnp.where(visible, piece, -jnp.inf)
                pieces.append(piece)
            scores = jnp.concatenate(pieces, axis=1) if len(pieces) > 1 else pieces[0]
            top = jnp.max(scores, axis=1, keepdims=True)
            exponent = jnp.exp2((scores - top) * factor)
            total = jnp.sum(exponent, axis=1, keepdims=True)
            numerator = jnp.dot(
                exponent.astype(jnp.bfloat16), values, preferred_element_type=jnp.float32
            )
            done = (numerator / total).astype(jnp.bfloat16)
            for low in range(0, tile, unit):
                which, where = sends((start + low) // unit, here_ref[0], here_ref[1])
                if not isinstance(where, int):
                    where = pl.multiple_of(where, unit)
                out_refs[which][pl.ds(where, unit), :] = done[low : low + unit]

    shape = jax.ShapeDtypeStruct((rows // outputs, value_width), jnp.bfloat16)
    return pl.pallas_call(
        kernel,
        out_shape=(shape,) * outputs,
        in_specs=[pl.BlockSpec(memory_space=pltpu.SMEM)]
        + [pl.BlockSpec(memory_space=pl.ANY)] * count
        + [pl.BlockSpec(memory_space=pltpu.VMEM)] * (len(queries) + 2),
        scratch_shapes=[
            pltpu.VMEM((columns, packed[0].shape[1]), jnp.bfloat16),
            pltpu.SemaphoreType.DMA((count,)),
        ],
        compiler_params=pltpu.CompilerParams(vmem_limit_bytes=VMEM_LIMIT),
        cost_estimate=pl.CostEstimate(
            flops=2 * rows * columns * (key_width + value_width),
            bytes_accessed=2 * columns * packed[0].shape[1],
            transcendentals=0,
        ),
        name="attend",
    )(here, *packed, *queries, limits, places)


def expel(place, pieces, weights, before, chunk, chunks, shape):
    rows, width = pieces[0].shape
    depth, step, single = 4 * width, weights[0].shape[0], width // 2
    last = shape is not None

    def kernel(place_ref, *refs):
        own, up, down, passed, far = refs[:5]
        weight_refs = refs[5 : 5 + len(weights)]
        rest = refs[5 + len(weights) :]
        before_refs, outs = rest[: len(before)], rest[len(before) :]
        z, core, y = place_ref[0], place_ref[1] & 1, place_ref[2]
        lower = jnp.where(z == 0, passed[...], up[...])
        upper = jnp.where(z == 3, passed[...], down[...])
        for side, weight in enumerate(weight_refs):
            lanes = slice(side * step, (side + 1) * step)
            total = before_refs[0][:, lanes] if before else None
            for block, at in (
                (own[...], z), (lower, (z + 3) & 3), (upper, (z + 1) & 3), (far[...], z ^ 2)
            ):
                starts = [((at * 2 + inner) * chunks + chunk) * single for inner in (y, 1 - y)]
                both = [weight[:, pl.ds(pl.multiple_of(start, single), single)] for start in starts]
                product = lax.dot_general(
                    block, jnp.concatenate(both, axis=1), (((1,), (1,)), ((), ())),
                    preferred_element_type=jnp.float32,
                )
                total = product if total is None else total + product
            if not last:
                outs[0][:, lanes] = total
                continue
            keep_ref, send_ref, hold_ref = outs
            hold_ref[...] = total.reshape(hold_ref.shape)
            keep_ref[:, :, :, lanes] = hold_ref[:, :, pl.ds(core, 1)][:, :, 0]
            send_ref[:, :, :, lanes] = hold_ref[:, :, pl.ds(1 - core, 1)][:, :, 0].astype(jnp.bfloat16)

    columns = step * len(weights)
    if last:
        groups, quarter = shape
        out_shape = (
            jax.ShapeDtypeStruct((groups, 2, quarter, columns), jnp.float32),
            jax.ShapeDtypeStruct((groups, 2, quarter, columns), jnp.bfloat16),
        )
        scratch = [pltpu.VMEM((groups, 2, 2, quarter, step), jnp.float32)]
    else:
        out_shape, scratch = jax.ShapeDtypeStruct((rows, columns), jnp.float32), []
    count = len(pieces) + len(weights) + len(before)
    return pl.pallas_call(
        kernel,
        out_shape=out_shape,
        in_specs=[pl.BlockSpec(memory_space=pltpu.SMEM)]
        + [pl.BlockSpec(memory_space=pltpu.VMEM)] * count,
        scratch_shapes=scratch,
        compiler_params=pltpu.CompilerParams(vmem_limit_bytes=VMEM_LIMIT),
        cost_estimate=pl.CostEstimate(
            flops=2 * rows * depth * columns, bytes_accessed=2 * depth * columns, transcendentals=0
        ),
        name="expel",
    )(place, *pieces, *weights, *before)


def line_pieces(block, axis):
    far = swap(block, axis, 2)
    up = lax.ppermute(block, axis, [(i, i + 1) for i in range(3)])
    down = lax.ppermute(block, axis, [(i + 1, i) for i in range(3)])
    passed = lax.ppermute(far, axis, [(1, 0), (2, 3)])
    return block, up, down, passed, far


def ring_pieces(block, axis):
    before = lax.ppermute(block, axis, [(i, (i + 1) % 4) for i in range(4)])
    after = lax.ppermute(block, axis, [((i + 1) % 4, i) for i in range(4)])
    return block, before, after, swap(block, axis, 2)


def gather_line(block, axis, dim):
    count = lax.axis_size(axis)
    if count != 4:
        return lax.all_gather(block, axis, axis=dim, tiled=True)
    me = lax.axis_index(axis)
    block, before, after, far = ring_pieces(block, axis)
    size = block.shape[dim]
    shape = list(block.shape)
    shape[dim] = count * size
    out = jnp.zeros(shape, block.dtype)
    for piece, place in ((block, me), (before, (me + 3) % 4), (after, (me + 1) % 4), (far, me ^ 2)):
        out = lax.dynamic_update_slice_in_dim(out, piece, place * size, dim)
    return out


def gather_pair(block, axis):
    if lax.axis_size(axis) != 2:
        return lax.all_gather(block, axis, axis=0)
    other = swap(block, axis, 1)
    first = lax.axis_index(axis) == 0
    return jnp.stack([jnp.where(first, block, other), jnp.where(first, other, block)])


def shards(
    tokens, raw_keys, raw_values, query_weight, output_weight,
    key_expand, key_mix, key_reduce, value_expand, value_mix, value_reduce,
):
    outer, inner, heads_axis = (lax.axis_size(name) for name in ("outer", "inner", "head"))
    z, y, h = (lax.axis_index(name) for name in ("outer", "inner", "head"))
    key_width, value_width = key_expand.shape[0], value_expand.shape[0]
    row_count, model = tokens.shape
    devices = outer * inner * heads_axis
    blocks = raw_keys.shape[0] // STRIDE
    context = raw_keys.shape[0] * devices - row_count * outer * inner
    part = query_weight.shape[0]
    fast = inner == 2 and outer == 4 and heads_axis == 4

    edge = jnp.concatenate([raw_keys[:STRIDE], raw_values[:STRIDE]], axis=1)
    edge = lax.ppermute(
        edge, ("outer", "inner", "head"), [(i + 1, i) for i in range(devices - 1)]
    )

    if fast:
        turned, edge = lax.optimization_barrier((output_weight.T, edge))
        out_weights = [turned, swap(turned, "inner", 1)]
    else:
        out_weights = lax.all_gather(output_weight, "inner", axis=1, tiled=True)

    seq_axes = ("outer", "inner") if fast else "outer"
    shares = outer * inner if fast else outer
    share = query_weight.shape[1] // shares

    def exchange(block):
        return lax.all_to_all(block, seq_axes, split_axis=0, concat_axis=0, tiled=True)

    if fast:
        sent = cut(query_weight, shares, 2)
    else:
        weight = exchange(
            jnp.stack([query_weight[:, i * share : (i + 1) * share] for i in range(shares)])
        )
        weight = lax.all_gather(weight, "inner", axis=1).reshape(model, share)
    heads_here = share // key_width

    if fast:
        quarter = row_count // heads_axis
        mine = lax.dynamic_slice_in_dim(tokens, h * quarter, quarter, 0)
        mine, before, after, far = ring_pieces(mine, "outer")
        begin, before, after, far, edge = lax.optimization_barrier(
            (sent[0], before, after, far, edge)
        )
        weight_first = exchange(begin)
        near = jnp.concatenate([mine, before, after, far], axis=0)
        follow, out_weights[1] = lax.optimization_barrier((near, out_weights[1]))
        beside = swap(follow, "inner", 1)
        pieces = [near, beside, swap(near, "head", 2)]
        steps = [(line, side, turn) for turn in (0, 2) for side in (0, 1) for line in range(4)]
        steps = steps + [(a, b, k ^ 1) for a, b, k in steps]
        def of_block(block, z, h):
            line, side, turn = steps[block]
            there = (z, (z + 3) & 3, (z + 1) & 3, z ^ 2)[line]
            return side, ((h ^ turn) * outer + there) * quarter

        bases = []
        for block, (_, side, _) in enumerate(steps):
            where = of_block(block, z, h)[1] // quarter
            bases.append((where % outer * inner + (y ^ side)) * row_count + where // outer * quarter)
        bases = jnp.stack(bases)[:, None] + jnp.arange(quarter)[None, :]
        layout = (quarter, inner, of_block)
    else:
        every = gather_line(tokens, "outer", 0)
        queries = [jnp.dot(every, weight, preferred_element_type=jnp.float32).astype(jnp.bfloat16)]
        bases = (jnp.arange(outer) * inner + y)[:, None] * row_count + jnp.arange(row_count)[None, :]
        layout = (row_count, 1, lambda block, z, h: (0, block * row_count))
    places = (context + bases).astype(jnp.int32).reshape(-1, 1)
    here = jnp.stack([z, h, y]).astype(jnp.int32)

    edge_keys, edge_values = edge[:, : raw_keys.shape[1]], edge[:, raw_keys.shape[1] :]
    packed = compress(
        raw_keys, raw_values, edge_keys, edge_values,
        key_expand, key_mix, key_reduce, value_expand, value_mix, value_reduce,
    )
    ids = np.arange(devices * blocks).reshape(outer, inner, heads_axis, blocks)
    if fast:
        stay = lax.dynamic_index_in_dim(packed, h, 0, False)
        away = [lax.dynamic_index_in_dim(packed, h ^ step, 0, False) for step in (1, 2, 3)]
        came = [swap(piece, "head", step) for step, piece in zip((1, 2, 3), away)]
        packed = jnp.concatenate([stay, *came], axis=0)
        bound = np.broadcast_to(ids.max(axis=(2, 3), keepdims=True), ids.shape)
    else:
        packed = jnp.broadcast_to(packed[:, None], (G, heads_axis // G, *packed.shape[1:]))
        packed = packed.reshape(heads_axis, blocks, -1)
        packed = lax.all_to_all(packed, "head", split_axis=0, concat_axis=0, tiled=True)
        packed = packed.reshape(heads_axis * blocks, -1)
        bound = ids
    if fast:
        packed = list(ring_pieces(packed, "outer"))
        first = swap(packed[0], "inner", 1)
        begin, rest, pieces, first = lax.optimization_barrier((sent[1], packed[1:], pieces, first))
        packed = [packed[0], *rest]
        packed += [first, *(swap(piece, "inner", 1) for piece in rest)]
        pieces.append(swap(pieces[1], "head", 2))
        packed, late = lax.optimization_barrier((packed, pieces[3]))
        partners = [swap(piece, "head", 1) for piece in (*pieces[:3], late)]
        queries = [project([*pieces, *partners], [weight_first, exchange(begin)])]

        def starts(index, z, y):
            return (y ^ (index // 4)) * 4 + (z, (z + 3) & 3, (z + 1) & 3, z ^ 2)[index % 4]

    else:
        packed = gather_line(packed, "outer", 0)
        packed = [gather_pair(packed, "inner").reshape(devices * blocks, -1)]

        def starts(index, z, y):
            return 0

    bound = (STRIDE * bound + BLK - 1).transpose(1, 0, 2, 3).reshape(-1)
    hidden = [bool((bound[i : i + LANES] > context).any()) for i in range(0, len(bound), LANES)]
    masked, start = [], 0
    for i in range(1, len(hidden) + 1):
        if i == len(hidden) or hidden[i] != hidden[start]:
            masked.append((start * LANES, min(i * LANES, len(bound)), hidden[start]))
            start = i
    if fast:
        column = np.arange(heads_axis)[None, None, :, None]
        ids = ids[:, :, :1] + (column ^ h) * blocks
        limits = (STRIDE * ids + BLK - 1).transpose(1, 0, 2, 3).reshape(1, -1).astype(jnp.int32)
    else:
        limits = (STRIDE * ids + BLK - 1).transpose(1, 0, 2, 3).reshape(1, -1)
        limits = jnp.asarray(limits, jnp.int32)

    total = None
    for head in range(heads_here):
        attended = attend(
            here, queries, head, packed, starts, limits, places, key_width, masked, layout
        )
        if fast:
            last = head == heads_here - 1
            block = jnp.concatenate([attended[0], swap(attended[1], "inner", 1)], axis=1)
            total = expel(
                here, line_pieces(block, "outer"), out_weights, [] if total is None else [total],
                head, heads_here, (heads_axis, quarter) if last else None,
            )
        else:
            attended = gather_line(attended[0], "outer", 1)
            rows = out_weights.reshape(outer, heads_here, value_width, -1)[:, head]
            product = jnp.dot(
                attended, rows.reshape(outer * value_width, -1), preferred_element_type=jnp.float32
            )
            total = product if total is None else total + product

    if fast:
        keep, send = total
        columns = keep.shape[-1]
        total = keep + swap(send, "head", 1).astype(jnp.float32)
        x = h // 2
        keep = lax.dynamic_index_in_dim(total, x, 1, False)
        send = lax.dynamic_index_in_dim(total, 1 - x, 1, False).astype(jnp.bfloat16)
        total = keep + swap(send, "head", 2).astype(jnp.float32)
        result = total.astype(jnp.bfloat16).reshape(row_count, columns)
        first, second = result[:, : columns // 2], result[:, columns // 2 :]
        result = jnp.concatenate(
            [jnp.where(y == 0, first, second), jnp.where(y == 0, second, first)], axis=1
        )
        route = [
            ((a * inner + b) * heads_axis + k, (k * inner + b) * heads_axis + a)
            for a in range(outer) for b in range(inner) for k in range(heads_axis)
        ]
        return lax.ppermute(result, ("outer", "inner", "head"), route)
    columns = total.shape[1]
    total = lax.psum_scatter(total, "head", scatter_dimension=0, tiled=True).astype(jnp.bfloat16)
    total = lax.all_gather(total, "head", axis=0, tiled=True)
    total = lax.all_to_all(
        total.reshape(outer, row_count, columns), "outer", split_axis=0, concat_axis=0, tiled=True
    )
    total = total.transpose(1, 0, 2).reshape(row_count, model)
    return lax.dynamic_slice_in_dim(total, h * (model // heads_axis), model // heads_axis, 1)


def solution(mesh):
    seq_count, head_count = mesh.shape["seq"], mesh.shape["head"]
    inner = seq_count // OUTER
    finer = Mesh(
        mesh.devices.reshape(OUTER, inner, head_count), ("outer", "inner", "head")
    )
    seq = ("outer", "inner")
    in_specs = (
        P(seq, None),
        P((*seq, "head"), None),
        P((*seq, "head"), None),
        P(seq, "head"),
        P("head", seq),
        P(), P(), P(), P(), P(), P(),
    )
    return jax.shard_map(
        shards, mesh=finer, in_specs=in_specs, out_specs=P(seq, "head"), check_vma=False
    )
```

```python
import jax
import jax.numpy as jnp
import numpy as np
from jax import lax
from jax.experimental import pallas as pl
from jax.experimental.pallas import tpu as pltpu
from jax.sharding import Mesh
from jax.sharding import PartitionSpec as P

G = 4
BLK = 32
STRIDE = 16
LANES = 128
OUTER = 4
VMEM_LIMIT = 20 * 1024 * 1024


def round_up(value, unit):
    return -(-value // unit) * unit


def swap(block, axis, bit):
    return lax.ppermute(block, axis, [(i, i ^ bit) for i in range(lax.axis_size(axis))])


def window_of(group, width):
    low = group * width // LANES * LANES
    return low, round_up((group + 1) * width, LANES) - low, group * width - low


def compress_one(raw_ref, edge_ref, expand_ref, mix_ref, reduce_ref, sorted_ref, hidden_ref, groups):
    width, units = expand_ref.shape
    tokens = raw_ref.shape[0]
    rows = 8 * STRIDE
    chunks = tokens // rows
    blocks = tokens // STRIDE
    to = lax.broadcasted_iota(jnp.int32, (rows, rows), 0)
    come = lax.broadcasted_iota(jnp.int32, (rows, rows), 1)
    order = (come == (to % 8) * STRIDE + to // 8).astype(jnp.bfloat16)
    for chunk in range(chunks):
        piece = slice(chunk * rows, (chunk + 1) * rows)
        sorted_ref[piece, :] = jnp.dot(
            order, raw_ref[piece, :], preferred_element_type=jnp.float32
        ).astype(jnp.bfloat16)
    tile = 256 if units % 256 == 0 else units
    for group in range(groups):
        low, span, offset = window_of(group, width)
        parts = []
        if offset:
            parts.append(jnp.zeros((offset, units), jnp.bfloat16))
        parts.append(expand_ref[...])
        if span - offset - width:
            parts.append(jnp.zeros((span - offset - width, units), jnp.bfloat16))
        expand = jnp.concatenate(parts, axis=0) if len(parts) > 1 else parts[0]
        for start in range(0, units, tile):
            lanes = slice(start, start + tile)
            weight = expand[:, lanes]
            projected = jnp.dot(
                sorted_ref[:, low : low + span], weight, preferred_element_type=jnp.float32
            ).reshape(chunks, STRIDE, 8, tile)
            mix_low = mix_ref[:STRIDE, lanes][None, :, None, :]
            mix_high = mix_ref[STRIDE:, lanes]
            first = jnp.sum(projected * mix_low, axis=1).reshape(blocks, tile)
            second = jnp.sum(projected * mix_high[None, :, None, :], axis=1).reshape(blocks, tile)
            edge = jnp.dot(edge_ref[:, low : low + span], weight, preferred_element_type=jnp.float32)
            edge = jnp.sum(edge * mix_high, axis=0, keepdims=True)
            hidden = first + jnp.concatenate([second[1:], edge], axis=0)
            half = 0.5 * hidden
            activated = half + half * lax.erf(hidden * np.float32(2.0**-0.5))
            hidden_ref[group * blocks : (group + 1) * blocks, lanes] = activated.astype(jnp.bfloat16)
    return jnp.dot(hidden_ref[...], reduce_ref[...], preferred_element_type=jnp.float32).astype(
        jnp.bfloat16
    )


def compress_kernel(
    raw_keys, raw_values, edge_keys, edge_values, key_expand, key_mix, key_reduce,
    value_expand, value_mix, value_reduce, packed, sorted_keys, sorted_values, hidden,
):
    groups, blocks, _ = packed.shape
    key_width = key_expand.shape[0]
    value_start = round_up(key_width, LANES)
    keys = compress_one(
        raw_keys, edge_keys, key_expand, key_mix, key_reduce, sorted_keys, hidden, groups
    )
    values = compress_one(
        raw_values, edge_values, value_expand, value_mix, value_reduce, sorted_values, hidden, groups
    )
    for group in range(groups):
        rows = slice(group * blocks, (group + 1) * blocks)
        packed[group, :, :key_width] = keys[rows]
        packed[group, :, key_width:value_start] = jnp.zeros(
            (blocks, value_start - key_width), jnp.bfloat16
        )
        packed[group, :, value_start:] = values[rows]


def compress(raw_keys, raw_values, edge_keys, edge_values, *weights):
    key_expand, _, _, value_expand, _, _ = weights
    units = key_expand.shape[1]
    tokens = raw_keys.shape[0]
    blocks = tokens // STRIDE
    width = round_up(key_expand.shape[0], LANES) + value_expand.shape[0]
    flops = 2 * tokens * units * (raw_keys.shape[1] + raw_values.shape[1])
    return pl.pallas_call(
        compress_kernel,
        out_shape=jax.ShapeDtypeStruct((G, blocks, width), jnp.bfloat16),
        scratch_shapes=[
            pltpu.VMEM(raw_keys.shape, jnp.bfloat16),
            pltpu.VMEM(raw_values.shape, jnp.bfloat16),
            pltpu.VMEM((G * blocks, units), jnp.bfloat16),
        ],
        compiler_params=pltpu.CompilerParams(vmem_limit_bytes=56 * 1024 * 1024),
        cost_estimate=pl.CostEstimate(
            flops=flops, bytes_accessed=2 * raw_keys.size, transcendentals=0
        ),
        name="compress",
    )(raw_keys, raw_values, edge_keys, edge_values, *weights)


def cut(weight, shares, parts):
    rows, columns = weight.shape
    share, part = columns // shares, rows // parts

    def kernel(in_ref, *out_refs):
        for index, out_ref in enumerate(out_refs):
            out_ref[0] = in_ref[index * part : (index + 1) * part, :]

    return pl.pallas_call(
        kernel,
        out_shape=(jax.ShapeDtypeStruct((shares, part, share), weight.dtype),) * parts,
        grid=(shares,),
        in_specs=[pl.BlockSpec((rows, share), lambda i: (0, i))],
        out_specs=(pl.BlockSpec((1, part, share), lambda i: (i, 0, 0)),) * parts,
        cost_estimate=pl.CostEstimate(flops=0, bytes_accessed=0, transcendentals=0),
        name="cut",
    )(weight)


def project(pieces, weights):
    part, depth = pieces[0].shape
    rows = part * len(pieces)
    shares, share, columns = weights[0].shape
    group = len(pieces) // 2
    count = len(pieces)

    def kernel(*refs):
        piece_refs, weight_refs = refs[:count], refs[count : count + len(weights)]
        out_ref, rows_ref, weight_ref, sems = refs[count + len(weights) :]
        copies = [
            pltpu.make_async_copy(
                piece, rows_ref.at[index * part : (index + 1) * part], sems.at[index]
            )
            for index, piece in enumerate(piece_refs)
        ]
        bring = []
        for index, weight in enumerate(weight_refs):
            for owner in range(shares):
                start = (owner * len(weights) + index) * share
                bring.append(
                    pltpu.make_async_copy(
                        weight.at[owner], weight_ref.at[start : start + share],
                        sems.at[count + len(bring)],
                    )
                )
        for copy in bring + copies:
            copy.start()
        for copy in bring:
            copy.wait()
        for start in range(0, count, group):
            for copy in copies[start : start + group]:
                copy.wait()
            place = slice(start * part, (start + group) * part)
            out_ref[place, :] = jnp.dot(
                rows_ref[place, :], weight_ref[...], preferred_element_type=jnp.float32
            ).astype(jnp.bfloat16)

    return pl.pallas_call(
        kernel,
        out_shape=jax.ShapeDtypeStruct((rows, columns), jnp.bfloat16),
        in_specs=[pl.BlockSpec(memory_space=pl.ANY)] * (count + len(weights)),
        scratch_shapes=[
            pltpu.VMEM((rows, depth), jnp.bfloat16),
            pltpu.VMEM((depth, columns), jnp.bfloat16),
            pltpu.SemaphoreType.DMA((count + len(weights) * shares,)),
        ],
        compiler_params=pltpu.CompilerParams(vmem_limit_bytes=VMEM_LIMIT),
        cost_estimate=pl.CostEstimate(
            flops=2 * rows * depth * columns, bytes_accessed=2 * rows * depth, transcendentals=0
        ),
        name="project",
    )(*pieces, *weights)


def attend(here, queries, head, packed, limits, places, key_width, masked, layout):
    rows_each = queries[0].shape[0]
    rows = rows_each * len(queries)
    value_start = round_up(key_width, LANES)
    value_width = packed.shape[1] - value_start
    columns = packed.shape[0]
    factor = np.float32(key_width**-0.5 * np.log2(np.e))
    tile = min(256, rows_each)
    unit, outputs, sends = layout

    def kernel(here_ref, *refs):
        query_refs = refs[: len(queries)]
        kv_ref, limit_ref, place_ref = refs[len(queries) : len(queries) + 3]
        out_refs = refs[len(queries) + 3 :]
        keys = kv_ref[:, :key_width]
        values = kv_ref[:, value_start:]
        for start in range(0, rows, tile):
            from_ref, at = query_refs[start // rows_each], start % rows_each
            query = from_ref[at : at + tile, head * key_width : (head + 1) * key_width]
            scores = lax.dot_general(
                query, keys, (((1,), (1,)), ((), ())), preferred_element_type=jnp.float32
            )
            pieces = []
            for low, high, hide in masked:
                piece = scores[:, low:high]
                if hide:
                    visible = limit_ref[:, low:high] <= place_ref[start : start + tile, :]
                    piece = jnp.where(visible, piece, -jnp.inf)
                pieces.append(piece)
            scores = jnp.concatenate(pieces, axis=1) if len(pieces) > 1 else pieces[0]
            top = jnp.max(scores, axis=1, keepdims=True)
            exponent = jnp.exp2((scores - top) * factor)
            total = jnp.sum(exponent, axis=1, keepdims=True)
            numerator = jnp.dot(
                exponent.astype(jnp.bfloat16), values, preferred_element_type=jnp.float32
            )
            done = (numerator / total).astype(jnp.bfloat16)
            for low in range(0, tile, unit):
                which, where = sends((start + low) // unit, here_ref[0], here_ref[1])
                if not isinstance(where, int):
                    where = pl.multiple_of(where, unit)
                out_refs[which][pl.ds(where, unit), :] = done[low : low + unit]

    shape = jax.ShapeDtypeStruct((rows // outputs, value_width), jnp.bfloat16)
    return pl.pallas_call(
        kernel,
        out_shape=(shape,) * outputs,
        in_specs=[pl.BlockSpec(memory_space=pltpu.SMEM)]
        + [pl.BlockSpec(memory_space=pltpu.VMEM)] * (len(queries) + 3),
        compiler_params=pltpu.CompilerParams(vmem_limit_bytes=VMEM_LIMIT),
        cost_estimate=pl.CostEstimate(
            flops=2 * rows * columns * (key_width + value_width),
            bytes_accessed=2 * packed.size,
            transcendentals=0,
        ),
        name="attend",
    )(here, *queries, packed, limits, places)


def expel(place, pieces, weights, before, chunk, chunks, shape):
    rows, width = pieces[0].shape
    depth, step, single = 4 * width, weights[0].shape[0], width // 2
    last = shape is not None

    def kernel(place_ref, *refs):
        own, up, down, passed, far = refs[:5]
        weight_refs = refs[5 : 5 + len(weights)]
        rest = refs[5 + len(weights) :]
        before_refs, outs = rest[: len(before)], rest[len(before) :]
        z, core, y = place_ref[0], place_ref[1] & 1, place_ref[2]
        lower = jnp.where(z == 0, passed[...], up[...])
        upper = jnp.where(z == 3, passed[...], down[...])
        for side, weight in enumerate(weight_refs):
            lanes = slice(side * step, (side + 1) * step)
            total = before_refs[0][:, lanes] if before else None
            for block, at in (
                (own[...], z), (lower, (z + 3) & 3), (upper, (z + 1) & 3), (far[...], z ^ 2)
            ):
                starts = [((at * 2 + inner) * chunks + chunk) * single for inner in (y, 1 - y)]
                both = [weight[:, pl.ds(pl.multiple_of(start, single), single)] for start in starts]
                product = lax.dot_general(
                    block, jnp.concatenate(both, axis=1), (((1,), (1,)), ((), ())),
                    preferred_element_type=jnp.float32,
                )
                total = product if total is None else total + product
            if not last:
                outs[0][:, lanes] = total
                continue
            keep_ref, send_ref, hold_ref = outs
            hold_ref[...] = total.reshape(hold_ref.shape)
            keep_ref[:, :, :, lanes] = hold_ref[:, :, pl.ds(core, 1)][:, :, 0]
            send_ref[:, :, :, lanes] = hold_ref[:, :, pl.ds(1 - core, 1)][:, :, 0].astype(jnp.bfloat16)

    columns = step * len(weights)
    if last:
        groups, quarter = shape
        out_shape = (
            jax.ShapeDtypeStruct((groups, 2, quarter, columns), jnp.float32),
            jax.ShapeDtypeStruct((groups, 2, quarter, columns), jnp.bfloat16),
        )
        scratch = [pltpu.VMEM((groups, 2, 2, quarter, step), jnp.float32)]
    else:
        out_shape, scratch = jax.ShapeDtypeStruct((rows, columns), jnp.float32), []
    count = len(pieces) + len(weights) + len(before)
    return pl.pallas_call(
        kernel,
        out_shape=out_shape,
        in_specs=[pl.BlockSpec(memory_space=pltpu.SMEM)]
        + [pl.BlockSpec(memory_space=pltpu.VMEM)] * count,
        scratch_shapes=scratch,
        compiler_params=pltpu.CompilerParams(vmem_limit_bytes=VMEM_LIMIT),
        cost_estimate=pl.CostEstimate(
            flops=2 * rows * depth * columns, bytes_accessed=2 * depth * columns, transcendentals=0
        ),
        name="expel",
    )(place, *pieces, *weights, *before)


def line_pieces(block, axis):
    far = swap(block, axis, 2)
    up = lax.ppermute(block, axis, [(i, i + 1) for i in range(3)])
    down = lax.ppermute(block, axis, [(i + 1, i) for i in range(3)])
    passed = lax.ppermute(far, axis, [(1, 0), (2, 3)])
    return block, up, down, passed, far


def ring_pieces(block, axis):
    before = lax.ppermute(block, axis, [(i, (i + 1) % 4) for i in range(4)])
    after = lax.ppermute(block, axis, [((i + 1) % 4, i) for i in range(4)])
    return block, before, after, swap(block, axis, 2)


def gather_line(block, axis, dim):
    count = lax.axis_size(axis)
    if count != 4:
        return lax.all_gather(block, axis, axis=dim, tiled=True)
    me = lax.axis_index(axis)
    block, before, after, far = ring_pieces(block, axis)
    size = block.shape[dim]
    shape = list(block.shape)
    shape[dim] = count * size
    out = jnp.zeros(shape, block.dtype)
    for piece, place in ((block, me), (before, (me + 3) % 4), (after, (me + 1) % 4), (far, me ^ 2)):
        out = lax.dynamic_update_slice_in_dim(out, piece, place * size, dim)
    return out


def gather_pair(block, axis):
    if lax.axis_size(axis) != 2:
        return lax.all_gather(block, axis, axis=0)
    other = swap(block, axis, 1)
    first = lax.axis_index(axis) == 0
    return jnp.stack([jnp.where(first, block, other), jnp.where(first, other, block)])


def shards(
    tokens, raw_keys, raw_values, query_weight, output_weight,
    key_expand, key_mix, key_reduce, value_expand, value_mix, value_reduce,
):
    outer, inner, heads_axis = (lax.axis_size(name) for name in ("outer", "inner", "head"))
    z, y, h = (lax.axis_index(name) for name in ("outer", "inner", "head"))
    key_width, value_width = key_expand.shape[0], value_expand.shape[0]
    row_count, model = tokens.shape
    devices = outer * inner * heads_axis
    blocks = raw_keys.shape[0] // STRIDE
    context = raw_keys.shape[0] * devices - row_count * outer * inner
    part = query_weight.shape[0]
    fast = inner == 2 and outer == 4 and heads_axis == 4

    edge = jnp.concatenate([raw_keys[:STRIDE], raw_values[:STRIDE]], axis=1)
    edge = lax.ppermute(
        edge, ("outer", "inner", "head"), [(i + 1, i) for i in range(devices - 1)]
    )

    if fast:
        turned, edge = lax.optimization_barrier((output_weight.T, edge))
        out_weights = [turned, swap(turned, "inner", 1)]
    else:
        out_weights = lax.all_gather(output_weight, "inner", axis=1, tiled=True)

    seq_axes = ("outer", "inner") if fast else "outer"
    shares = outer * inner if fast else outer
    share = query_weight.shape[1] // shares

    def exchange(block):
        return lax.all_to_all(block, seq_axes, split_axis=0, concat_axis=0, tiled=True)

    if fast:
        sent = cut(query_weight, shares, 2)
    else:
        weight = exchange(
            jnp.stack([query_weight[:, i * share : (i + 1) * share] for i in range(shares)])
        )
        weight = lax.all_gather(weight, "inner", axis=1).reshape(model, share)
    heads_here = share // key_width

    if fast:
        quarter = row_count // heads_axis
        mine = lax.dynamic_slice_in_dim(tokens, h * quarter, quarter, 0)
        mine, before, after, far = ring_pieces(mine, "outer")
        begin, before, edge = lax.optimization_barrier((sent[0], before, edge))
        weight_first = exchange(begin)
        near = jnp.concatenate([mine, before, after, far], axis=0)
        beside = swap(near, "inner", 1)
        pieces = [near, beside, swap(near, "head", 2)]
        steps = [(line, side, turn) for turn in (0, 2) for side in (0, 1) for line in range(4)]
        steps = steps + [(a, b, k ^ 1) for a, b, k in steps]
        def of_block(block, z, h):
            line, side, turn = steps[block]
            there = (z, (z + 3) & 3, (z + 1) & 3, z ^ 2)[line]
            return side, ((h ^ turn) * outer + there) * quarter

        bases = []
        for block, (_, side, _) in enumerate(steps):
            where = of_block(block, z, h)[1] // quarter
            bases.append((where % outer * inner + (y ^ side)) * row_count + where // outer * quarter)
        bases = jnp.stack(bases)[:, None] + jnp.arange(quarter)[None, :]
        layout = (quarter, inner, of_block)
    else:
        every = gather_line(tokens, "outer", 0)
        queries = [jnp.dot(every, weight, preferred_element_type=jnp.float32).astype(jnp.bfloat16)]
        bases = (jnp.arange(outer) * inner + y)[:, None] * row_count + jnp.arange(row_count)[None, :]
        layout = (row_count, 1, lambda block, z, h: (0, block * row_count))
    places = (context + bases).astype(jnp.int32).reshape(-1, 1)
    here = jnp.stack([z, h, y]).astype(jnp.int32)

    edge_keys, edge_values = edge[:, : raw_keys.shape[1]], edge[:, raw_keys.shape[1] :]
    packed = compress(
        raw_keys, raw_values, edge_keys, edge_values,
        key_expand, key_mix, key_reduce, value_expand, value_mix, value_reduce,
    )
    ids = np.arange(devices * blocks).reshape(outer, inner, heads_axis, blocks)
    if fast:
        stay = lax.dynamic_index_in_dim(packed, h, 0, False)
        away = [lax.dynamic_index_in_dim(packed, h ^ step, 0, False) for step in (1, 2, 3)]
        came = [swap(piece, "head", step) for step, piece in zip((1, 2, 3), away)]
        packed = jnp.concatenate([stay, *came], axis=0)
        bound = np.broadcast_to(ids.max(axis=(2, 3), keepdims=True), ids.shape)
    else:
        packed = jnp.broadcast_to(packed[:, None], (G, heads_axis // G, *packed.shape[1:]))
        packed = packed.reshape(heads_axis, blocks, -1)
        packed = lax.all_to_all(packed, "head", split_axis=0, concat_axis=0, tiled=True)
        packed = packed.reshape(heads_axis * blocks, -1)
        bound = ids
    if fast:
        packed, out_weights[1] = lax.optimization_barrier((packed, out_weights[1]))
    packed = gather_line(packed, "outer", 0)
    if fast:
        begin, packed, pieces = lax.optimization_barrier((sent[1], packed, pieces))
        pieces.append(swap(pieces[1], "head", 2))
        partners = [swap(piece, "head", 1) for piece in pieces]
        queries = [project([*pieces, *partners], [weight_first, exchange(begin)])]
    packed = gather_pair(packed, "inner").reshape(devices * blocks, -1)
    bound = (STRIDE * bound + BLK - 1).transpose(1, 0, 2, 3).reshape(-1)
    hidden = [bool((bound[i : i + LANES] > context).any()) for i in range(0, len(bound), LANES)]
    masked, start = [], 0
    for i in range(1, len(hidden) + 1):
        if i == len(hidden) or hidden[i] != hidden[start]:
            masked.append((start * LANES, min(i * LANES, len(bound)), hidden[start]))
            start = i
    if fast:
        column = np.arange(heads_axis)[None, None, :, None]
        ids = ids[:, :, :1] + (column ^ h) * blocks
        limits = (STRIDE * ids + BLK - 1).transpose(1, 0, 2, 3).reshape(1, -1).astype(jnp.int32)
    else:
        limits = (STRIDE * ids + BLK - 1).transpose(1, 0, 2, 3).reshape(1, -1)
        limits = jnp.asarray(limits, jnp.int32)

    total = None
    for head in range(heads_here):
        attended = attend(
            here, queries, head, packed, limits, places, key_width, masked, layout
        )
        if fast:
            last = head == heads_here - 1
            block = jnp.concatenate([attended[0], swap(attended[1], "inner", 1)], axis=1)
            total = expel(
                here, line_pieces(block, "outer"), out_weights, [] if total is None else [total],
                head, heads_here, (heads_axis, quarter) if last else None,
            )
        else:
            attended = gather_line(attended[0], "outer", 1)
            rows = out_weights.reshape(outer, heads_here, value_width, -1)[:, head]
            product = jnp.dot(
                attended, rows.reshape(outer * value_width, -1), preferred_element_type=jnp.float32
            )
            total = product if total is None else total + product

    if fast:
        keep, send = total
        columns = keep.shape[-1]
        total = keep + swap(send, "head", 1).astype(jnp.float32)
        x = h // 2
        keep = lax.dynamic_index_in_dim(total, x, 1, False)
        send = lax.dynamic_index_in_dim(total, 1 - x, 1, False).astype(jnp.bfloat16)
        total = keep + swap(send, "head", 2).astype(jnp.float32)
        result = total.astype(jnp.bfloat16).reshape(row_count, columns)
        first, second = result[:, : columns // 2], result[:, columns // 2 :]
        result = jnp.concatenate(
            [jnp.where(y == 0, first, second), jnp.where(y == 0, second, first)], axis=1
        )
        route = [
            ((a * inner + b) * heads_axis + k, (k * inner + b) * heads_axis + a)
            for a in range(outer) for b in range(inner) for k in range(heads_axis)
        ]
        return lax.ppermute(result, ("outer", "inner", "head"), route)
    columns = total.shape[1]
    total = lax.psum_scatter(total, "head", scatter_dimension=0, tiled=True).astype(jnp.bfloat16)
    total = lax.all_gather(total, "head", axis=0, tiled=True)
    total = lax.all_to_all(
        total.reshape(outer, row_count, columns), "outer", split_axis=0, concat_axis=0, tiled=True
    )
    total = total.transpose(1, 0, 2).reshape(row_count, model)
    return lax.dynamic_slice_in_dim(total, h * (model // heads_axis), model // heads_axis, 1)


def solution(mesh):
    seq_count, head_count = mesh.shape["seq"], mesh.shape["head"]
    inner = seq_count // OUTER
    finer = Mesh(
        mesh.devices.reshape(OUTER, inner, head_count), ("outer", "inner", "head")
    )
    seq = ("outer", "inner")
    in_specs = (
        P(seq, None),
        P((*seq, "head"), None),
        P((*seq, "head"), None),
        P(seq, "head"),
        P("head", seq),
        P(), P(), P(), P(), P(), P(),
    )
    return jax.shard_map(
        shards, mesh=finer, in_specs=in_specs, out_specs=P(seq, "head"), check_vma=False
    )
```

```python
import jax
import jax.numpy as jnp
import numpy as np
from jax import lax
from jax.experimental import pallas as pl
from jax.experimental.pallas import tpu as pltpu
from jax.sharding import Mesh
from jax.sharding import PartitionSpec as P

G = 4
BLK = 32
STRIDE = 16
LANES = 128
OUTER = 4
VMEM_LIMIT = 20 * 1024 * 1024


def round_up(value, unit):
    return -(-value // unit) * unit


def swap(block, axis, bit):
    return lax.ppermute(block, axis, [(i, i ^ bit) for i in range(lax.axis_size(axis))])


def window_of(group, width):
    low = group * width // LANES * LANES
    return low, round_up((group + 1) * width, LANES) - low, group * width - low


def compress_one(raw_ref, edge_ref, expand_ref, mix_ref, reduce_ref, sorted_ref, hidden_ref, groups):
    width, units = expand_ref.shape
    tokens = raw_ref.shape[0]
    rows = 8 * STRIDE
    chunks = tokens // rows
    blocks = tokens // STRIDE
    to = lax.broadcasted_iota(jnp.int32, (rows, rows), 0)
    come = lax.broadcasted_iota(jnp.int32, (rows, rows), 1)
    order = (come == (to % 8) * STRIDE + to // 8).astype(jnp.bfloat16)
    for chunk in range(chunks):
        piece = slice(chunk * rows, (chunk + 1) * rows)
        sorted_ref[piece, :] = jnp.dot(
            order, raw_ref[piece, :], preferred_element_type=jnp.float32
        ).astype(jnp.bfloat16)
    tile = 256 if units % 256 == 0 else units
    for group in range(groups):
        low, span, offset = window_of(group, width)
        parts = []
        if offset:
            parts.append(jnp.zeros((offset, units), jnp.bfloat16))
        parts.append(expand_ref[...])
        if span - offset - width:
            parts.append(jnp.zeros((span - offset - width, units), jnp.bfloat16))
        expand = jnp.concatenate(parts, axis=0) if len(parts) > 1 else parts[0]
        for start in range(0, units, tile):
            lanes = slice(start, start + tile)
            weight = expand[:, lanes]
            projected = jnp.dot(
                sorted_ref[:, low : low + span], weight, preferred_element_type=jnp.float32
            ).reshape(chunks, STRIDE, 8, tile)
            mix_low = mix_ref[:STRIDE, lanes][None, :, None, :]
            mix_high = mix_ref[STRIDE:, lanes]
            first = jnp.sum(projected * mix_low, axis=1).reshape(blocks, tile)
            second = jnp.sum(projected * mix_high[None, :, None, :], axis=1).reshape(blocks, tile)
            edge = jnp.dot(edge_ref[:, low : low + span], weight, preferred_element_type=jnp.float32)
            edge = jnp.sum(edge * mix_high, axis=0, keepdims=True)
            hidden = first + jnp.concatenate([second[1:], edge], axis=0)
            half = 0.5 * hidden
            activated = half + half * lax.erf(hidden * np.float32(2.0**-0.5))
            hidden_ref[group * blocks : (group + 1) * blocks, lanes] = activated.astype(jnp.bfloat16)
    return jnp.dot(hidden_ref[...], reduce_ref[...], preferred_element_type=jnp.float32).astype(
        jnp.bfloat16
    )


def compress_kernel(
    raw_keys, raw_values, edge_keys, edge_values, key_expand, key_mix, key_reduce,
    value_expand, value_mix, value_reduce, packed, sorted_keys, sorted_values, hidden,
):
    groups, blocks, _ = packed.shape
    key_width = key_expand.shape[0]
    value_start = round_up(key_width, LANES)
    keys = compress_one(
        raw_keys, edge_keys, key_expand, key_mix, key_reduce, sorted_keys, hidden, groups
    )
    values = compress_one(
        raw_values, edge_values, value_expand, value_mix, value_reduce, sorted_values, hidden, groups
    )
    for group in range(groups):
        rows = slice(group * blocks, (group + 1) * blocks)
        packed[group, :, :key_width] = keys[rows]
        packed[group, :, key_width:value_start] = jnp.zeros(
            (blocks, value_start - key_width), jnp.bfloat16
        )
        packed[group, :, value_start:] = values[rows]


def compress(raw_keys, raw_values, edge_keys, edge_values, *weights):
    key_expand, _, _, value_expand, _, _ = weights
    units = key_expand.shape[1]
    tokens = raw_keys.shape[0]
    blocks = tokens // STRIDE
    width = round_up(key_expand.shape[0], LANES) + value_expand.shape[0]
    flops = 2 * tokens * units * (raw_keys.shape[1] + raw_values.shape[1])
    return pl.pallas_call(
        compress_kernel,
        out_shape=jax.ShapeDtypeStruct((G, blocks, width), jnp.bfloat16),
        scratch_shapes=[
            pltpu.VMEM(raw_keys.shape, jnp.bfloat16),
            pltpu.VMEM(raw_values.shape, jnp.bfloat16),
            pltpu.VMEM((G * blocks, units), jnp.bfloat16),
        ],
        compiler_params=pltpu.CompilerParams(vmem_limit_bytes=56 * 1024 * 1024),
        cost_estimate=pl.CostEstimate(
            flops=flops, bytes_accessed=2 * raw_keys.size, transcendentals=0
        ),
        name="compress",
    )(raw_keys, raw_values, edge_keys, edge_values, *weights)


def cut(weight, shares, parts):
    rows, columns = weight.shape
    share, part = columns // shares, rows // parts

    def kernel(in_ref, *out_refs):
        for index, out_ref in enumerate(out_refs):
            out_ref[0] = in_ref[index * part : (index + 1) * part, :]

    return pl.pallas_call(
        kernel,
        out_shape=(jax.ShapeDtypeStruct((shares, part, share), weight.dtype),) * parts,
        grid=(shares,),
        in_specs=[pl.BlockSpec((rows, share), lambda i: (0, i))],
        out_specs=(pl.BlockSpec((1, part, share), lambda i: (i, 0, 0)),) * parts,
        cost_estimate=pl.CostEstimate(flops=0, bytes_accessed=0, transcendentals=0),
        name="cut",
    )(weight)


def project(pieces, weights):
    part, depth = pieces[0].shape
    rows = part * len(pieces)
    shares, share, columns = weights[0].shape
    group = len(pieces) // 2
    count = len(pieces)

    def kernel(*refs):
        piece_refs, weight_refs = refs[:count], refs[count : count + len(weights)]
        out_ref, rows_ref, weight_ref, sems = refs[count + len(weights) :]
        copies = [
            pltpu.make_async_copy(
                piece, rows_ref.at[index * part : (index + 1) * part], sems.at[index]
            )
            for index, piece in enumerate(piece_refs)
        ]
        bring = []
        for index, weight in enumerate(weight_refs):
            for owner in range(shares):
                start = (owner * len(weights) + index) * share
                bring.append(
                    pltpu.make_async_copy(
                        weight.at[owner], weight_ref.at[start : start + share],
                        sems.at[count + len(bring)],
                    )
                )
        for copy in bring + copies:
            copy.start()
        for copy in bring:
            copy.wait()
        for start in range(0, count, group):
            for copy in copies[start : start + group]:
                copy.wait()
            place = slice(start * part, (start + group) * part)
            out_ref[place, :] = jnp.dot(
                rows_ref[place, :], weight_ref[...], preferred_element_type=jnp.float32
            ).astype(jnp.bfloat16)

    return pl.pallas_call(
        kernel,
        out_shape=jax.ShapeDtypeStruct((rows, columns), jnp.bfloat16),
        in_specs=[pl.BlockSpec(memory_space=pl.ANY)] * (count + len(weights)),
        scratch_shapes=[
            pltpu.VMEM((rows, depth), jnp.bfloat16),
            pltpu.VMEM((depth, columns), jnp.bfloat16),
            pltpu.SemaphoreType.DMA((count + len(weights) * shares,)),
        ],
        compiler_params=pltpu.CompilerParams(vmem_limit_bytes=VMEM_LIMIT),
        cost_estimate=pl.CostEstimate(
            flops=2 * rows * depth * columns, bytes_accessed=2 * rows * depth, transcendentals=0
        ),
        name="project",
    )(*pieces, *weights)


def attend(here, queries, heads, packed, limits, places, key_width, masked, layout):
    rows_each = queries[0].shape[0]
    rows = rows_each * len(queries)
    value_start = round_up(key_width, LANES)
    value_width = packed.shape[1] - value_start
    columns = packed.shape[0]
    factor = np.float32(key_width**-0.5 * np.log2(np.e))
    tile = min(256, rows_each)
    unit, outputs, sends = layout

    def kernel(here_ref, *refs):
        query_refs = refs[: len(queries)]
        kv_ref, limit_ref, place_ref = refs[len(queries) : len(queries) + 3]
        out_refs = refs[len(queries) + 3 :]
        keys = kv_ref[:, :key_width]
        values = kv_ref[:, value_start:]
        for order, start in [(o, r) for o in range(len(heads)) for r in range(0, rows, tile)]:
            head, lanes = heads[order], slice(order * value_width, (order + 1) * value_width)
            from_ref, at = query_refs[start // rows_each], start % rows_each
            query = from_ref[at : at + tile, head * key_width : (head + 1) * key_width]
            scores = lax.dot_general(
                query, keys, (((1,), (1,)), ((), ())), preferred_element_type=jnp.float32
            )
            pieces = []
            for low, high, hide in masked:
                piece = scores[:, low:high]
                if hide:
                    visible = limit_ref[:, low:high] <= place_ref[start : start + tile, :]
                    piece = jnp.where(visible, piece, -jnp.inf)
                pieces.append(piece)
            scores = jnp.concatenate(pieces, axis=1) if len(pieces) > 1 else pieces[0]
            top = jnp.max(scores, axis=1, keepdims=True)
            exponent = jnp.exp2((scores - top) * factor)
            total = jnp.sum(exponent, axis=1, keepdims=True)
            numerator = jnp.dot(
                exponent.astype(jnp.bfloat16), values, preferred_element_type=jnp.float32
            )
            done = (numerator / total).astype(jnp.bfloat16)
            for low in range(0, tile, unit):
                which, where = sends((start + low) // unit, here_ref[0], here_ref[1])
                if not isinstance(where, int):
                    where = pl.multiple_of(where, unit)
                out_refs[which][pl.ds(where, unit), lanes] = done[low : low + unit]

    shape = jax.ShapeDtypeStruct((rows // outputs, len(heads) * value_width), jnp.bfloat16)
    return pl.pallas_call(
        kernel,
        out_shape=(shape,) * outputs,
        in_specs=[pl.BlockSpec(memory_space=pltpu.SMEM)]
        + [pl.BlockSpec(memory_space=pltpu.VMEM)] * (len(queries) + 3),
        compiler_params=pltpu.CompilerParams(vmem_limit_bytes=VMEM_LIMIT),
        cost_estimate=pl.CostEstimate(
            flops=2 * rows * columns * (key_width + value_width),
            bytes_accessed=2 * packed.size,
            transcendentals=0,
        ),
        name="attend",
    )(here, *queries, packed, limits, places)


def expel(place, pieces, weights, before, chunk, chunks, shape):
    rows, width = pieces[0].shape
    depth, step, single = 4 * width, weights[0].shape[0], width // 2
    last = shape is not None

    def kernel(place_ref, *refs):
        own, up, down, passed, far = refs[:5]
        weight_refs = refs[5 : 5 + len(weights)]
        rest = refs[5 + len(weights) :]
        before_refs, outs = rest[: len(before)], rest[len(before) :]
        z, core, y = place_ref[0], place_ref[1] & 1, place_ref[2]
        lower = jnp.where(z == 0, passed[...], up[...])
        upper = jnp.where(z == 3, passed[...], down[...])
        for side, weight in enumerate(weight_refs):
            lanes = slice(side * step, (side + 1) * step)
            total = before_refs[0][:, lanes] if before else None
            for block, at in (
                (own[...], z), (lower, (z + 3) & 3), (upper, (z + 1) & 3), (far[...], z ^ 2)
            ):
                starts = [((at * 2 + inner) * chunks + chunk) * single for inner in (y, 1 - y)]
                both = [weight[:, pl.ds(pl.multiple_of(start, single), single)] for start in starts]
                product = lax.dot_general(
                    block, jnp.concatenate(both, axis=1), (((1,), (1,)), ((), ())),
                    preferred_element_type=jnp.float32,
                )
                total = product if total is None else total + product
            if not last:
                outs[0][:, lanes] = total
                continue
            keep_ref, send_ref, hold_ref = outs
            hold_ref[...] = total.reshape(hold_ref.shape)
            keep_ref[:, :, :, lanes] = hold_ref[:, :, pl.ds(core, 1)][:, :, 0]
            send_ref[:, :, :, lanes] = hold_ref[:, :, pl.ds(1 - core, 1)][:, :, 0].astype(jnp.bfloat16)

    columns = step * len(weights)
    if last:
        groups, quarter = shape
        out_shape = (
            jax.ShapeDtypeStruct((groups, 2, quarter, columns), jnp.float32),
            jax.ShapeDtypeStruct((groups, 2, quarter, columns), jnp.bfloat16),
        )
        scratch = [pltpu.VMEM((groups, 2, 2, quarter, step), jnp.float32)]
    else:
        out_shape, scratch = jax.ShapeDtypeStruct((rows, columns), jnp.float32), []
    count = len(pieces) + len(weights) + len(before)
    return pl.pallas_call(
        kernel,
        out_shape=out_shape,
        in_specs=[pl.BlockSpec(memory_space=pltpu.SMEM)]
        + [pl.BlockSpec(memory_space=pltpu.VMEM)] * count,
        scratch_shapes=scratch,
        compiler_params=pltpu.CompilerParams(vmem_limit_bytes=VMEM_LIMIT),
        cost_estimate=pl.CostEstimate(
            flops=2 * rows * depth * columns, bytes_accessed=2 * depth * columns, transcendentals=0
        ),
        name="expel",
    )(place, *pieces, *weights, *before)


def line_pieces(block, axis):
    far = swap(block, axis, 2)
    up = lax.ppermute(block, axis, [(i, i + 1) for i in range(3)])
    down = lax.ppermute(block, axis, [(i + 1, i) for i in range(3)])
    passed = lax.ppermute(far, axis, [(1, 0), (2, 3)])
    return block, up, down, passed, far


def ring_pieces(block, axis):
    before = lax.ppermute(block, axis, [(i, (i + 1) % 4) for i in range(4)])
    after = lax.ppermute(block, axis, [((i + 1) % 4, i) for i in range(4)])
    return block, before, after, swap(block, axis, 2)


def gather_line(block, axis, dim):
    count = lax.axis_size(axis)
    if count != 4:
        return lax.all_gather(block, axis, axis=dim, tiled=True)
    me = lax.axis_index(axis)
    block, before, after, far = ring_pieces(block, axis)
    size = block.shape[dim]
    shape = list(block.shape)
    shape[dim] = count * size
    out = jnp.zeros(shape, block.dtype)
    for piece, place in ((block, me), (before, (me + 3) % 4), (after, (me + 1) % 4), (far, me ^ 2)):
        out = lax.dynamic_update_slice_in_dim(out, piece, place * size, dim)
    return out


def gather_pair(block, axis):
    if lax.axis_size(axis) != 2:
        return lax.all_gather(block, axis, axis=0)
    other = swap(block, axis, 1)
    first = lax.axis_index(axis) == 0
    return jnp.stack([jnp.where(first, block, other), jnp.where(first, other, block)])


def shards(
    tokens, raw_keys, raw_values, query_weight, output_weight,
    key_expand, key_mix, key_reduce, value_expand, value_mix, value_reduce,
):
    outer, inner, heads_axis = (lax.axis_size(name) for name in ("outer", "inner", "head"))
    z, y, h = (lax.axis_index(name) for name in ("outer", "inner", "head"))
    key_width, value_width = key_expand.shape[0], value_expand.shape[0]
    row_count, model = tokens.shape
    devices = outer * inner * heads_axis
    blocks = raw_keys.shape[0] // STRIDE
    context = raw_keys.shape[0] * devices - row_count * outer * inner
    part = query_weight.shape[0]
    fast = inner == 2 and outer == 4 and heads_axis == 4

    edge = jnp.concatenate([raw_keys[:STRIDE], raw_values[:STRIDE]], axis=1)
    edge = lax.ppermute(
        edge, ("outer", "inner", "head"), [(i + 1, i) for i in range(devices - 1)]
    )

    if fast:
        turned, edge = lax.optimization_barrier((output_weight.T, edge))
        out_weights = [turned, swap(turned, "inner", 1)]
    else:
        out_weights = lax.all_gather(output_weight, "inner", axis=1, tiled=True)

    seq_axes = ("outer", "inner") if fast else "outer"
    shares = outer * inner if fast else outer
    share = query_weight.shape[1] // shares

    def exchange(block):
        return lax.all_to_all(block, seq_axes, split_axis=0, concat_axis=0, tiled=True)

    if fast:
        sent = cut(query_weight, shares, 2)
    else:
        weight = exchange(
            jnp.stack([query_weight[:, i * share : (i + 1) * share] for i in range(shares)])
        )
        weight = lax.all_gather(weight, "inner", axis=1).reshape(model, share)
    heads_here = share // key_width

    if fast:
        quarter = row_count // heads_axis
        mine = lax.dynamic_slice_in_dim(tokens, h * quarter, quarter, 0)
        mine, before, after, far = ring_pieces(mine, "outer")
        begin, before, after, far, edge = lax.optimization_barrier(
            (sent[0], before, after, far, edge)
        )
        weight_first = exchange(begin)
        near = jnp.concatenate([mine, before, after, far], axis=0)
        beside = swap(near, "inner", 1)
        pieces = [near, beside, swap(near, "head", 2)]
        steps = [(line, side, turn) for turn in (0, 2) for side in (0, 1) for line in range(4)]
        steps = steps + [(a, b, k ^ 1) for a, b, k in steps]
        def of_block(block, z, h):
            line, side, turn = steps[block]
            there = (z, (z + 3) & 3, (z + 1) & 3, z ^ 2)[line]
            return side, ((h ^ turn) * outer + there) * quarter

        bases = []
        for block, (_, side, _) in enumerate(steps):
            where = of_block(block, z, h)[1] // quarter
            bases.append((where % outer * inner + (y ^ side)) * row_count + where // outer * quarter)
        bases = jnp.stack(bases)[:, None] + jnp.arange(quarter)[None, :]
        layout = (quarter, inner, of_block)
    else:
        every = gather_line(tokens, "outer", 0)
        queries = [jnp.dot(every, weight, preferred_element_type=jnp.float32).astype(jnp.bfloat16)]
        bases = (jnp.arange(outer) * inner + y)[:, None] * row_count + jnp.arange(row_count)[None, :]
        layout = (row_count, 1, lambda block, z, h: (0, block * row_count))
    places = (context + bases).astype(jnp.int32).reshape(-1, 1)
    here = jnp.stack([z, h, y]).astype(jnp.int32)

    edge_keys, edge_values = edge[:, : raw_keys.shape[1]], edge[:, raw_keys.shape[1] :]
    packed = compress(
        raw_keys, raw_values, edge_keys, edge_values,
        key_expand, key_mix, key_reduce, value_expand, value_mix, value_reduce,
    )
    ids = np.arange(devices * blocks).reshape(outer, inner, heads_axis, blocks)
    if fast:
        stay = lax.dynamic_index_in_dim(packed, h, 0, False)
        away = [lax.dynamic_index_in_dim(packed, h ^ step, 0, False) for step in (1, 2, 3)]
        came = [swap(piece, "head", step) for step, piece in zip((1, 2, 3), away)]
        packed = jnp.concatenate([stay, *came], axis=0)
        bound = np.broadcast_to(ids.max(axis=(2, 3), keepdims=True), ids.shape)
    else:
        packed = jnp.broadcast_to(packed[:, None], (G, heads_axis // G, *packed.shape[1:]))
        packed = packed.reshape(heads_axis, blocks, -1)
        packed = lax.all_to_all(packed, "head", split_axis=0, concat_axis=0, tiled=True)
        packed = packed.reshape(heads_axis * blocks, -1)
        bound = ids
    if fast:
        packed, out_weights[1] = lax.optimization_barrier((packed, out_weights[1]))
    packed = gather_line(packed, "outer", 0)
    if fast:
        begin, packed, pieces = lax.optimization_barrier((sent[1], packed, pieces))
        pieces.append(swap(pieces[1], "head", 2))
        partners = [swap(piece, "head", 1) for piece in pieces]
        queries = [project([*pieces, *partners], [weight_first, exchange(begin)])]
    packed = gather_pair(packed, "inner").reshape(devices * blocks, -1)
    bound = (STRIDE * bound + BLK - 1).transpose(1, 0, 2, 3).reshape(-1)
    hidden = [bool((bound[i : i + LANES] > context).any()) for i in range(0, len(bound), LANES)]
    masked, start = [], 0
    for i in range(1, len(hidden) + 1):
        if i == len(hidden) or hidden[i] != hidden[start]:
            masked.append((start * LANES, min(i * LANES, len(bound)), hidden[start]))
            start = i
    if fast:
        column = np.arange(heads_axis)[None, None, :, None]
        ids = ids[:, :, :1] + (column ^ h) * blocks
        limits = (STRIDE * ids + BLK - 1).transpose(1, 0, 2, 3).reshape(1, -1).astype(jnp.int32)
    else:
        limits = (STRIDE * ids + BLK - 1).transpose(1, 0, 2, 3).reshape(1, -1)
        limits = jnp.asarray(limits, jnp.int32)

    total = None
    for head in range(1 if fast else heads_here):
        heads = tuple(range(heads_here)) if fast else (head,)
        attended = attend(
            here, queries, heads, packed, limits, places, key_width, masked, layout
        )
        if fast:
            block = jnp.concatenate([attended[0], swap(attended[1], "inner", 1)], axis=1)
            total = expel(
                here, line_pieces(block, "outer"), out_weights, [] if total is None else [total],
                0, 1, (heads_axis, quarter),
            )
        else:
            attended = gather_line(attended[0], "outer", 1)
            rows = out_weights.reshape(outer, heads_here, value_width, -1)[:, head]
            product = jnp.dot(
                attended, rows.reshape(outer * value_width, -1), preferred_element_type=jnp.float32
            )
            total = product if total is None else total + product

    if fast:
        keep, send = total
        columns = keep.shape[-1]
        total = keep + swap(send, "head", 1).astype(jnp.float32)
        x = h // 2
        keep = lax.dynamic_index_in_dim(total, x, 1, False)
        send = lax.dynamic_index_in_dim(total, 1 - x, 1, False).astype(jnp.bfloat16)
        total = keep + swap(send, "head", 2).astype(jnp.float32)
        result = total.astype(jnp.bfloat16).reshape(row_count, columns)
        first, second = result[:, : columns // 2], result[:, columns // 2 :]
        result = jnp.concatenate(
            [jnp.where(y == 0, first, second), jnp.where(y == 0, second, first)], axis=1
        )
        route = [
            ((a * inner + b) * heads_axis + k, (k * inner + b) * heads_axis + a)
            for a in range(outer) for b in range(inner) for k in range(heads_axis)
        ]
        return lax.ppermute(result, ("outer", "inner", "head"), route)
    columns = total.shape[1]
    total = lax.psum_scatter(total, "head", scatter_dimension=0, tiled=True).astype(jnp.bfloat16)
    total = lax.all_gather(total, "head", axis=0, tiled=True)
    total = lax.all_to_all(
        total.reshape(outer, row_count, columns), "outer", split_axis=0, concat_axis=0, tiled=True
    )
    total = total.transpose(1, 0, 2).reshape(row_count, model)
    return lax.dynamic_slice_in_dim(total, h * (model // heads_axis), model // heads_axis, 1)


def solution(mesh):
    seq_count, head_count = mesh.shape["seq"], mesh.shape["head"]
    inner = seq_count // OUTER
    finer = Mesh(
        mesh.devices.reshape(OUTER, inner, head_count), ("outer", "inner", "head")
    )
    seq = ("outer", "inner")
    in_specs = (
        P(seq, None),
        P((*seq, "head"), None),
        P((*seq, "head"), None),
        P(seq, "head"),
        P("head", seq),
        P(), P(), P(), P(), P(), P(),
    )
    return jax.shard_map(
        shards, mesh=finer, in_specs=in_specs, out_specs=P(seq, "head"), check_vma=False
    )
```
